128 devices in a mesh: ep: 16 (over z, x), dp: 8 (over y, core).
Axes of the slice: x: 4, y: 4, z: 4, core: 2. Of those that a mesh axis runs over, the one named last changes fastest.
Arguments:
- tokens: bfloat16 [8192, 4096], P(('ep', 'dp')), may hold values from -6 to 6
- cotangent: bfloat16 [8192, 4096], P(('ep', 'dp')), may hold values from -6 to 6
- expert_ids: int32 [8192, 8], P(('ep', 'dp')), may hold values from 0 to 15, all different within a row; in each aligned block of 64 rows (0 to 63, 64 to 127, ...) at most 33 rows name the same one
- gate_fixed: int32 [8192, 8], P(('ep', 'dp')), may hold values from 1 to 4095
- gate_up: bfloat16 [16, 4096, 1536], P('ep'), may hold values from -0.09375 to 0.09375
- down_weight: bfloat16 [16, 768, 4096], P('ep'), may hold values from -0.4375 to 0.4375
Outputs:
- layer_out: bfloat16 [8192, 4096], P(('ep', 'dp'))
- token_grad: bfloat16 [8192, 4096], P(('ep', 'dp'))
- gate_up_grad: bfloat16 [16, 4096, 1536], P('ep', 'dp')
- down_grad: bfloat16 [16, 768, 4096], P('ep', None, 'dp')
The draws below stay inside these ranges and needn't reach their ends.
Inputs may be any that keep to these rules, and one draw needn't show every extreme that they name: `expert_ids`: each row names 8 different experts. Among the tokens of one device (aligned blocks of 64 rows) no expert is named more than 33 times, and in every draw some expert is named exactly 33 times in some block.
All inputs are finite; a program needn't handle non-finite values.
Results may differ from the reference program's by a relative error of at most 0.017.
Values may be sent and summed in bfloat16 or wider, within the bound.
A program may use at most 192 MiB of HBM per device.

```python
import math
import jax
import jax.numpy as jnp
import numpy as np
from jax import lax

D = 4096
TOP = 8
HID = 768
TOK_DEV = 64
EXPERTS = 16
CAP = 33
TOKENS = 8192
N_EP = 16
N_DP = 8


def set_ends(array, key, least, top_value):
    index_at = [jax.random.randint(jax.random.fold_in(key, axis), (), 0, length) for axis, length in enumerate(array.shape)]
    widest = array.shape.index(max(array.shape))
    beside = index_at[:widest] + [(index_at[widest] + 1) % array.shape[widest]] + index_at[widest + 1:]
    return array.at[tuple(index_at)].set(least).at[tuple(beside)].set(top_value)


def levels(stream_key, extent, shards, smallest, largest):
    def one(dim, parts):
        draws = jax.random.uniform(jax.random.fold_in(jax.random.fold_in(stream_key, 6), dim), (parts,), jnp.float32, smallest / len(shards), largest / len(shards))
        return jnp.repeat(jnp.exp(draws), extent[dim] // parts).reshape((-1,) + (1,) * (len(extent) - dim - 1))

    level = one(*shards[0])
    for cut in shards[1:]:
        level = level * one(*cut)
    return level


def shared_out(stream_key, own, number, rows, amount, top, bound, slope):
    order = jax.random.permutation(stream_key, amount)
    crowded, common = load_shares(amount, rows * top, bound, slope, True), load_shares(amount, rows * top, bound, slope, False)
    places = jnp.arange(amount)

    def named(sizes, turn):
        used = int((sizes > 0).sum())
        fixed = max(1, used // 4)
        passed = fixed + (places - fixed + turn * (used - fixed)) % max(1, amount - fixed)
        return jnp.zeros((amount,), jnp.int32).at[order[jnp.where(places < fixed, places, passed)]].set(jnp.asarray(sizes, jnp.int32))

    sizes = jnp.where(number % 4 == 0, named(crowded, number // 4), named(common, number - number // 4 - 1))
    mixed = jax.random.permutation(jax.random.fold_in(own, 3), amount)
    source_of, receiver = mixed[0:amount // 2 * 2:2], mixed[1:amount // 2 * 2:2]
    slack = jnp.minimum(sizes[source_of] - 1, bound - sizes[receiver]) // 2
    slack = jnp.where((source_of == order[0]) | (receiver == order[0]) | (sizes[receiver] == 0), 0, jnp.maximum(slack, 0))
    passed = jax.random.randint(jax.random.fold_in(own, 4), (amount // 2,), 0, 1 << 20) % (slack + 1)
    sizes = sizes.at[source_of].add(-passed).at[receiver].add(passed)
    labels = jnp.searchsorted(jnp.cumsum(sizes), jnp.arange(rows * top), side="right").astype(jnp.int32)
    grid = labels.reshape(top, rows).T
    grid = grid[jax.random.permutation(jax.random.fold_in(own, 1), rows)]
    turn = jax.random.randint(jax.random.fold_in(own, 2), (rows, 1), 0, top)
    return jnp.take_along_axis(grid, (jnp.arange(top)[None, :] + turn) % top, axis=1)


def load_shares(amount, total, bound, lean, full):
    weights = [(1 << 20) // math.isqrt(standing ** lean) + 1 for standing in range(1, amount + 1)]
    largest = bound if full else min(bound, max(-(-total // amount), total * weights[0] // sum(weights)))
    least = 1 if total - largest >= amount - 1 else 0
    given, rest = [largest] + [least] * (amount - 1), total - largest - least * (amount - 1)
    while rest > 0:
        movable = [i for i in range(1, amount) if given[i] < largest] or [i for i in range(1, amount) if given[i] < bound]
        pool, budget = sum([weights[i] for i in movable]), rest
        for i in movable:
            more = min(bound - given[i], max(1, budget * weights[i] // pool), rest)
            given[i] = given[i] + more
            rest = rest - more
    return np.array(given)


def bell_draw(rng, shape, width, limit, cuts=(), kind=jnp.bfloat16):
    entries = width * jax.random.normal(rng, shape, jnp.float32)
    if cuts:
        entries = entries * levels(rng, shape, cuts, -0.22, 0.18)
    return jnp.clip(entries, -limit, limit).astype(kind)


def setup_inputs(seed: int = 0) -> dict:
    key_list = jax.random.split(jax.random.key(seed), 7)
    tokens = bell_draw(key_list[0], (TOKENS, D), 1.0, 6.0, ((0, 128),))
    cotangent = bell_draw(key_list[1], (TOKENS, D), 1.0, 6.0, ((0, 128),))
    expert_ids_keys = jax.random.split(jax.random.fold_in(key_list[2], 1), TOKENS // TOK_DEV)
    expert_ids_turns = jax.random.permutation(jax.random.fold_in(key_list[2], 3), TOKENS // TOK_DEV)
    expert_ids = jax.vmap(lambda own, number: shared_out(jax.random.fold_in(key_list[2], 2), own, number, TOK_DEV, EXPERTS, TOP, CAP, 2))(expert_ids_keys, expert_ids_turns).reshape((TOKENS, TOP))
    gate_fixed = set_ends(jax.random.randint(key_list[3], (TOKENS, TOP), 1, 4096), jax.random.fold_in(key_list[3], 1), 1, 4095).astype(jnp.int32)
    gate_up = bell_draw(key_list[4], (EXPERTS, D, 2 * HID), D ** -0.5, 0.09375, ((0, 16),))
    down_weight = bell_draw(key_list[5], (EXPERTS, HID, D), (HID // 4) ** -0.5, 0.4375, ((0, 16),))
    return dict(tokens=tokens, cotangent=cotangent, expert_ids=expert_ids, gate_fixed=gate_fixed, gate_up=gate_up, down_weight=down_weight)


def reference(tokens, cotangent, expert_ids, gate_fixed, gate_up, down_weight):
    blocks = TOKENS // TOK_DEV
    pair_count = TOK_DEV * TOP
    gate_int = gate_fixed.astype(jnp.float32)
    gate_share = gate_int / jnp.sum(gate_int, axis=1, keepdims=True)
    block_ids = expert_ids.reshape(blocks, pair_count)
    onehot = (block_ids[:, :, None] == jnp.arange(EXPERTS, dtype=jnp.int32)[None, None, :]).astype(jnp.int32)
    slot_rank = jnp.sum((jnp.cumsum(onehot, axis=1) - onehot) * onehot, axis=2)
    block_index = jnp.broadcast_to(jnp.arange(blocks, dtype=jnp.int32)[:, None], (blocks, pair_count))
    pair_index = jnp.broadcast_to(jnp.arange(pair_count, dtype=jnp.int32)[None, :], (blocks, pair_count))
    slot_table = jnp.full((EXPERTS, blocks, CAP), pair_count, jnp.int32)
    slot_table = slot_table.at[block_ids, block_index, slot_rank].set(pair_index)
    block_start = (jnp.arange(blocks, dtype=jnp.int32) * TOK_DEV)[:, None]

    def one_expert(totals, inputs):
        out_total, grad_total = totals
        slot_ids, in_matrix, out_matrix = inputs
        is_live = (slot_ids < pair_count).reshape(-1)
        clipped = jnp.minimum(slot_ids, pair_count - 1)
        token_index = (block_start + clipped // TOP).reshape(-1)
        which_k = (clipped % TOP).reshape(-1)
        slot_gate = jnp.where(is_live, gate_share[token_index, which_k], 0.0)
        slot_rows = jnp.where(is_live[:, None], tokens[token_index], jnp.zeros((), jnp.bfloat16))
        slot_grad = (slot_gate[:, None] * cotangent[token_index].astype(jnp.float32)).astype(jnp.bfloat16)
        pre_act = jnp.dot(slot_rows, in_matrix, preferred_element_type=jnp.float32)
        gate_pre = pre_act[:, :HID]
        up_pre = pre_act[:, HID:]
        logistic = jax.nn.sigmoid(gate_pre)
        hidden = (gate_pre * logistic * up_pre).astype(jnp.bfloat16)
        expert_out = jnp.dot(hidden, out_matrix, preferred_element_type=jnp.float32).astype(jnp.bfloat16)
        out_total = out_total.at[token_index].add(slot_gate[:, None] * expert_out.astype(jnp.float32))
        hidden_grad = jnp.dot(slot_grad, out_matrix.T, preferred_element_type=jnp.float32)
        pre_grad = jnp.concatenate(
            [hidden_grad * up_pre * logistic * (1.0 + gate_pre * (1.0 - logistic)), hidden_grad * gate_pre * logistic],
            axis=1).astype(jnp.bfloat16)
        slot_input_grad = jnp.dot(pre_grad, in_matrix.T, preferred_element_type=jnp.float32).astype(jnp.bfloat16)
        grad_total = grad_total.at[token_index].add(
            jnp.where(is_live[:, None], slot_input_grad.astype(jnp.float32), 0.0))
        rows_wide = slot_rows.astype(jnp.float32).reshape(N_EP, N_DP, CAP, D)
        pre_wide = pre_grad.astype(jnp.float32).reshape(N_EP, N_DP, CAP, 2 * HID)
        part_in = lax.optimization_barrier(
            jnp.einsum("escd,esch->sdh", rows_wide, pre_wide, precision=lax.Precision.HIGHEST).astype(jnp.bfloat16))
        hidden_wide = hidden.astype(jnp.float32).reshape(N_EP, N_DP, CAP, HID)
        grad_wide = slot_grad.astype(jnp.float32).reshape(N_EP, N_DP, CAP, D)
        part_out = lax.optimization_barrier(
            jnp.einsum("esch,escd->shd", hidden_wide, grad_wide, precision=lax.Precision.HIGHEST).astype(jnp.bfloat16))
        in_grad = jnp.sum(part_in.astype(jnp.float32), axis=0).astype(jnp.bfloat16)
        out_grad = jnp.sum(part_out.astype(jnp.float32), axis=0).astype(jnp.bfloat16)
        return (out_total, grad_total), (in_grad, out_grad)

    start_totals = (jnp.zeros((TOKENS, D), jnp.float32), jnp.zeros((TOKENS, D), jnp.float32))
    totals, grads = lax.scan(one_expert, start_totals, (slot_table, gate_up, down_weight))
    return totals[0].astype(jnp.bfloat16), totals[1].astype(jnp.bfloat16), grads[0], grads[1]
```

```python
import functools

import jax
import jax.numpy as jnp
from jax import lax
from jax.experimental import pallas as pl
from jax.experimental.pallas import tpu as pltpu
from jax.sharding import PartitionSpec as P

BF16 = jnp.bfloat16
F32 = jnp.float32
MESH = pl.DeviceIdType.MESH
TOK = 64
WIDTH = 4096
HALF = WIDTH // 2
CHUNK = HALF // 4
HID = 768
MAIN = 32
ROWS = 16 * MAIN + 16
ORDER = (2, 1, 3)


def place():
    ep = lax.axis_index("ep")
    return ep // 4, ep % 4


def peer(axis, distance):
    z, x = place()
    if axis == "z":
        z = lax.rem(z + distance, 4)
    else:
        x = lax.rem(x + distance, 4)
    return {"ep": z * 4 + x, "dp": lax.axis_index("dp")}


def first_axis(route):
    return ("z", "x")[route]


def second_axis(route):
    return ("x", "z")[route]


def coord(axis):
    z, x = place()
    return z if axis == "z" else x


def expert_at(route, position):
    z, x = place()
    return z * 4 + position if route == 0 else position * 4 + x


def iota(shape, dim):
    return lax.broadcasted_iota(jnp.int32, shape, dim)


def enter(peers):
    barrier = pltpu.get_barrier_semaphore()
    for device in peers:
        pl.semaphore_signal(barrier, 1, device_id=device, device_id_type=MESH)
    pl.semaphore_wait(barrier, len(peers))


def remote(src, dst, send_sem, recv_sem, device):
    return pltpu.make_async_remote_copy(
        src_ref=src,
        dst_ref=dst,
        send_sem=send_sem,
        recv_sem=recv_sem,
        device_id=device,
        device_id_type=MESH,
    )


def pick_row(table, index):
    rows = iota(table.shape, 0)
    return jnp.sum(jnp.where(rows == index, table, 0.0), axis=0, keepdims=True)


def slot_rows(rank, chunk):
    source = iota((1, 4 * TOK), 1) // TOK
    rank = rank.astype(jnp.int32)
    main = jnp.where(rank >= 0, rank + MAIN * source, -1)
    return jnp.where(rank == MAIN, 4 * MAIN + 4 * chunk + source, main)


def overflow_target(route, shape, dim):
    row = iota(shape, dim)
    sender, chunk, source = row // 16, lax.rem(row, 16) // 4, lax.rem(row, 4)
    slot = sender * 4 + source if route == 0 else source * 4 + sender
    return slot, chunk


def dispatch_kernel(
    ids_ref,
    gate_ref,
    tok_ref,
    cot_ref,
    wgu_hbm,
    wd_hbm,
    out_hbm,
    sig_hbm,
    x_hbm,
    g_hbm,
    h_hbm,
    pg_hbm,
    rank_out,
    share_out,
    wgu,
    wd,
    meta_own,
    meta,
    gathered,
    staged,
    staged_over,
    over,
    xbuf,
    gbuf,
    pre,
    hid,
    pgb,
    obuf,
    sbuf,
    local_sem,
    meta_send,
    meta_recv,
    gat_send,
    gat_recv,
    main_send,
    main_recv,
    over_send,
    over_recv,
):
    z, x = place()
    load_gu = pltpu.make_async_copy(wgu_hbm.at[0], wgu, local_sem.at[0])
    load_d = pltpu.make_async_copy(wd_hbm.at[0], wd, local_sem.at[1])
    load_gu.start()
    load_d.start()

    gates = gate_ref[...].astype(F32)
    share = gates / jnp.sum(gates, axis=0, keepdims=True)
    ids = ids_ref[...]
    expert = iota((16, TOK), 0)
    named = jnp.zeros((16, TOK), F32)
    weight = jnp.zeros((16, TOK), F32)
    for k in range(8):
        hit = ids[k : k + 1, :] == expert
        named += jnp.where(hit, 1.0, 0.0)
        weight += jnp.where(hit, share[k : k + 1, :], 0.0)
    before = jnp.where(iota((TOK, TOK), 0) < iota((TOK, TOK), 1), 1.0, 0.0)
    rank = jnp.dot(named.astype(BF16), before.astype(BF16), preferred_element_type=F32)
    rank = jnp.where(named > 0.0, rank, -1.0)
    meta_own[...] = jnp.concatenate([rank, weight], axis=1)

    enter([peer(axis, d) for axis in ("z", "x") for d in ORDER])

    sends = []
    meta_recvs = []
    for route in range(2):
        here = coord(first_axis(route))
        for d in ORDER:
            copy = remote(
                meta_own,
                meta.at[route, here],
                meta_send.at[route, d],
                meta_recv.at[route, d],
                peer(first_axis(route), d),
            )
            copy.start()
            sends.append(copy)
            meta_recvs.append(copy)
        meta[route, pl.ds(here, 1)] = meta_own[...][None]

    sources = (tok_ref, cot_ref)

    def gather_start(which):
        copies = ([], [])
        for d in ORDER:
            for route in range(2):
                here = coord(first_axis(route))
                copy = remote(
                    sources[which].at[:, pl.ds(route * HALF, HALF)],
                    gathered.at[which, route, pl.ds(pl.multiple_of(here * TOK, TOK), TOK), :],
                    gat_send.at[which, route, d],
                    gat_recv.at[which, route, d],
                    peer(first_axis(route), d),
                )
                copy.start()
                sends.append(copy)
                copies[route].append(copy)
        for route in range(2):
            here = coord(first_axis(route))
            gathered[which, route, pl.ds(pl.multiple_of(here * TOK, TOK), TOK), :] = sources[
                which
            ][:, route * HALF : (route + 1) * HALF]
        return copies

    tok_copies = gather_start(0)
    for copy in meta_recvs:
        copy.wait_recv()
    for route in range(2):
        rank_out[route] = jnp.concatenate([meta[route, s][:, :TOK] for s in range(4)], axis=1)
        share_out[route] = jnp.concatenate([meta[route, s][:, TOK:] for s in range(4)], axis=1)

    buffers = (xbuf, gbuf)

    def select(which, route, d):
        position = lax.rem(coord(second_axis(route)) + d, 4)
        expert = expert_at(route, position)
        rank_row = pick_row(rank_out[route], expert)
        share_row = pick_row(share_out[route], expert)
        here = coord(second_axis(route))
        target = buffers[which]
        total = jnp.zeros((16, CHUNK), F32)
        for c in range(4):
            hit = slot_rows(rank_row, c) == iota((4 * MAIN + 16, 4 * TOK), 0)
            choose = jnp.where(hit, 1.0, 0.0).astype(BF16)
            rows = jnp.dot(
                choose,
                gathered[which, route, :, c * CHUNK : (c + 1) * CHUNK],
                preferred_element_type=F32,
            )
            if which == 1:
                rows = rows * jnp.sum(jnp.where(hit, share_row, 0.0), axis=1, keepdims=True)
            main = rows[: 4 * MAIN].astype(BF16)
            total += rows[4 * MAIN :]
            if d:
                staged[which, route, d - 1, :, c * CHUNK : (c + 1) * CHUNK] = main
            else:
                columns = slice(route * HALF + c * CHUNK, route * HALF + (c + 1) * CHUNK)
                if route == 0:
                    target[pl.ds(pl.multiple_of(here * 128, 128), 128), columns] = main
                else:
                    for s in range(4):
                        first = pl.multiple_of((s * 4 + here) * MAIN, MAIN)
                        target[pl.ds(first, MAIN), columns] = main[s * MAIN : (s + 1) * MAIN]
        mine = pl.ds(pl.multiple_of(here * 16, 16), 16)
        if not d:
            over[which, route, mine, :] = total.astype(BF16)
            return []
        staged_over[which, route, d - 1] = total.astype(BF16)
        device = peer(second_axis(route), d)
        columns = pl.ds(route * HALF, HALF)
        copies = []
        if route == 0:
            copies.append(
                remote(
                    staged.at[which, route, d - 1],
                    target.at[pl.ds(pl.multiple_of(here * 128, 128), 128), columns],
                    main_send.at[which, route, d, 0],
                    main_recv.at[which, route, d, 0],
                    device,
                )
            )
        else:
            for s in range(4):
                first = pl.multiple_of((s * 4 + here) * MAIN, MAIN)
                copies.append(
                    remote(
                        staged.at[which, route, d - 1, pl.ds(s * MAIN, MAIN), :],
                        target.at[pl.ds(first, MAIN), columns],
                        main_send.at[which, route, d, s],
                        main_recv.at[which, route, d, s],
                        device,
                    )
                )
        copies.append(
            remote(
                staged_over.at[which, route, d - 1],
                over.at[which, route, mine, :],
                over_send.at[which, route, d],
                over_recv.at[which, route, d],
                device,
            )
        )
        for copy in copies:
            copy.start()
        sends.extend(copies)
        return copies

    def second_hop(which, gather_copies):
        arrivals = []
        for route in range(2):
            for copy in gather_copies[route]:
                copy.wait_recv()
        for d in ORDER:
            for route in range(2):
                arrivals.extend(select(which, route, d))
        return arrivals

    def finish(which, arrivals):
        for route in range(2):
            select(which, route, 0)
        for copy in arrivals:
            copy.wait_recv()
        for route in range(2):
            slot, chunk = overflow_target(route, (16, 64), 1)
            for c in range(4):
                spread = jnp.where((slot == iota((16, 64), 0)) & (chunk == c), 1.0, 0.0)
                first = route * HALF + c * CHUNK
                buffers[which][16 * MAIN : ROWS, first : first + CHUNK] = jnp.dot(
                    spread.astype(BF16), over[which, route], preferred_element_type=F32
                ).astype(BF16)

    x_arrivals = second_hop(0, tok_copies)
    cot_copies = gather_start(1)
    load_gu.wait()
    load_d.wait()
    g_arrivals = second_hop(1, cot_copies)
    finish(0, x_arrivals)
    store_x = pltpu.make_async_copy(xbuf, x_hbm, local_sem.at[2])
    store_x.start()

    @pl.loop(0, 3)
    def _(n):
        u_cols = pl.ds(pl.multiple_of(n * 256, 256), 256)
        v_cols = pl.ds(pl.multiple_of(HID + n * 256, 256), 256)
        u = jnp.dot(xbuf[...], wgu[:, u_cols], preferred_element_type=F32)
        pre[:, u_cols] = u
        v = jnp.dot(xbuf[...], wgu[:, v_cols], preferred_element_type=F32)
        pre[:, v_cols] = v
        hid[:, u_cols] = (pre[:, u_cols] * jax.nn.sigmoid(pre[:, u_cols]) * v).astype(BF16)

    store_h = pltpu.make_async_copy(hid, h_hbm, local_sem.at[3])
    store_h.start()

    @pl.loop(0, WIDTH // 256)
    def _(n):
        cols = pl.ds(pl.multiple_of(n * 256, 256), 256)
        obuf[:, cols] = jnp.dot(hid[...], wd[:, cols], preferred_element_type=F32).astype(BF16)

    store_o = pltpu.make_async_copy(obuf, out_hbm, local_sem.at[4])
    store_o.start()
    finish(1, g_arrivals)
    store_g = pltpu.make_async_copy(gbuf, g_hbm, local_sem.at[5])
    store_g.start()

    @pl.loop(0, 3)
    def _(n):
        u_cols = pl.ds(pl.multiple_of(n * 256, 256), 256)
        v_cols = pl.ds(pl.multiple_of(HID + n * 256, 256), 256)
        grad = lax.dot_general(
            gbuf[...], wd[u_cols, :], (((1,), (1,)), ((), ())), preferred_element_type=F32
        )
        u = pre[:, u_cols]
        logistic = jax.nn.sigmoid(u)
        pgb[:, v_cols] = (grad * u * logistic).astype(BF16)
        pgb[:, u_cols] = (
            grad * pre[:, v_cols] * logistic * (1.0 + u * (1.0 - logistic))
        ).astype(BF16)

    store_p = pltpu.make_async_copy(pgb, pg_hbm, local_sem.at[6])
    store_p.start()

    @pl.loop(0, WIDTH // 256)
    def _(n):
        cols = pl.ds(pl.multiple_of(n * 256, 256), 256)
        sbuf[:, cols] = lax.dot_general(
            pgb[...], wgu[cols, :], (((1,), (1,)), ((), ())), preferred_element_type=F32
        ).astype(BF16)

    store_s = pltpu.make_async_copy(sbuf, sig_hbm, local_sem.at[7])
    store_s.start()
    for copy in (store_x, store_h, store_o, store_g, store_p, store_s):
        copy.wait()
    for copy in sends:
        copy.wait_send()


def return_kernel(
    out_hbm,
    sig_hbm,
    rank_ref,
    share_ref,
    layer_out,
    token_grad,
    tail,
    compact,
    rows,
    rows_over,
    partial,
    final,
    local_sem,
    main_send,
    main_recv,
    over_send,
    over_recv,
    part_send,
    part_recv,
):
    z, x = place()
    inputs = (out_hbm, sig_hbm)
    loads = []
    for which in range(2):
        copy = pltpu.make_async_copy(
            inputs[which].at[pl.ds(16 * MAIN, 16), :], tail.at[which], local_sem.at[which]
        )
        copy.start()
        loads.append(copy)
    enter([peer(axis, d) for axis in ("z", "x") for d in ORDER])
    sends = []

    def pieces(which, route, position, slot):
        columns = pl.ds(route * HALF, HALF)
        if route == 0:
            first = pl.multiple_of(position * 128, 128)
            return [
                (inputs[which].at[pl.ds(first, 128), columns], rows.at[which, route, slot])
            ]
        found = []
        for s in range(4):
            first = pl.multiple_of((s * 4 + position) * MAIN, MAIN)
            found.append(
                (
                    inputs[which].at[pl.ds(first, MAIN), columns],
                    rows.at[which, route, slot, pl.ds(s * MAIN, MAIN), :],
                )
            )
        return found

    def first_hop(which):
        arrivals = [[], []]
        for d in ORDER:
            for route in range(2):
                here = coord(second_axis(route))
                there = lax.rem(here + d, 4)
                for s, (src, dst) in enumerate(pieces(which, route, there, here)):
                    copy = remote(
                        src,
                        dst,
                        main_send.at[which, route, d, s],
                        main_recv.at[which, route, d, s],
                        peer(second_axis(route), d),
                    )
                    copy.start()
                    sends.append(copy)
                    arrivals[route].append(copy)
        owns = [[], []]
        for route in range(2):
            here = coord(second_axis(route))
            for s, (src, dst) in enumerate(pieces(which, route, here, here)):
                copy = pltpu.make_async_copy(src, dst, local_sem.at[2 + which * 8 + route * 4 + s])
                copy.start()
                owns[route].append(copy)
        loads[which].wait()
        for route in range(2):
            here = coord(second_axis(route))
            slot, chunk = overflow_target(route, (64, 16), 0)
            total = jnp.zeros((64, CHUNK), F32)
            for c in range(4):
                take = jnp.where((slot == iota((64, 16), 1)) & (chunk == c), 1.0, 0.0)
                first = route * HALF + c * CHUNK
                total += jnp.dot(
                    take.astype(BF16),
                    tail[which, :, first : first + CHUNK],
                    preferred_element_type=F32,
                )
            compact[which, route] = total.astype(BF16)
            mine = pl.ds(pl.multiple_of(here * 16, 16), 16)
            rows_over[which, route, mine, :] = compact[which, route, mine, :]
            for d in ORDER:
                there = lax.rem(here + d, 4)
                copy = remote(
                    compact.at[which, route, pl.ds(pl.multiple_of(there * 16, 16), 16), :],
                    rows_over.at[which, route, mine, :],
                    over_send.at[which, route, d],
                    over_recv.at[which, route, d],
                    peer(second_axis(route), d),
                )
                copy.start()
                sends.append(copy)
                arrivals[route].append(copy)
        return arrivals, owns

    def combine(which, arrivals, owns):
        finals = []
        for route in range(2):
            for copy in arrivals[route]:
                copy.wait_recv()
            for copy in owns[route]:
                copy.wait()
            ranks = [pick_row(rank_ref[route], expert_at(route, p)) for p in range(4)]
            shares = [pick_row(share_ref[route], expert_at(route, p)) for p in range(4)]
            for c in range(4):
                main, rest = [], []
                for p in range(4):
                    hit = slot_rows(ranks[p], c) == iota((4 * MAIN + 16, 4 * TOK), 0)
                    value = shares[p] if which == 0 else 1.0
                    spread = jnp.where(hit, value, 0.0)
                    main.append(spread[: 4 * MAIN])
                    rest.append(spread[4 * MAIN :])
                main = jnp.concatenate(main, axis=0).astype(BF16)
                rest = jnp.concatenate(rest, axis=0).astype(BF16)
                columns = slice(c * CHUNK, (c + 1) * CHUNK)
                along = (((0,), (0,)), ((), ()))
                total = lax.dot_general(
                    main,
                    rows[which, route, :, :, columns].reshape(16 * MAIN, CHUNK),
                    along,
                    preferred_element_type=F32,
                ) + lax.dot_general(
                    rest, rows_over[which, route], along, preferred_element_type=F32
                )
                partial[which, route, :, columns] = total.astype(BF16)
            here = coord(first_axis(route))
            for d in ORDER:
                there = lax.rem(here + d, 4)
                copy = remote(
                    partial.at[which, route, pl.ds(pl.multiple_of(there * TOK, TOK), TOK), :],
                    final.at[which, route, d - 1],
                    part_send.at[which, route, d],
                    part_recv.at[which, route, d],
                    peer(first_axis(route), d),
                )
                copy.start()
                sends.append(copy)
                finals.append(copy)
        return finals

    def finish(which, finals, result):
        for copy in finals:
            copy.wait_recv()
        for route in range(2):
            here = coord(first_axis(route))
            own = partial[which, route, pl.ds(pl.multiple_of(here * TOK, TOK), TOK), :]
            total = own.astype(F32)
            for d in range(3):
                total += final[which, route, d].astype(F32)
            result[:, route * HALF : (route + 1) * HALF] = total.astype(BF16)

    out_state = first_hop(0)
    sig_state = first_hop(1)
    out_finals = combine(0, *out_state)
    sig_finals = combine(1, *sig_state)
    finish(0, out_finals, layer_out)
    finish(1, sig_finals, token_grad)
    for copy in sends:
        copy.wait_send()


VMEM = pl.BlockSpec(memory_space=pltpu.VMEM)
ANY = pl.BlockSpec(memory_space=pl.ANY)
DMA = pltpu.SemaphoreType.DMA


def dispatch(ids, gates, tokens, cotangent, gate_up, down_weight):
    wide = jax.ShapeDtypeStruct((ROWS, WIDTH), BF16)
    table = jax.ShapeDtypeStruct((2, 16, 4 * TOK), F32)
    return pl.pallas_call(
        dispatch_kernel,
        out_shape=(
            wide,
            wide,
            wide,
            wide,
            jax.ShapeDtypeStruct((ROWS, HID), BF16),
            jax.ShapeDtypeStruct((ROWS, 2 * HID), BF16),
            table,
            table,
        ),
        in_specs=[VMEM] * 4 + [ANY] * 2,
        out_specs=(ANY,) * 6 + (VMEM,) * 2,
        scratch_shapes=[
            pltpu.VMEM((WIDTH, 2 * HID), BF16),
            pltpu.VMEM((HID, WIDTH), BF16),
            pltpu.VMEM((16, 2 * TOK), F32),
            pltpu.VMEM((2, 4, 16, 2 * TOK), F32),
            pltpu.VMEM((2, 2, 4 * TOK, HALF), BF16),
            pltpu.VMEM((2, 2, 3, 4 * MAIN, HALF), BF16),
            pltpu.VMEM((2, 2, 3, 16, CHUNK), BF16),
            pltpu.VMEM((2, 2, 64, CHUNK), BF16),
            pltpu.VMEM((ROWS, WIDTH), BF16),
            pltpu.VMEM((ROWS, WIDTH), BF16),
            pltpu.VMEM((ROWS, 2 * HID), F32),
            pltpu.VMEM((ROWS, HID), BF16),
            pltpu.VMEM((ROWS, 2 * HID), BF16),
            pltpu.VMEM((ROWS, WIDTH), BF16),
            pltpu.VMEM((ROWS, WIDTH), BF16),
            DMA((8,)),
            DMA((2, 4)),
            DMA((2, 4)),
            DMA((2, 2, 4)),
            DMA((2, 2, 4)),
            DMA((2, 2, 4, 4)),
            DMA((2, 2, 4, 4)),
            DMA((2, 2, 4)),
            DMA((2, 2, 4)),
        ],
        compiler_params=pltpu.CompilerParams(
            collective_id=0, has_side_effects=True, vmem_limit_bytes=60 << 20
        ),
        cost_estimate=pl.CostEstimate(
            flops=20 * 10**9, bytes_accessed=40 * 10**6, transcendentals=10**6
        ),
    )(ids, gates, tokens, cotangent, gate_up, down_weight)


def give_back(out_rows, sig_rows, rank, share):
    result = jax.ShapeDtypeStruct((TOK, WIDTH), BF16)
    return pl.pallas_call(
        return_kernel,
        out_shape=(result, result),
        in_specs=[ANY] * 2 + [VMEM] * 2,
        out_specs=(VMEM, VMEM),
        scratch_shapes=[
            pltpu.VMEM((2, 16, WIDTH), BF16),
            pltpu.VMEM((2, 2, 64, CHUNK), BF16),
            pltpu.VMEM((2, 2, 4, 4 * MAIN, HALF), BF16),
            pltpu.VMEM((2, 2, 64, CHUNK), BF16),
            pltpu.VMEM((2, 2, 4 * TOK, HALF), BF16),
            pltpu.VMEM((2, 2, 3, TOK, HALF), BF16),
            DMA((18,)),
            DMA((2, 2, 4, 4)),
            DMA((2, 2, 4, 4)),
            DMA((2, 2, 4)),
            DMA((2, 2, 4)),
            DMA((2, 2, 4)),
            DMA((2, 2, 4)),
        ],
        compiler_params=pltpu.CompilerParams(
            collective_id=1, has_side_effects=True, vmem_limit_bytes=40 << 20
        ),
        cost_estimate=pl.CostEstimate(
            flops=6 * 10**9, bytes_accessed=300 * 10**6, transcendentals=0
        ),
    )(out_rows, sig_rows, rank, share)


def per_device(tokens, cotangent, expert_ids, gate_fixed, gate_up, down_weight):
    out_rows, sig_rows, x_rows, g_rows, hidden, pre_grad, rank, share = dispatch(
        expert_ids.T, gate_fixed.T, tokens, cotangent, gate_up, down_weight
    )
    along = (((0,), (0,)), ((), ()))
    part_out = lax.dot_general(hidden, g_rows, along, preferred_element_type=F32)
    part_in = lax.dot_general(x_rows, pre_grad, along, preferred_element_type=F32)
    grad_out = lax.psum_scatter(part_out.astype(BF16), "dp", scatter_dimension=1, tiled=True)
    grad_in = lax.psum_scatter(part_in.astype(BF16), "dp", scatter_dimension=0, tiled=True)
    layer_out, token_grad = give_back(out_rows, sig_rows, rank, share)
    return layer_out, token_grad, grad_in[None], grad_out[None]


def solution(mesh):
    rows = P(("ep", "dp"), None)
    return jax.shard_map(
        per_device,
        mesh=mesh,
        in_specs=(rows, rows, rows, rows, P("ep", None, None), P("ep", None, None)),
        out_specs=(rows, rows, P("ep", "dp", None), P("ep", None, "dp")),
        check_vma=False,
    )
```

```python
import functools

import jax
import jax.numpy as jnp
from jax import lax
from jax.experimental import pallas as pl
from jax.experimental.pallas import tpu as pltpu
from jax.sharding import PartitionSpec as P

BF16 = jnp.bfloat16
F32 = jnp.float32
MESH = pl.DeviceIdType.MESH
TOK = 64
WIDTH = 4096
HALF = WIDTH // 2
CHUNK = HALF // 4
HID = 768
MAIN = 32
ROWS = 16 * MAIN + 16
ORDER = (2, 1, 3)


def place():
    ep = lax.axis_index("ep")
    return ep // 4, ep % 4


def peer(axis, distance):
    z, x = place()
    if axis == "z":
        z = lax.rem(z + distance, 4)
    else:
        x = lax.rem(x + distance, 4)
    return {"ep": z * 4 + x, "dp": lax.axis_index("dp")}


def along_y(distance):
    dp = lax.axis_index("dp")
    return {"ep": lax.axis_index("ep"), "dp": lax.rem(dp + 2 * distance, 8)}


def other_core():
    dp = lax.axis_index("dp")
    return {"ep": lax.axis_index("ep"), "dp": dp + 1 - 2 * lax.rem(dp, 2)}


def first_axis(route):
    return ("z", "x")[route]


def second_axis(route):
    return ("x", "z")[route]


def coord(axis):
    z, x = place()
    return z if axis == "z" else x


def expert_at(route, position):
    z, x = place()
    return z * 4 + position if route == 0 else position * 4 + x


def iota(shape, dim):
    return lax.broadcasted_iota(jnp.int32, shape, dim)


def enter(peers):
    barrier = pltpu.get_barrier_semaphore()
    for device in peers:
        pl.semaphore_signal(barrier, 1, device_id=device, device_id_type=MESH)
    pl.semaphore_wait(barrier, len(peers))


def remote(src, dst, send_sem, recv_sem, device):
    return pltpu.make_async_remote_copy(
        src_ref=src,
        dst_ref=dst,
        send_sem=send_sem,
        recv_sem=recv_sem,
        device_id=device,
        device_id_type=MESH,
    )


def pick_row(table, index):
    rows = iota(table.shape, 0)
    return jnp.sum(jnp.where(rows == index, table, 0.0), axis=0, keepdims=True)


def slot_rows(rank, chunk):
    source = iota((1, 4 * TOK), 1) // TOK
    rank = rank.astype(jnp.int32)
    main = jnp.where(rank >= 0, rank + MAIN * source, -1)
    return jnp.where(rank == MAIN, 4 * MAIN + 4 * chunk + source, main)


def overflow_target(route, shape, dim):
    row = iota(shape, dim)
    sender, chunk, source = row // 16, lax.rem(row, 16) // 4, lax.rem(row, 4)
    slot = sender * 4 + source if route == 0 else source * 4 + sender
    return slot, chunk


def dispatch_kernel(
    ids_ref,
    gate_ref,
    tok_ref,
    cot_ref,
    wgu_hbm,
    wd_hbm,
    out_hbm,
    x_hbm,
    g_hbm,
    h_hbm,
    pg_hbm,
    rank_out,
    share_out,
    wgu,
    wd,
    meta_own,
    meta,
    gathered,
    staged,
    staged_over,
    over,
    xbuf,
    gbuf,
    pre,
    hid,
    pgb,
    obuf,
    local_sem,
    meta_send,
    meta_recv,
    gat_send,
    gat_recv,
    main_send,
    main_recv,
    over_send,
    over_recv,
    core_send,
    core_recv,
):
    z, x = place()
    load_gu = pltpu.make_async_copy(wgu_hbm.at[0], wgu, local_sem.at[0])
    load_d = pltpu.make_async_copy(wd_hbm.at[0], wd, local_sem.at[1])
    load_gu.start()
    load_d.start()

    gates = gate_ref[...].astype(F32)
    share = gates / jnp.sum(gates, axis=0, keepdims=True)
    ids = ids_ref[...]
    expert = iota((16, TOK), 0)
    named = jnp.zeros((16, TOK), F32)
    weight = jnp.zeros((16, TOK), F32)
    for k in range(8):
        hit = ids[k : k + 1, :] == expert
        named += jnp.where(hit, 1.0, 0.0)
        weight += jnp.where(hit, share[k : k + 1, :], 0.0)
    before = jnp.where(iota((TOK, TOK), 0) < iota((TOK, TOK), 1), 1.0, 0.0)
    rank = jnp.dot(named.astype(BF16), before.astype(BF16), preferred_element_type=F32)
    rank = jnp.where(named > 0.0, rank, -1.0)
    meta_own[...] = jnp.concatenate([rank, weight], axis=1)

    enter([peer(axis, d) for axis in ("z", "x") for d in ORDER] + [other_core()])

    sends = []
    meta_recvs = []
    for route in range(2):
        here = coord(first_axis(route))
        for d in ORDER:
            copy = remote(
                meta_own,
                meta.at[route, here],
                meta_send.at[route, d],
                meta_recv.at[route, d],
                peer(first_axis(route), d),
            )
            copy.start()
            sends.append(copy)
            meta_recvs.append(copy)
        meta[route, pl.ds(here, 1)] = meta_own[...][None]

    sources = (tok_ref, cot_ref)

    def block(which, route, position, columns):
        rows = pl.ds(pl.multiple_of(position * TOK, TOK), TOK)
        return gathered.at[which, route, rows, columns]

    def gather_start(which):
        copies = [{}, {}]
        for d in (1, 3):
            for route in range(2):
                here = coord(first_axis(route))
                copy = remote(
                    sources[which].at[:, pl.ds(route * HALF, HALF)],
                    block(which, route, here, pl.ds(0, HALF)),
                    gat_send.at[which, route, d],
                    gat_recv.at[which, route, d],
                    peer(first_axis(route), d),
                )
                copy.start()
                sends.append(copy)
                copies[route][d] = copy
        for route in range(2):
            here = coord(first_axis(route))
            gathered[which, route, pl.ds(pl.multiple_of(here * TOK, TOK), TOK), :] = sources[
                which
            ][:, route * HALF : (route + 1) * HALF]
        return copies

    def gather_pass(which, copies):
        passed = []
        for d in (1, 3):
            for route in range(2):
                copies[route][d].wait_recv()
                axis = first_axis(route)
                behind = lax.rem(coord(axis) + 4 - d, 4)
                columns = pl.ds((d // 2) * (HALF // 2), HALF // 2)
                copy = remote(
                    block(which, route, behind, columns),
                    block(which, route, behind, columns),
                    gat_send.at[which, route, d - 1],
                    gat_recv.at[which, route, d - 1],
                    peer(axis, d),
                )
                copy.start()
                sends.append(copy)
                passed.append(copy)
        return passed

    tok_copies = gather_start(0)
    cot_copies = gather_start(1)
    for copy in meta_recvs:
        copy.wait_recv()
    for route in range(2):
        rank_out[route] = jnp.concatenate([meta[route, s][:, :TOK] for s in range(4)], axis=1)
        share_out[route] = jnp.concatenate([meta[route, s][:, TOK:] for s in range(4)], axis=1)

    buffers = (xbuf, gbuf)

    def select(which, route, d):
        position = lax.rem(coord(second_axis(route)) + d, 4)
        expert = expert_at(route, position)
        rank_row = pick_row(rank_out[route], expert)
        share_row = pick_row(share_out[route], expert)
        here = coord(second_axis(route))
        target = buffers[which]
        total = jnp.zeros((16, CHUNK), F32)
        for c in range(4):
            hit = slot_rows(rank_row, c) == iota((4 * MAIN + 16, 4 * TOK), 0)
            choose = jnp.where(hit, 1.0, 0.0).astype(BF16)
            rows = jnp.dot(
                choose,
                gathered[which, route, :, c * CHUNK : (c + 1) * CHUNK],
                preferred_element_type=F32,
            )
            if which == 1:
                rows = rows * jnp.sum(jnp.where(hit, share_row, 0.0), axis=1, keepdims=True)
            main = rows[: 4 * MAIN].astype(BF16)
            total += rows[4 * MAIN :]
            if d:
                staged[which, route, d - 1, :, c * CHUNK : (c + 1) * CHUNK] = main
            else:
                columns = slice(route * HALF + c * CHUNK, route * HALF + (c + 1) * CHUNK)
                if route == 0:
                    target[pl.ds(pl.multiple_of(here * 128, 128), 128), columns] = main
                else:
                    for s in range(4):
                        first = pl.multiple_of((s * 4 + here) * MAIN, MAIN)
                        target[pl.ds(first, MAIN), columns] = main[s * MAIN : (s + 1) * MAIN]
        mine = pl.ds(pl.multiple_of(here * 16, 16), 16)
        if not d:
            over[which, route, mine, :] = total.astype(BF16)
            return []
        staged_over[which, route, d - 1] = total.astype(BF16)
        device = peer(second_axis(route), d)
        columns = pl.ds(route * HALF, HALF)
        copies = []
        if route == 0:
            copies.append(
                remote(
                    staged.at[which, route, d - 1],
                    target.at[pl.ds(pl.multiple_of(here * 128, 128), 128), columns],
                    main_send.at[which, route, d, 0],
                    main_recv.at[which, route, d, 0],
                    device,
                )
            )
        else:
            for s in range(4):
                first = pl.multiple_of((s * 4 + here) * MAIN, MAIN)
                copies.append(
                    remote(
                        staged.at[which, route, d - 1, pl.ds(s * MAIN, MAIN), :],
                        target.at[pl.ds(first, MAIN), columns],
                        main_send.at[which, route, d, s],
                        main_recv.at[which, route, d, s],
                        device,
                    )
                )
        copies.append(
            remote(
                staged_over.at[which, route, d - 1],
                over.at[which, route, mine, :],
                over_send.at[which, route, d],
                over_recv.at[which, route, d],
                device,
            )
        )
        for copy in copies:
            copy.start()
        sends.extend(copies)
        return copies

    def second_hop(which, passed):
        arrivals = []
        for copy in passed:
            copy.wait_recv()
        for d in ORDER:
            for route in range(2):
                arrivals.extend(select(which, route, d))
        return arrivals

    def finish(which, arrivals):
        for route in range(2):
            select(which, route, 0)
        for copy in arrivals:
            copy.wait_recv()
        for route in range(2):
            slot, chunk = overflow_target(route, (16, 64), 1)
            for c in range(4):
                spread = jnp.where((slot == iota((16, 64), 0)) & (chunk == c), 1.0, 0.0)
                first = route * HALF + c * CHUNK
                buffers[which][16 * MAIN : ROWS, first : first + CHUNK] = jnp.dot(
                    spread.astype(BF16), over[which, route], preferred_element_type=F32
                ).astype(BF16)

    tok_passed = gather_pass(0, tok_copies)
    cot_passed = gather_pass(1, cot_copies)
    x_arrivals = second_hop(0, tok_passed)
    g_arrivals = second_hop(1, cot_passed)
    load_gu.wait()
    load_d.wait()

    core = lax.rem(lax.axis_index("dp"), 2)
    stores = []
    shared = []

    def store(src, dst):
        copy = pltpu.make_async_copy(src, dst, local_sem.at[2 + len(stores)])
        copy.start()
        stores.append(copy)

    def share(src, dst):
        slot = len(shared)
        copy = remote(src, dst, core_send.at[slot], core_recv.at[slot], other_core())
        copy.start()
        shared.append(copy)

    mine, theirs = pl.ds(0, ROWS), pl.ds(ROWS, ROWS)

    def split(src, dst):
        for block in range(4):
            there = pl.ds(block * 512, 512)
            keep = pl.ds(pl.multiple_of((2 * block + core) * 512, 512), 512)
            give = pl.ds(pl.multiple_of((2 * block + 1 - core) * 512, 512), 512)
            share(src.at[:, give], dst.at[theirs, there])
            store(src.at[:, keep], dst.at[mine, there])

    finish(0, x_arrivals)
    split(xbuf, x_hbm)

    @pl.loop(0, 3)
    def _(n):
        u_cols = pl.ds(pl.multiple_of(n * 256, 256), 256)
        v_cols = pl.ds(pl.multiple_of(HID + n * 256, 256), 256)
        u = jnp.dot(xbuf[...], wgu[:, u_cols], preferred_element_type=F32)
        pre[:, u_cols] = u
        v = jnp.dot(xbuf[...], wgu[:, v_cols], preferred_element_type=F32)
        pre[:, v_cols] = v
        hid[:, u_cols] = (pre[:, u_cols] * jax.nn.sigmoid(pre[:, u_cols]) * v).astype(BF16)

    share(hid, h_hbm.at[theirs])
    store(hid, h_hbm.at[mine])

    @pl.loop(0, WIDTH // 256)
    def _(n):
        cols = pl.ds(pl.multiple_of(n * 256, 256), 256)
        obuf[:, cols] = jnp.dot(hid[...], wd[:, cols], preferred_element_type=F32).astype(BF16)

    store(obuf, out_hbm)
    finish(1, g_arrivals)
    split(gbuf, g_hbm)

    @pl.loop(0, 3)
    def _(n):
        u_cols = pl.ds(pl.multiple_of(n * 256, 256), 256)
        v_cols = pl.ds(pl.multiple_of(HID + n * 256, 256), 256)
        grad = lax.dot_general(
            gbuf[...], wd[u_cols, :], (((1,), (1,)), ((), ())), preferred_element_type=F32
        )
        u = pre[:, u_cols]
        logistic = jax.nn.sigmoid(u)
        pgb[:, v_cols] = (grad * u * logistic).astype(BF16)
        pgb[:, u_cols] = (
            grad * pre[:, v_cols] * logistic * (1.0 + u * (1.0 - logistic))
        ).astype(BF16)

    share(pgb, pg_hbm.at[theirs])
    store(pgb, pg_hbm.at[mine])
    for copy in stores + shared:
        copy.wait()
    for copy in sends:
        copy.wait_send()


def return_kernel(
    out_hbm,
    wgu_hbm,
    x_hbm,
    g_hbm,
    h_hbm,
    pg_hbm,
    rank_ref,
    share_ref,
    layer_out,
    token_grad,
    grad_in,
    grad_out,
    xb,
    gb,
    hb,
    pgb,
    wgu,
    sig,
    sum_in,
    sum_out,
    near_in,
    near_out,
    far_in,
    far_out,
    tail,
    compact,
    rows,
    rows_over,
    partial,
    final,
    local_sem,
    wgu_sem,
    main_send,
    main_recv,
    over_send,
    over_recv,
    part_send,
    part_recv,
    dp_send,
    dp_recv,
):
    z, x = place()
    inputs = (out_hbm, sig)
    fetch = []
    for slot, (src, dst) in enumerate(((h_hbm, hb), (g_hbm, gb), (x_hbm, xb), (pg_hbm, pgb))):
        copy = pltpu.make_async_copy(src, dst, local_sem.at[18 + slot])
        copy.start()
        fetch.append(copy)
    load_tail = pltpu.make_async_copy(
        out_hbm.at[pl.ds(16 * MAIN, 16), :], tail, local_sem.at[0]
    )
    load_tail.start()

    def wgu_tile(n):
        rows = pl.ds(pl.multiple_of(n * 256, 256), 256)
        slot = lax.rem(n, 2)
        return pltpu.make_async_copy(wgu_hbm.at[0, rows, :], wgu.at[slot], wgu_sem.at[slot])

    wgu_tile(0).start()
    enter(
        [peer(axis, d) for axis in ("z", "x") for d in ORDER] + [along_y(d) for d in (1, 3)]
    )
    sends = []

    def pieces(which, route, position, slot):
        columns = pl.ds(route * HALF, HALF)
        if route == 0:
            first = pl.multiple_of(position * 128, 128)
            return [
                (inputs[which].at[pl.ds(first, 128), columns], rows.at[which, route, slot])
            ]
        found = []
        for s in range(4):
            first = pl.multiple_of((s * 4 + position) * MAIN, MAIN)
            found.append(
                (
                    inputs[which].at[pl.ds(first, MAIN), columns],
                    rows.at[which, route, slot, pl.ds(s * MAIN, MAIN), :],
                )
            )
        return found

    def first_hop(which):
        arrivals = [[], []]
        for d in ORDER:
            for route in range(2):
                here = coord(second_axis(route))
                there = lax.rem(here + d, 4)
                for s, (src, dst) in enumerate(pieces(which, route, there, here)):
                    copy = remote(
                        src,
                        dst,
                        main_send.at[which, route, d, s],
                        main_recv.at[which, route, d, s],
                        peer(second_axis(route), d),
                    )
                    copy.start()
                    sends.append(copy)
                    arrivals[route].append(copy)
        owns = [[], []]
        for route in range(2):
            here = coord(second_axis(route))
            for s, (src, dst) in enumerate(pieces(which, route, here, here)):
                copy = pltpu.make_async_copy(src, dst, local_sem.at[2 + which * 8 + route * 4 + s])
                copy.start()
                owns[route].append(copy)
        if which == 0:
            load_tail.wait()
        last = tail if which == 0 else sig.at[pl.ds(16 * MAIN, 16), :]
        for route in range(2):
            here = coord(second_axis(route))
            slot, chunk = overflow_target(route, (64, 16), 0)
            total = jnp.zeros((64, CHUNK), F32)
            for c in range(4):
                take = jnp.where((slot == iota((64, 16), 1)) & (chunk == c), 1.0, 0.0)
                first = route * HALF + c * CHUNK
                total += jnp.dot(
                    take.astype(BF16),
                    last[:, first : first + CHUNK],
                    preferred_element_type=F32,
                )
            compact[which, route] = total.astype(BF16)
            mine = pl.ds(pl.multiple_of(here * 16, 16), 16)
            rows_over[which, route, mine, :] = compact[which, route, mine, :]
            for d in ORDER:
                there = lax.rem(here + d, 4)
                copy = remote(
                    compact.at[which, route, pl.ds(pl.multiple_of(there * 16, 16), 16), :],
                    rows_over.at[which, route, mine, :],
                    over_send.at[which, route, d],
                    over_recv.at[which, route, d],
                    peer(second_axis(route), d),
                )
                copy.start()
                sends.append(copy)
                arrivals[route].append(copy)
        return arrivals, owns

    def combine(which, arrivals, owns):
        finals = []
        for route in range(2):
            for copy in arrivals[route]:
                copy.wait_recv()
            for copy in owns[route]:
                copy.wait()
            ranks = [pick_row(rank_ref[route], expert_at(route, p)) for p in range(4)]
            shares = [pick_row(share_ref[route], expert_at(route, p)) for p in range(4)]
            for c in range(4):
                main, rest = [], []
                for p in range(4):
                    hit = slot_rows(ranks[p], c) == iota((4 * MAIN + 16, 4 * TOK), 0)
                    value = shares[p] if which == 0 else 1.0
                    spread = jnp.where(hit, value, 0.0)
                    main.append(spread[: 4 * MAIN])
                    rest.append(spread[4 * MAIN :])
                main = jnp.concatenate(main, axis=0).astype(BF16)
                rest = jnp.concatenate(rest, axis=0).astype(BF16)
                columns = slice(c * CHUNK, (c + 1) * CHUNK)
                along = (((0,), (0,)), ((), ()))
                total = lax.dot_general(
                    main,
                    rows[which, route, :, :, columns].reshape(16 * MAIN, CHUNK),
                    along,
                    preferred_element_type=F32,
                ) + lax.dot_general(
                    rest, rows_over[which, route], along, preferred_element_type=F32
                )
                partial[which, route, :, columns] = total.astype(BF16)
            here = coord(first_axis(route))
            for d in ORDER:
                there = lax.rem(here + d, 4)
                copy = remote(
                    partial.at[which, route, pl.ds(pl.multiple_of(there * TOK, TOK), TOK), :],
                    final.at[which, route, d - 1],
                    part_send.at[which, route, d],
                    part_recv.at[which, route, d],
                    peer(first_axis(route), d),
                )
                copy.start()
                sends.append(copy)
                finals.append(copy)
        return finals

    def finish(which, finals, result):
        for copy in finals:
            copy.wait_recv()
        for route in range(2):
            here = coord(first_axis(route))
            own = partial[which, route, pl.ds(pl.multiple_of(here * TOK, TOK), TOK), :]
            total = own.astype(F32)
            for d in range(3):
                total += final[which, route, d].astype(F32)
            result[:, route * HALF : (route + 1) * HALF] = total.astype(BF16)

    along = (((0,), (0,)), ((), ()))
    y = lax.axis_index("dp") // 2

    def weight_block(ahead):
        first = lax.rem(y + ahead, 4) * 512
        cols = pl.ds(pl.multiple_of(first, 512), 512)

        @pl.loop(0, 3)
        def _(n):
            piece = pl.ds(pl.multiple_of(n * 256, 256), 256)
            sum_out[ahead, piece, :] = lax.dot_general(
                hb[:, piece], gb[:, cols], along, preferred_element_type=F32
            ).astype(BF16)

        @pl.loop(0, 2)
        def _(n):
            piece = pl.ds(pl.multiple_of(n * 256, 256), 256)
            part = pl.ds(pl.multiple_of(first + n * 256, 256), 256)
            sum_in[ahead, piece, :] = lax.dot_general(
                xb[:, part], pgb[...], along, preferred_element_type=F32
            ).astype(BF16)

    half_in = (pl.ds(0, 256), pl.ds(256, 256))
    half_out = (pl.ds(0, HID // 2), pl.ds(HID // 2, HID // 2))

    def pass_half(ahead, half, side, dst_in, dst_out, slot):
        found = []
        for kind, (src, dst) in enumerate(
            (
                (sum_out.at[ahead, half_out[half], :], dst_out),
                (sum_in.at[ahead, half_in[half], :], dst_in),
            )
        ):
            copy = remote(
                src,
                dst,
                dp_send.at[slot, side, kind],
                dp_recv.at[slot, side, kind],
                along_y((1, 3)[side]),
            )
            copy.start()
            sends.append(copy)
            found.append(copy)
        return found

    out_state = first_hop(0)
    for copy in fetch:
        copy.wait()
    weight_block(2)
    near = [
        pass_half(2, side, side, near_in.at[side], near_out.at[side], 0) for side in range(2)
    ]
    ends = []
    for side, ahead in ((0, 1), (1, 3)):
        weight_block(ahead)
        half = 1 - side
        ends += pass_half(
            ahead,
            half,
            side,
            far_in.at[side, half_in[half], :],
            far_out.at[side, half_out[half], :],
            1,
        )

    @pl.loop(0, WIDTH // 256)
    def _(n):
        @pl.when(n + 1 < WIDTH // 256)
        def _():
            wgu_tile(n + 1).start()

        wgu_tile(n).wait()
        cols = pl.ds(pl.multiple_of(n * 256, 256), 256)
        sig[:, cols] = lax.dot_general(
            pgb[:ROWS, :],
            wgu[lax.rem(n, 2)],
            (((1,), (1,)), ((), ())),
            preferred_element_type=F32,
        ).astype(BF16)

    sig_state = first_hop(1)
    weight_block(0)
    for side, ahead in ((0, 1), (1, 3)):
        for copy in near[side]:
            copy.wait_recv()
        part = half_in[side]
        sum_in[ahead, part, :] = (
            sum_in[ahead, part, :].astype(F32) + near_in[side].astype(F32)
        ).astype(BF16)
        part = half_out[side]
        sum_out[ahead, part, :] = (
            sum_out[ahead, part, :].astype(F32) + near_out[side].astype(F32)
        ).astype(BF16)
        ends += pass_half(
            ahead,
            side,
            side,
            far_in.at[side, half_in[side], :],
            far_out.at[side, half_out[side], :],
            2,
        )
    out_finals = combine(0, *out_state)
    sig_finals = combine(1, *sig_state)
    finish(0, out_finals, layer_out)
    finish(1, sig_finals, token_grad)
    for copy in ends:
        copy.wait_recv()

    @pl.loop(0, 4)
    def _(n):
        part = pl.ds(pl.multiple_of(n * 128, 128), 128)
        total = sum_in[0, part, :].astype(F32)
        total += far_in[0, part, :].astype(F32) + far_in[1, part, :].astype(F32)
        grad_in[part, :] = total.astype(BF16)
        part = pl.ds(pl.multiple_of(n * 192, 192), 192)
        total = sum_out[0, part, :].astype(F32)
        total += far_out[0, part, :].astype(F32) + far_out[1, part, :].astype(F32)
        grad_out[part, :] = total.astype(BF16)

    for copy in sends:
        copy.wait_send()


VMEM = pl.BlockSpec(memory_space=pltpu.VMEM)
ANY = pl.BlockSpec(memory_space=pl.ANY)
DMA = pltpu.SemaphoreType.DMA


def dispatch(ids, gates, tokens, cotangent, gate_up, down_weight):
    table = jax.ShapeDtypeStruct((2, 16, 4 * TOK), F32)
    return pl.pallas_call(
        dispatch_kernel,
        out_shape=(
            jax.ShapeDtypeStruct((ROWS, WIDTH), BF16),
            jax.ShapeDtypeStruct((2 * ROWS, HALF), BF16),
            jax.ShapeDtypeStruct((2 * ROWS, HALF), BF16),
            jax.ShapeDtypeStruct((2 * ROWS, HID), BF16),
            jax.ShapeDtypeStruct((2 * ROWS, 2 * HID), BF16),
            table,
            table,
        ),
        in_specs=[VMEM] * 4 + [ANY] * 2,
        out_specs=(ANY,) * 5 + (VMEM,) * 2,
        scratch_shapes=[
            pltpu.VMEM((WIDTH, 2 * HID), BF16),
            pltpu.VMEM((HID, WIDTH), BF16),
            pltpu.VMEM((16, 2 * TOK), F32),
            pltpu.VMEM((2, 4, 16, 2 * TOK), F32),
            pltpu.VMEM((2, 2, 4 * TOK, HALF), BF16),
            pltpu.VMEM((2, 2, 3, 4 * MAIN, HALF), BF16),
            pltpu.VMEM((2, 2, 3, 16, CHUNK), BF16),
            pltpu.VMEM((2, 2, 64, CHUNK), BF16),
            pltpu.VMEM((ROWS, WIDTH), BF16),
            pltpu.VMEM((ROWS, WIDTH), BF16),
            pltpu.VMEM((ROWS, 2 * HID), F32),
            pltpu.VMEM((ROWS, HID), BF16),
            pltpu.VMEM((ROWS, 2 * HID), BF16),
            pltpu.VMEM((ROWS, WIDTH), BF16),
            DMA((16,)),
            DMA((2, 4)),
            DMA((2, 4)),
            DMA((2, 2, 4)),
            DMA((2, 2, 4)),
            DMA((2, 2, 4, 4)),
            DMA((2, 2, 4, 4)),
            DMA((2, 2, 4)),
            DMA((2, 2, 4)),
            DMA((10,)),
            DMA((10,)),
        ],
        compiler_params=pltpu.CompilerParams(
            collective_id=0, has_side_effects=True, vmem_limit_bytes=60 << 20
        ),
        cost_estimate=pl.CostEstimate(
            flops=20 * 10**9, bytes_accessed=40 * 10**6, transcendentals=10**6
        ),
    )(ids, gates, tokens, cotangent, gate_up, down_weight)


def give_back(out_rows, gate_up, x_rows, g_rows, hidden, pre_grad, rank, share):
    result = jax.ShapeDtypeStruct((TOK, WIDTH), BF16)
    return pl.pallas_call(
        return_kernel,
        out_shape=(
            result,
            result,
            jax.ShapeDtypeStruct((512, 2 * HID), BF16),
            jax.ShapeDtypeStruct((HID, 512), BF16),
        ),
        in_specs=[ANY] * 6 + [VMEM] * 2,
        out_specs=(VMEM,) * 4,
        scratch_shapes=[
            pltpu.VMEM((2 * ROWS, HALF), BF16),
            pltpu.VMEM((2 * ROWS, HALF), BF16),
            pltpu.VMEM((2 * ROWS, HID), BF16),
            pltpu.VMEM((2 * ROWS, 2 * HID), BF16),
            pltpu.VMEM((2, 256, 2 * HID), BF16),
            pltpu.VMEM((ROWS, WIDTH), BF16),
            pltpu.VMEM((4, 512, 2 * HID), BF16),
            pltpu.VMEM((4, HID, 512), BF16),
            pltpu.VMEM((2, 256, 2 * HID), BF16),
            pltpu.VMEM((2, HID // 2, 512), BF16),
            pltpu.VMEM((2, 512, 2 * HID), BF16),
            pltpu.VMEM((2, HID, 512), BF16),
            pltpu.VMEM((16, WIDTH), BF16),
            pltpu.VMEM((2, 2, 64, CHUNK), BF16),
            pltpu.VMEM((2, 2, 4, 4 * MAIN, HALF), BF16),
            pltpu.VMEM((2, 2, 64, CHUNK), BF16),
            pltpu.VMEM((2, 2, 4 * TOK, HALF), BF16),
            pltpu.VMEM((2, 2, 3, TOK, HALF), BF16),
            DMA((22,)),
            DMA((2,)),
            DMA((2, 2, 4, 4)),
            DMA((2, 2, 4, 4)),
            DMA((2, 2, 4)),
            DMA((2, 2, 4)),
            DMA((2, 2, 4)),
            DMA((2, 2, 4)),
            DMA((3, 2, 2)),
            DMA((3, 2, 2)),
        ],
        compiler_params=pltpu.CompilerParams(
            collective_id=1, has_side_effects=True, vmem_limit_bytes=62 << 20
        ),
        cost_estimate=pl.CostEstimate(
            flops=26 * 10**9, bytes_accessed=100 * 10**6, transcendentals=0
        ),
    )(out_rows, gate_up, x_rows, g_rows, hidden, pre_grad, rank, share)


def per_device(tokens, cotangent, expert_ids, gate_fixed, gate_up, down_weight):
    out_rows, x_rows, g_rows, hidden, pre_grad, rank, share = dispatch(
        expert_ids.T, gate_fixed.T, tokens, cotangent, gate_up, down_weight
    )
    layer_out, token_grad, grad_in, grad_out = give_back(
        out_rows, gate_up, x_rows, g_rows, hidden, pre_grad, rank, share
    )
    return layer_out, token_grad, grad_in[None], grad_out[None]


def solution(mesh):
    rows = P(("ep", "dp"), None)
    return jax.shard_map(
        per_device,
        mesh=mesh,
        in_specs=(rows, rows, rows, rows, P("ep", None, None), P("ep", None, None)),
        out_specs=(rows, rows, P("ep", "dp", None), P("ep", None, "dp")),
        check_vma=False,
    )
```

```python
import functools

import jax
import jax.numpy as jnp
from jax import lax
from jax.experimental import pallas as pl
from jax.experimental.pallas import tpu as pltpu
from jax.sharding import PartitionSpec as P

BF16 = jnp.bfloat16
F32 = jnp.float32
MESH = pl.DeviceIdType.MESH
TOK = 64
WIDTH = 4096
HALF = WIDTH // 2
CHUNK = HALF // 4
HID = 768
MAIN = 32
ROWS = 16 * MAIN + 16
ORDER = (2, 1, 3)


def place():
    ep = lax.axis_index("ep")
    return ep // 4, ep % 4


def peer(axis, distance):
    z, x = place()
    if axis == "z":
        z = lax.rem(z + distance, 4)
    else:
        x = lax.rem(x + distance, 4)
    return {"ep": z * 4 + x, "dp": lax.axis_index("dp")}


def along_y(distance):
    dp = lax.axis_index("dp")
    return {"ep": lax.axis_index("ep"), "dp": lax.rem(dp + 2 * distance, 8)}


def other_core():
    dp = lax.axis_index("dp")
    return {"ep": lax.axis_index("ep"), "dp": dp + 1 - 2 * lax.rem(dp, 2)}


def first_axis(route):
    return ("z", "x")[route]


def second_axis(route):
    return ("x", "z")[route]


def coord(axis):
    z, x = place()
    return z if axis == "z" else x


def expert_at(route, position):
    z, x = place()
    return z * 4 + position if route == 0 else position * 4 + x


def iota(shape, dim):
    return lax.broadcasted_iota(jnp.int32, shape, dim)


def enter(peers):
    barrier = pltpu.get_barrier_semaphore()
    for device in peers:
        pl.semaphore_signal(barrier, 1, device_id=device, device_id_type=MESH)
    pl.semaphore_wait(barrier, len(peers))


def remote(src, dst, send_sem, recv_sem, device):
    return pltpu.make_async_remote_copy(
        src_ref=src,
        dst_ref=dst,
        send_sem=send_sem,
        recv_sem=recv_sem,
        device_id=device,
        device_id_type=MESH,
    )


def pick_row(table, index):
    rows = iota(table.shape, 0)
    return jnp.sum(jnp.where(rows == index, table, 0.0), axis=0, keepdims=True)


def slot_rows(rank, chunk):
    source = iota((1, 4 * TOK), 1) // TOK
    rank = rank.astype(jnp.int32)
    main = jnp.where(rank >= 0, rank + MAIN * source, -1)
    return jnp.where(rank == MAIN, 4 * MAIN + 4 * chunk + source, main)


def overflow_target(route, shape, dim):
    row = iota(shape, dim)
    sender, chunk, source = row // 16, lax.rem(row, 16) // 4, lax.rem(row, 4)
    slot = sender * 4 + source if route == 0 else source * 4 + sender
    return slot, chunk


def dispatch_kernel(
    ids_ref,
    gate_ref,
    tok_ref,
    cot_ref,
    wgu_hbm,
    wd_hbm,
    out_hbm,
    x_hbm,
    g_hbm,
    h_hbm,
    pre_hbm,
    rank_out,
    share_out,
    wgu,
    wd,
    meta_own,
    meta,
    gathered,
    staged,
    staged_over,
    over,
    xbuf,
    own,
    own_over,
    pre,
    hid,
    obuf,
    local_sem,
    meta_send,
    meta_recv,
    gat_send,
    gat_recv,
    main_send,
    main_recv,
    over_send,
    over_recv,
    core_send,
    core_recv,
):
    z, x = place()
    load_gu = pltpu.make_async_copy(wgu_hbm.at[0], wgu, local_sem.at[0])
    load_d = pltpu.make_async_copy(wd_hbm.at[0], wd, local_sem.at[1])
    load_gu.start()
    load_d.start()

    gates = gate_ref[...].astype(F32)
    share = gates / jnp.sum(gates, axis=0, keepdims=True)
    ids = ids_ref[...]
    expert = iota((16, TOK), 0)
    named = jnp.zeros((16, TOK), F32)
    weight = jnp.zeros((16, TOK), F32)
    for k in range(8):
        hit = ids[k : k + 1, :] == expert
        named += jnp.where(hit, 1.0, 0.0)
        weight += jnp.where(hit, share[k : k + 1, :], 0.0)
    before = jnp.where(iota((TOK, TOK), 0) < iota((TOK, TOK), 1), 1.0, 0.0)
    rank = jnp.dot(named.astype(BF16), before.astype(BF16), preferred_element_type=F32)
    rank = jnp.where(named > 0.0, rank, -1.0)
    meta_own[...] = jnp.concatenate([rank, weight], axis=1)

    enter([peer(axis, d) for axis in ("z", "x") for d in ORDER] + [other_core()])

    sends = []
    meta_recvs = []
    for route in range(2):
        here = coord(first_axis(route))
        for d in ORDER:
            copy = remote(
                meta_own,
                meta.at[route, here],
                meta_send.at[route, d],
                meta_recv.at[route, d],
                peer(first_axis(route), d),
            )
            copy.start()
            sends.append(copy)
            meta_recvs.append(copy)
        meta[route, pl.ds(here, 1)] = meta_own[...][None]

    sources = (tok_ref, cot_ref)

    def block(which, route, position, columns):
        rows = pl.ds(pl.multiple_of(position * TOK, TOK), TOK)
        return gathered.at[which, route, rows, columns]

    def gather_start(which):
        copies = [{}, {}]
        for d in (1, 3):
            for route in range(2):
                here = coord(first_axis(route))
                copy = remote(
                    sources[which].at[:, pl.ds(route * HALF, HALF)],
                    block(which, route, here, pl.ds(0, HALF)),
                    gat_send.at[which, route, d],
                    gat_recv.at[which, route, d],
                    peer(first_axis(route), d),
                )
                copy.start()
                sends.append(copy)
                copies[route][d] = copy
        for route in range(2):
            here = coord(first_axis(route))
            gathered[which, route, pl.ds(pl.multiple_of(here * TOK, TOK), TOK), :] = sources[
                which
            ][:, route * HALF : (route + 1) * HALF]
        return copies

    def gather_pass(which, copies):
        passed = []
        for d in (1, 3):
            for route in range(2):
                copies[route][d].wait_recv()
                axis = first_axis(route)
                behind = lax.rem(coord(axis) + 4 - d, 4)
                columns = pl.ds((d // 2) * (HALF // 2), HALF // 2)
                copy = remote(
                    block(which, route, behind, columns),
                    block(which, route, behind, columns),
                    gat_send.at[which, route, d - 1],
                    gat_recv.at[which, route, d - 1],
                    peer(axis, d),
                )
                copy.start()
                sends.append(copy)
                passed.append(copy)
        return passed

    tok_copies = gather_start(0)
    cot_copies = gather_start(1)
    for copy in meta_recvs:
        copy.wait_recv()
    for route in range(2):
        rank_out[route] = jnp.concatenate([meta[route, s][:, :TOK] for s in range(4)], axis=1)
        share_out[route] = jnp.concatenate([meta[route, s][:, TOK:] for s in range(4)], axis=1)

    buffers = (xbuf, g_hbm)

    def select(which, route, d):
        position = lax.rem(coord(second_axis(route)) + d, 4)
        expert = expert_at(route, position)
        rank_row = pick_row(rank_out[route], expert)
        share_row = pick_row(share_out[route], expert)
        here = coord(second_axis(route))
        target = buffers[which]
        total = jnp.zeros((16, CHUNK), F32)
        for c in range(4):
            hit = slot_rows(rank_row, c) == iota((4 * MAIN + 16, 4 * TOK), 0)
            choose = jnp.where(hit, 1.0, 0.0).astype(BF16)
            rows = jnp.dot(
                choose,
                gathered[which, route, :, c * CHUNK : (c + 1) * CHUNK],
                preferred_element_type=F32,
            )
            if which == 1:
                rows = rows * jnp.sum(jnp.where(hit, share_row, 0.0), axis=1, keepdims=True)
            main = rows[: 4 * MAIN].astype(BF16)
            total += rows[4 * MAIN :]
            if which == 1 and not d:
                own[route, :, c * CHUNK : (c + 1) * CHUNK] = main
            elif d:
                staged[which, route, d - 1, :, c * CHUNK : (c + 1) * CHUNK] = main
            else:
                columns = slice(route * HALF + c * CHUNK, route * HALF + (c + 1) * CHUNK)
                if route == 0:
                    target[pl.ds(pl.multiple_of(here * 128, 128), 128), columns] = main
                else:
                    for s in range(4):
                        first = pl.multiple_of((s * 4 + here) * MAIN, MAIN)
                        target[pl.ds(first, MAIN), columns] = main[s * MAIN : (s + 1) * MAIN]
        mine = pl.ds(pl.multiple_of(here * 16, 16), 16)
        if not d:
            over[which, route, mine, :] = total.astype(BF16)
            return []
        staged_over[which, route, d - 1] = total.astype(BF16)
        device = peer(second_axis(route), d)
        columns = pl.ds(route * HALF, HALF)
        copies = []
        if route == 0:
            copies.append(
                remote(
                    staged.at[which, route, d - 1],
                    target.at[pl.ds(pl.multiple_of(here * 128, 128), 128), columns],
                    main_send.at[which, route, d, 0],
                    main_recv.at[which, route, d, 0],
                    device,
                )
            )
        else:
            for s in range(4):
                first = pl.multiple_of((s * 4 + here) * MAIN, MAIN)
                copies.append(
                    remote(
                        staged.at[which, route, d - 1, pl.ds(s * MAIN, MAIN), :],
                        target.at[pl.ds(first, MAIN), columns],
                        main_send.at[which, route, d, s],
                        main_recv.at[which, route, d, s],
                        device,
                    )
                )
        copies.append(
            remote(
                staged_over.at[which, route, d - 1],
                over.at[which, route, mine, :],
                over_send.at[which, route, d],
                over_recv.at[which, route, d],
                device,
            )
        )
        for copy in copies:
            copy.start()
        sends.extend(copies)
        return copies

    def second_hop(which, passed):
        arrivals = []
        for copy in passed:
            copy.wait_recv()
        for d in ORDER:
            for route in range(2):
                arrivals.extend(select(which, route, d))
        return arrivals

    def finish(which, arrivals):
        for copy in arrivals:
            copy.wait_recv()
        for route in range(2):
            slot, chunk = overflow_target(route, (16, 64), 1)
            for c in range(4):
                spread = jnp.where((slot == iota((16, 64), 0)) & (chunk == c), 1.0, 0.0)
                first = route * HALF + c * CHUNK
                tail = jnp.dot(
                    spread.astype(BF16), over[which, route], preferred_element_type=F32
                ).astype(BF16)
                if which == 0:
                    xbuf[16 * MAIN : ROWS, first : first + CHUNK] = tail
                else:
                    own_over[:, first : first + CHUNK] = tail

    tok_passed = gather_pass(0, tok_copies)
    cot_passed = gather_pass(1, cot_copies)
    x_arrivals = second_hop(0, tok_passed)
    g_arrivals = second_hop(1, cot_passed)
    for which in range(2):
        for route in range(2):
            select(which, route, 0)
    load_gu.wait()
    load_d.wait()

    core = lax.rem(lax.axis_index("dp"), 2)
    stores = []
    shared = []

    def store(src, dst):
        copy = pltpu.make_async_copy(src, dst, local_sem.at[2 + len(stores)])
        copy.start()
        stores.append(copy)

    def share(src, dst):
        slot = len(shared)
        copy = remote(src, dst, core_send.at[slot], core_recv.at[slot], other_core())
        copy.start()
        shared.append(copy)

    for route in range(2):
        here = coord(second_axis(route))
        columns = pl.ds(route * HALF, HALF)
        if route == 0:
            first = pl.multiple_of(here * 128, 128)
            store(own.at[route], g_hbm.at[pl.ds(first, 128), columns])
        else:
            for s in range(4):
                first = pl.multiple_of((s * 4 + here) * MAIN, MAIN)
                store(
                    own.at[route, pl.ds(s * MAIN, MAIN), :],
                    g_hbm.at[pl.ds(first, MAIN), columns],
                )

    mine, theirs = pl.ds(0, ROWS), pl.ds(ROWS, ROWS)

    def split(src, dst):
        for block in range(4):
            there = pl.ds(block * 512, 512)
            keep = pl.ds(pl.multiple_of((2 * block + core) * 512, 512), 512)
            give = pl.ds(pl.multiple_of((2 * block + 1 - core) * 512, 512), 512)
            share(src.at[:, give], dst.at[theirs, there])
            store(src.at[:, keep], dst.at[mine, there])

    finish(0, x_arrivals)
    split(xbuf, x_hbm)

    @pl.loop(0, 3)
    def _(n):
        u_cols = pl.ds(pl.multiple_of(n * 256, 256), 256)
        v_cols = pl.ds(pl.multiple_of(HID + n * 256, 256), 256)
        u = jnp.dot(xbuf[...], wgu[:, u_cols], preferred_element_type=F32)
        pre[:, u_cols] = u
        v = jnp.dot(xbuf[...], wgu[:, v_cols], preferred_element_type=F32)
        pre[:, v_cols] = v
        hid[:, u_cols] = (pre[:, u_cols] * jax.nn.sigmoid(pre[:, u_cols]) * v).astype(BF16)

    share(hid, h_hbm.at[theirs])
    store(pre, pre_hbm)
    store(hid, h_hbm.at[mine])

    @pl.loop(0, WIDTH // 256)
    def _(n):
        cols = pl.ds(pl.multiple_of(n * 256, 256), 256)
        obuf[:, cols] = jnp.dot(hid[...], wd[:, cols], preferred_element_type=F32).astype(BF16)

    store(obuf, out_hbm)
    finish(1, g_arrivals)
    store(own_over, g_hbm.at[pl.ds(16 * MAIN, 16), :])
    for copy in stores + shared:
        copy.wait()
    for copy in sends:
        copy.wait_send()


def return_kernel(
    out_hbm,
    wgu_hbm,
    x_hbm,
    g_hbm,
    h_hbm,
    pre_hbm,
    wd_hbm,
    rank_ref,
    share_ref,
    layer_out,
    token_grad,
    grad_out,
    own_in,
    far_in,
    xb,
    gb,
    gall,
    hb,
    pre,
    wd,
    pgb,
    wgu,
    sum_in,
    sum_out,
    near_in,
    near_out,
    far_out,
    tail,
    compact,
    rows,
    rows_over,
    partial,
    final,
    local_sem,
    wgu_sem,
    main_send,
    main_recv,
    over_send,
    over_recv,
    part_send,
    part_recv,
    dp_send,
    dp_recv,
    core_send,
    core_recv,
):
    z, x = place()
    y = lax.axis_index("dp") // 2
    core = lax.rem(lax.axis_index("dp"), 2)
    sig = gall
    inputs = (out_hbm, sig)
    mine, theirs = pl.ds(0, ROWS), pl.ds(ROWS, ROWS)
    fetch = {}

    def load(name, src, dst):
        copy = pltpu.make_async_copy(src, dst, local_sem.at[18 + len(fetch)])
        copy.start()
        fetch[name] = copy

    def columns_of(ahead, of_core):
        first = (2 * lax.rem(y + ahead, 4) + of_core) * 512
        return pl.ds(pl.multiple_of(first, 512), 512)

    def place_of(ahead):
        return pl.ds(pl.multiple_of(lax.rem(y + ahead, 4) * 512, 512), 512)

    load("h", h_hbm, hb)
    for ahead in (2, 1, 3, 0):
        load(ahead, g_hbm.at[:, columns_of(ahead, core)], gb.at[mine, place_of(ahead)])
    load("g", g_hbm, gall)
    load("d", wd_hbm.at[0], wd)
    load("pre", pre_hbm, pre)
    load("x", x_hbm, xb)
    load_tail = pltpu.make_async_copy(
        out_hbm.at[pl.ds(16 * MAIN, 16), :], tail, local_sem.at[0]
    )
    load_tail.start()

    def wgu_tile(n):
        rows = pl.ds(pl.multiple_of(n * 256, 256), 256)
        slot = lax.rem(n, 2)
        return pltpu.make_async_copy(wgu_hbm.at[0, rows, :], wgu.at[slot], wgu_sem.at[slot])

    wgu_tile(0).start()
    enter(
        [peer(axis, d) for axis in ("z", "x") for d in ORDER]
        + [along_y(d) for d in (1, 3)]
        + [other_core()]
    )
    sends = []
    swaps = {}
    for ahead in (2, 1, 3, 0):
        swaps[ahead] = remote(
            g_hbm.at[:, columns_of(ahead, 1 - core)],
            gb.at[theirs, place_of(ahead)],
            core_send.at[ahead],
            core_recv.at[ahead],
            other_core(),
        )
        swaps[ahead].start()

    def pieces(which, route, position, slot):
        columns = pl.ds(route * HALF, HALF)
        if route == 0:
            first = pl.multiple_of(position * 128, 128)
            return [
                (inputs[which].at[pl.ds(first, 128), columns], rows.at[which, route, slot])
            ]
        found = []
        for s in range(4):
            first = pl.multiple_of((s * 4 + position) * MAIN, MAIN)
            found.append(
                (
                    inputs[which].at[pl.ds(first, MAIN), columns],
                    rows.at[which, route, slot, pl.ds(s * MAIN, MAIN), :],
                )
            )
        return found

    def first_hop(which):
        arrivals = [[], []]
        for d in ORDER:
            for route in range(2):
                here = coord(second_axis(route))
                there = lax.rem(here + d, 4)
                for s, (src, dst) in enumerate(pieces(which, route, there, here)):
                    copy = remote(
                        src,
                        dst,
                        main_send.at[which, route, d, s],
                        main_recv.at[which, route, d, s],
                        peer(second_axis(route), d),
                    )
                    copy.start()
                    sends.append(copy)
                    arrivals[route].append(copy)
        owns = [[], []]
        for route in range(2):
            here = coord(second_axis(route))
            for s, (src, dst) in enumerate(pieces(which, route, here, here)):
                copy = pltpu.make_async_copy(src, dst, local_sem.at[2 + which * 8 + route * 4 + s])
                copy.start()
                owns[route].append(copy)
        if which == 0:
            load_tail.wait()
        last = tail if which == 0 else sig.at[pl.ds(16 * MAIN, 16), :]
        for route in range(2):
            here = coord(second_axis(route))
            slot, chunk = overflow_target(route, (64, 16), 0)
            total = jnp.zeros((64, CHUNK), F32)
            for c in range(4):
                take = jnp.where((slot == iota((64, 16), 1)) & (chunk == c), 1.0, 0.0)
                first = route * HALF + c * CHUNK
                total += jnp.dot(
                    take.astype(BF16),
                    last[:, first : first + CHUNK],
                    preferred_element_type=F32,
                )
            compact[which, route] = total.astype(BF16)
            mine = pl.ds(pl.multiple_of(here * 16, 16), 16)
            rows_over[which, route, mine, :] = compact[which, route, mine, :]
            for d in ORDER:
                there = lax.rem(here + d, 4)
                copy = remote(
                    compact.at[which, route, pl.ds(pl.multiple_of(there * 16, 16), 16), :],
                    rows_over.at[which, route, mine, :],
                    over_send.at[which, route, d],
                    over_recv.at[which, route, d],
                    peer(second_axis(route), d),
                )
                copy.start()
                sends.append(copy)
                arrivals[route].append(copy)
        return arrivals, owns

    def combine(which, arrivals, owns):
        finals = []
        for route in range(2):
            for copy in arrivals[route]:
                copy.wait_recv()
            for copy in owns[route]:
                copy.wait()
            ranks = [pick_row(rank_ref[route], expert_at(route, p)) for p in range(4)]
            shares = [pick_row(share_ref[route], expert_at(route, p)) for p in range(4)]
            for c in range(4):
                main, rest = [], []
                for p in range(4):
                    hit = slot_rows(ranks[p], c) == iota((4 * MAIN + 16, 4 * TOK), 0)
                    value = shares[p] if which == 0 else 1.0
                    spread = jnp.where(hit, value, 0.0)
                    main.append(spread[: 4 * MAIN])
                    rest.append(spread[4 * MAIN :])
                main = jnp.concatenate(main, axis=0).astype(BF16)
                rest = jnp.concatenate(rest, axis=0).astype(BF16)
                columns = slice(c * CHUNK, (c + 1) * CHUNK)
                along = (((0,), (0,)), ((), ()))
                total = lax.dot_general(
                    main,
                    rows[which, route, :, :, columns].reshape(16 * MAIN, CHUNK),
                    along,
                    preferred_element_type=F32,
                ) + lax.dot_general(
                    rest, rows_over[which, route], along, preferred_element_type=F32
                )
                partial[which, route, :, columns] = total.astype(BF16)
            here = coord(first_axis(route))
            for d in ORDER:
                there = lax.rem(here + d, 4)
                copy = remote(
                    partial.at[which, route, pl.ds(pl.multiple_of(there * TOK, TOK), TOK), :],
                    final.at[which, route, d - 1],
                    part_send.at[which, route, d],
                    part_recv.at[which, route, d],
                    peer(first_axis(route), d),
                )
                copy.start()
                sends.append(copy)
                finals.append(copy)
        return finals

    def finish(which, finals, result):
        for copy in finals:
            copy.wait_recv()
        for route in range(2):
            here = coord(first_axis(route))
            own = partial[which, route, pl.ds(pl.multiple_of(here * TOK, TOK), TOK), :]
            total = own.astype(F32)
            for d in range(3):
                total += final[which, route, d].astype(F32)
            result[:, route * HALF : (route + 1) * HALF] = total.astype(BF16)

    along = (((0,), (0,)), ((), ()))

    def weight_out(ahead):
        cols = place_of(ahead)

        @pl.loop(0, 3)
        def _(n):
            piece = pl.ds(pl.multiple_of(n * 256, 256), 256)
            sum_out[ahead, piece, :] = lax.dot_general(
                hb[:, piece], gb[:, cols], along, preferred_element_type=F32
            ).astype(BF16)

    def weight_in(ahead):
        first = lax.rem(y + ahead, 4) * 512

        @pl.loop(0, 2)
        def _(n):
            piece = pl.ds(pl.multiple_of(n * 256, 256), 256)
            part = pl.ds(pl.multiple_of(first + n * 256, 256), 256)
            sum_in[ahead, piece, :] = lax.dot_general(
                xb[:, part], pgb[...], along, preferred_element_type=F32
            ).astype(BF16)

    half_in = (pl.ds(0, 256), pl.ds(256, 256))
    half_out = (pl.ds(0, HID // 2), pl.ds(HID // 2, HID // 2))

    sums = (sum_out, sum_in)
    nears = (near_out, near_in)
    fars = (far_out, far_in)
    halves = (half_out, half_in)

    def pass_half(kind, ahead, half, side, dst, slot):
        copy = remote(
            sums[kind].at[ahead, halves[kind][half], :],
            dst,
            dp_send.at[slot, side, kind],
            dp_recv.at[slot, side, kind],
            along_y((1, 3)[side]),
        )
        copy.start()
        sends.append(copy)
        return copy

    def pass_near(kind):
        return [pass_half(kind, 2, side, side, nears[kind].at[side], 0) for side in range(2)]

    def pass_far(kind, side):
        ahead, half = (1, 3)[side], 1 - side
        return pass_half(kind, ahead, half, side, fars[kind].at[side, halves[kind][half], :], 1)

    def pass_sum(kind, near):
        found = []
        for side, ahead in ((0, 1), (1, 3)):
            near[side].wait_recv()
            part = halves[kind][side]
            sums[kind][ahead, part, :] = (
                sums[kind][ahead, part, :].astype(F32) + nears[kind][side].astype(F32)
            ).astype(BF16)
            found.append(
                pass_half(kind, ahead, side, side, fars[kind].at[side, part, :], 2)
            )
        return found

    ends_out, ends_in = [], []
    fetch["h"].wait()
    for ahead in (2, 1, 3):
        fetch[ahead].wait()
        swaps[ahead].wait_recv()
        weight_out(ahead)
        if ahead == 2:
            near_sent_out = pass_near(0)
            out_state = first_hop(0)
        else:
            ends_out.append(pass_far(0, ahead // 2))
    fetch["g"].wait()
    fetch["d"].wait()
    fetch["pre"].wait()

    @pl.loop(0, 3)
    def _(n):
        u_cols = pl.ds(pl.multiple_of(n * 256, 256), 256)
        v_cols = pl.ds(pl.multiple_of(HID + n * 256, 256), 256)
        grad = lax.dot_general(
            gall[...], wd[u_cols, :], (((1,), (1,)), ((), ())), preferred_element_type=F32
        )
        u = pre[:, u_cols]
        logistic = jax.nn.sigmoid(u)
        pgb[:ROWS, v_cols] = (grad * u * logistic).astype(BF16)
        pgb[:ROWS, u_cols] = (
            grad * pre[:, v_cols] * logistic * (1.0 + u * (1.0 - logistic))
        ).astype(BF16)

    swap = remote(
        pgb.at[mine], pgb.at[theirs], core_send.at[4], core_recv.at[4], other_core()
    )
    swap.start()
    fetch["x"].wait()
    swap.wait_recv()
    weight_in(2)
    near_sent_in = pass_near(1)
    ends_out += pass_sum(0, near_sent_out)
    for ahead in (1, 3):
        weight_in(ahead)
        ends_in.append(pass_far(1, ahead // 2))

    @pl.loop(0, WIDTH // 256)
    def _(n):
        @pl.when(n + 1 < WIDTH // 256)
        def _():
            wgu_tile(n + 1).start()

        wgu_tile(n).wait()
        cols = pl.ds(pl.multiple_of(n * 256, 256), 256)
        sig[:, cols] = lax.dot_general(
            pgb[:ROWS, :],
            wgu[lax.rem(n, 2)],
            (((1,), (1,)), ((), ())),
            preferred_element_type=F32,
        ).astype(BF16)

    sig_state = first_hop(1)
    fetch[0].wait()
    swaps[0].wait_recv()
    weight_out(0)
    weight_in(0)
    store_own = pltpu.make_async_copy(sum_in.at[0], own_in, local_sem.at[1])
    store_own.start()
    out_finals = combine(0, *out_state)
    ends_in += pass_sum(1, near_sent_in)
    for copy in ends_out:
        copy.wait_recv()

    @pl.loop(0, 4)
    def _(n):
        part = pl.ds(pl.multiple_of(n * 192, 192), 192)
        total = sum_out[0, part, :].astype(F32)
        total += far_out[0, part, :].astype(F32) + far_out[1, part, :].astype(F32)
        grad_out[part, :] = total.astype(BF16)

    finish(0, out_finals, layer_out)
    sig_finals = combine(1, *sig_state)
    finish(1, sig_finals, token_grad)
    store_own.wait()
    for copy in ends_in:
        copy.wait_recv()
    for copy in sends + [swaps[ahead] for ahead in range(4)] + [swap]:
        copy.wait_send()


def last_kernel(out_in, grad_in, down_in, own_in, far_in, layer_out, token_grad, gate_up, down):
    layer_out[...] = out_in[...]
    token_grad[...] = grad_in[...]
    down[...] = down_in[...]
    total = far_in[0].astype(F32) + far_in[1].astype(F32)
    gate_up[...] = (total + own_in[...].astype(F32)).astype(BF16)


VMEM = pl.BlockSpec(memory_space=pltpu.VMEM)
ANY = pl.BlockSpec(memory_space=pl.ANY)
DMA = pltpu.SemaphoreType.DMA


def dispatch(ids, gates, tokens, cotangent, gate_up, down_weight):
    table = jax.ShapeDtypeStruct((2, 16, 4 * TOK), F32)
    return pl.pallas_call(
        dispatch_kernel,
        out_shape=(
            jax.ShapeDtypeStruct((ROWS, WIDTH), BF16),
            jax.ShapeDtypeStruct((2 * ROWS, HALF), BF16),
            jax.ShapeDtypeStruct((ROWS, WIDTH), BF16),
            jax.ShapeDtypeStruct((2 * ROWS, HID), BF16),
            jax.ShapeDtypeStruct((ROWS, 2 * HID), F32),
            table,
            table,
        ),
        in_specs=[VMEM] * 4 + [ANY] * 2,
        out_specs=(ANY,) * 5 + (VMEM,) * 2,
        scratch_shapes=[
            pltpu.VMEM((WIDTH, 2 * HID), BF16),
            pltpu.VMEM((HID, WIDTH), BF16),
            pltpu.VMEM((16, 2 * TOK), F32),
            pltpu.VMEM((2, 4, 16, 2 * TOK), F32),
            pltpu.VMEM((2, 2, 4 * TOK, HALF), BF16),
            pltpu.VMEM((2, 2, 3, 4 * MAIN, HALF), BF16),
            pltpu.VMEM((2, 2, 3, 16, CHUNK), BF16),
            pltpu.VMEM((2, 2, 64, CHUNK), BF16),
            pltpu.VMEM((ROWS, WIDTH), BF16),
            pltpu.VMEM((2, 4 * MAIN, HALF), BF16),
            pltpu.VMEM((16, WIDTH), BF16),
            pltpu.VMEM((ROWS, 2 * HID), F32),
            pltpu.VMEM((ROWS, HID), BF16),
            pltpu.VMEM((ROWS, WIDTH), BF16),
            DMA((16,)),
            DMA((2, 4)),
            DMA((2, 4)),
            DMA((2, 2, 4)),
            DMA((2, 2, 4)),
            DMA((2, 2, 4, 4)),
            DMA((2, 2, 4, 4)),
            DMA((2, 2, 4)),
            DMA((2, 2, 4)),
            DMA((5,)),
            DMA((5,)),
        ],
        compiler_params=pltpu.CompilerParams(
            collective_id=0, has_side_effects=True, vmem_limit_bytes=60 << 20
        ),
        cost_estimate=pl.CostEstimate(
            flops=20 * 10**9, bytes_accessed=40 * 10**6, transcendentals=10**6
        ),
    )(ids, gates, tokens, cotangent, gate_up, down_weight)


def give_back(out_rows, gate_up, x_rows, g_rows, hidden, pre_act, down_weight, rank, share):
    result = jax.ShapeDtypeStruct((TOK, WIDTH), BF16)
    return pl.pallas_call(
        return_kernel,
        out_shape=(
            result,
            result,
            jax.ShapeDtypeStruct((HID, 512), BF16),
            jax.ShapeDtypeStruct((512, 2 * HID), BF16),
            jax.ShapeDtypeStruct((2, 512, 2 * HID), BF16),
        ),
        in_specs=[ANY] * 7 + [VMEM] * 2,
        out_specs=(VMEM,) * 3 + (ANY,) * 2,
        scratch_shapes=[
            pltpu.VMEM((2 * ROWS, HALF), BF16),
            pltpu.VMEM((2 * ROWS, HALF), BF16),
            pltpu.VMEM((ROWS, WIDTH), BF16),
            pltpu.VMEM((2 * ROWS, HID), BF16),
            pltpu.VMEM((ROWS, 2 * HID), F32),
            pltpu.VMEM((HID, WIDTH), BF16),
            pltpu.VMEM((2 * ROWS, 2 * HID), BF16),
            pltpu.VMEM((2, 256, 2 * HID), BF16),
            pltpu.VMEM((4, 512, 2 * HID), BF16),
            pltpu.VMEM((4, HID, 512), BF16),
            pltpu.VMEM((2, 256, 2 * HID), BF16),
            pltpu.VMEM((2, HID // 2, 512), BF16),
            pltpu.VMEM((2, HID, 512), BF16),
            pltpu.VMEM((16, WIDTH), BF16),
            pltpu.VMEM((2, 2, 64, CHUNK), BF16),
            pltpu.VMEM((2, 2, 4, 4 * MAIN, HALF), BF16),
            pltpu.VMEM((2, 2, 64, CHUNK), BF16),
            pltpu.VMEM((2, 2, 4 * TOK, HALF), BF16),
            pltpu.VMEM((2, 2, 3, TOK, HALF), BF16),
            DMA((27,)),
            DMA((2,)),
            DMA((2, 2, 4, 4)),
            DMA((2, 2, 4, 4)),
            DMA((2, 2, 4)),
            DMA((2, 2, 4)),
            DMA((2, 2, 4)),
            DMA((2, 2, 4)),
            DMA((3, 2, 2)),
            DMA((3, 2, 2)),
            DMA((5,)),
            DMA((5,)),
        ],
        compiler_params=pltpu.CompilerParams(
            collective_id=1, has_side_effects=True, vmem_limit_bytes=62 << 20
        ),
        cost_estimate=pl.CostEstimate(
            flops=26 * 10**9, bytes_accessed=100 * 10**6, transcendentals=0
        ),
    )(out_rows, gate_up, x_rows, g_rows, hidden, pre_act, down_weight, rank, share)


def last(out, grad, down, own, far):
    steps = 4

    def cut(shape):
        return pl.BlockSpec((shape[0] // steps, shape[1]), lambda n: (n, 0))

    row, wide, tall = (TOK, WIDTH), (512, 2 * HID), (HID, 512)
    outs = (row, row, wide, tall)
    return pl.pallas_call(
        last_kernel,
        grid=(steps,),
        out_shape=tuple(jax.ShapeDtypeStruct(shape, BF16) for shape in outs),
        in_specs=[
            cut(row),
            cut(row),
            cut(tall),
            cut(wide),
            pl.BlockSpec((2, wide[0] // steps, wide[1]), lambda n: (0, n, 0)),
        ],
        out_specs=tuple(cut(shape) for shape in outs),
        cost_estimate=pl.CostEstimate(
            flops=10**6, bytes_accessed=12 * 10**6, transcendentals=0
        ),
    )(out, grad, down, own, far)


def per_device(tokens, cotangent, expert_ids, gate_fixed, gate_up, down_weight):
    out_rows, x_rows, g_rows, hidden, pre_act, rank, share = dispatch(
        expert_ids.T, gate_fixed.T, tokens, cotangent, gate_up, down_weight
    )
    layer_out, token_grad, grad_in, grad_out = last(
        *give_back(
            out_rows, gate_up, x_rows, g_rows, hidden, pre_act, down_weight, rank, share
        )
    )
    return layer_out, token_grad, grad_in[None], grad_out[None]


def solution(mesh):
    rows = P(("ep", "dp"), None)
    return jax.shard_map(
        per_device,
        mesh=mesh,
        in_specs=(rows, rows, rows, rows, P("ep", None, None), P("ep", None, None)),
        out_specs=(rows, rows, P("ep", "dp", None), P("ep", None, "dp")),
        check_vma=False,
    )
```

```python
import functools

import jax
import jax.numpy as jnp
from jax import lax
from jax.experimental import pallas as pl
from jax.experimental.pallas import tpu as pltpu
from jax.sharding import PartitionSpec as P

BF16 = jnp.bfloat16
F32 = jnp.float32
MESH = pl.DeviceIdType.MESH
TOK = 64
WIDTH = 4096
HALF = WIDTH // 2
CHUNK = HALF // 4
HID = 768
MAIN = 32
ROWS = 16 * MAIN + 16
ORDER = (2, 1, 3)


def place():
    ep = lax.axis_index("ep")
    return ep // 4, ep % 4


def peer(axis, distance):
    z, x = place()
    if axis == "z":
        z = lax.rem(z + distance, 4)
    else:
        x = lax.rem(x + distance, 4)
    return {"ep": z * 4 + x, "dp": lax.axis_index("dp")}


def along_y(distance):
    dp = lax.axis_index("dp")
    return {"ep": lax.axis_index("ep"), "dp": lax.rem(dp + 2 * distance, 8)}


def other_core():
    dp = lax.axis_index("dp")
    return {"ep": lax.axis_index("ep"), "dp": dp + 1 - 2 * lax.rem(dp, 2)}


def first_axis(route):
    return ("z", "x")[route]


def second_axis(route):
    return ("x", "z")[route]


def coord(axis):
    z, x = place()
    return z if axis == "z" else x


def expert_at(route, position):
    z, x = place()
    return z * 4 + position if route == 0 else position * 4 + x


def iota(shape, dim):
    return lax.broadcasted_iota(jnp.int32, shape, dim)


def enter(peers):
    barrier = pltpu.get_barrier_semaphore()
    for device in peers:
        pl.semaphore_signal(barrier, 1, device_id=device, device_id_type=MESH)
    pl.semaphore_wait(barrier, len(peers))


def remote(src, dst, send_sem, recv_sem, device):
    return pltpu.make_async_remote_copy(
        src_ref=src,
        dst_ref=dst,
        send_sem=send_sem,
        recv_sem=recv_sem,
        device_id=device,
        device_id_type=MESH,
    )


def pick_row(table, index):
    rows = iota(table.shape, 0)
    return jnp.sum(jnp.where(rows == index, table, 0.0), axis=0, keepdims=True)


def slot_rows(rank, chunk):
    source = iota((1, 4 * TOK), 1) // TOK
    rank = rank.astype(jnp.int32)
    main = jnp.where(rank >= 0, rank + MAIN * source, -1)
    return jnp.where(rank == MAIN, 4 * MAIN + 4 * chunk + source, main)


def overflow_target(route, shape, dim):
    row = iota(shape, dim)
    sender, chunk, source = row // 16, lax.rem(row, 16) // 4, lax.rem(row, 4)
    slot = sender * 4 + source if route == 0 else source * 4 + sender
    return slot, chunk


def dispatch_kernel(
    ids_ref,
    gate_ref,
    tok_ref,
    cot_ref,
    wgu_hbm,
    wd_hbm,
    out_hbm,
    x_hbm,
    g_hbm,
    h_hbm,
    pre_hbm,
    rank_out,
    share_out,
    wgu,
    wd,
    meta_own,
    meta,
    gathered,
    staged,
    staged_over,
    over,
    xbuf,
    own,
    own_over,
    pre,
    hid,
    obuf,
    local_sem,
    meta_send,
    meta_recv,
    gat_send,
    gat_recv,
    main_send,
    main_recv,
    over_send,
    over_recv,
    core_send,
    core_recv,
):
    z, x = place()
    load_gu = pltpu.make_async_copy(wgu_hbm.at[0], wgu, local_sem.at[0])
    load_d = pltpu.make_async_copy(wd_hbm.at[0], wd, local_sem.at[1])
    load_gu.start()
    load_d.start()

    gates = gate_ref[...].astype(F32)
    share = gates / jnp.sum(gates, axis=0, keepdims=True)
    ids = ids_ref[...]
    expert = iota((16, TOK), 0)
    named = jnp.zeros((16, TOK), F32)
    weight = jnp.zeros((16, TOK), F32)
    for k in range(8):
        hit = ids[k : k + 1, :] == expert
        named += jnp.where(hit, 1.0, 0.0)
        weight += jnp.where(hit, share[k : k + 1, :], 0.0)
    before = jnp.where(iota((TOK, TOK), 0) < iota((TOK, TOK), 1), 1.0, 0.0)
    rank = jnp.dot(named.astype(BF16), before.astype(BF16), preferred_element_type=F32)
    rank = jnp.where(named > 0.0, rank, -1.0)
    meta_own[...] = jnp.concatenate([rank, weight], axis=1)

    enter([peer(axis, d) for axis in ("z", "x") for d in ORDER] + [other_core()])

    sends = []
    meta_recvs = []
    for route in range(2):
        here = coord(first_axis(route))
        for d in ORDER:
            copy = remote(
                meta_own,
                meta.at[route, here],
                meta_send.at[route, d],
                meta_recv.at[route, d],
                peer(first_axis(route), d),
            )
            copy.start()
            sends.append(copy)
            meta_recvs.append(copy)
        meta[route, pl.ds(here, 1)] = meta_own[...][None]

    sources = (tok_ref, cot_ref)

    def block(which, route, position, columns):
        rows = pl.ds(pl.multiple_of(position * TOK, TOK), TOK)
        return gathered.at[which, route, rows, columns]

    def gather_start(which):
        copies = [{}, {}]
        for d in (1, 3):
            for route in range(2):
                here = coord(first_axis(route))
                copy = remote(
                    sources[which].at[:, pl.ds(route * HALF, HALF)],
                    block(which, route, here, pl.ds(0, HALF)),
                    gat_send.at[which, route, d],
                    gat_recv.at[which, route, d],
                    peer(first_axis(route), d),
                )
                copy.start()
                sends.append(copy)
                copies[route][d] = copy
        for route in range(2):
            here = coord(first_axis(route))
            gathered[which, route, pl.ds(pl.multiple_of(here * TOK, TOK), TOK), :] = sources[
                which
            ][:, route * HALF : (route + 1) * HALF]
        return copies

    def gather_pass(which, copies):
        passed = []
        for d in (1, 3):
            for route in range(2):
                copies[route][d].wait_recv()
                axis = first_axis(route)
                behind = lax.rem(coord(axis) + 4 - d, 4)
                columns = pl.ds((d // 2) * (HALF // 2), HALF // 2)
                copy = remote(
                    block(which, route, behind, columns),
                    block(which, route, behind, columns),
                    gat_send.at[which, route, d - 1],
                    gat_recv.at[which, route, d - 1],
                    peer(axis, d),
                )
                copy.start()
                sends.append(copy)
                passed.append(copy)
        return passed

    tok_copies = gather_start(0)
    cot_copies = gather_start(1)
    for copy in meta_recvs:
        copy.wait_recv()
    for route in range(2):
        rank_out[route] = jnp.concatenate([meta[route, s][:, :TOK] for s in range(4)], axis=1)
        share_out[route] = jnp.concatenate([meta[route, s][:, TOK:] for s in range(4)], axis=1)

    buffers = (xbuf, g_hbm)

    def select(which, route, d):
        position = lax.rem(coord(second_axis(route)) + d, 4)
        expert = expert_at(route, position)
        rank_row = pick_row(rank_out[route], expert)
        share_row = pick_row(share_out[route], expert)
        here = coord(second_axis(route))
        target = buffers[which]
        total = jnp.zeros((16, CHUNK), F32)
        for c in range(4):
            hit = slot_rows(rank_row, c) == iota((4 * MAIN + 16, 4 * TOK), 0)
            choose = jnp.where(hit, 1.0, 0.0).astype(BF16)
            rows = jnp.dot(
                choose,
                gathered[which, route, :, c * CHUNK : (c + 1) * CHUNK],
                preferred_element_type=F32,
            )
            if which == 1:
                rows = rows * jnp.sum(jnp.where(hit, share_row, 0.0), axis=1, keepdims=True)
            main = rows[: 4 * MAIN].astype(BF16)
            total += rows[4 * MAIN :]
            if which == 1 and not d:
                own[route, :, c * CHUNK : (c + 1) * CHUNK] = main
            elif d:
                staged[which, route, d - 1, :, c * CHUNK : (c + 1) * CHUNK] = main
            else:
                columns = slice(route * HALF + c * CHUNK, route * HALF + (c + 1) * CHUNK)
                if route == 0:
                    target[pl.ds(pl.multiple_of(here * 128, 128), 128), columns] = main
                else:
                    for s in range(4):
                        first = pl.multiple_of((s * 4 + here) * MAIN, MAIN)
                        target[pl.ds(first, MAIN), columns] = main[s * MAIN : (s + 1) * MAIN]
        mine = pl.ds(pl.multiple_of(here * 16, 16), 16)
        if not d:
            over[which, route, mine, :] = total.astype(BF16)
            return []
        staged_over[which, route, d - 1] = total.astype(BF16)
        device = peer(second_axis(route), d)
        columns = pl.ds(route * HALF, HALF)
        copies = []
        if route == 0:
            copies.append(
                remote(
                    staged.at[which, route, d - 1],
                    target.at[pl.ds(pl.multiple_of(here * 128, 128), 128), columns],
                    main_send.at[which, route, d, 0],
                    main_recv.at[which, route, d, 0],
                    device,
                )
            )
        else:
            for s in range(4):
                first = pl.multiple_of((s * 4 + here) * MAIN, MAIN)
                copies.append(
                    remote(
                        staged.at[which, route, d - 1, pl.ds(s * MAIN, MAIN), :],
                        target.at[pl.ds(first, MAIN), columns],
                        main_send.at[which, route, d, s],
                        main_recv.at[which, route, d, s],
                        device,
                    )
                )
        copies.append(
            remote(
                staged_over.at[which, route, d - 1],
                over.at[which, route, mine, :],
                over_send.at[which, route, d],
                over_recv.at[which, route, d],
                device,
            )
        )
        for copy in copies:
            copy.start()
        sends.extend(copies)
        return copies

    def second_hop(which, passed):
        arrivals = []
        for copy in passed:
            copy.wait_recv()
        for d in ORDER:
            for route in range(2):
                arrivals.extend(select(which, route, d))
        return arrivals

    def finish(which, arrivals):
        for copy in arrivals:
            copy.wait_recv()
        for route in range(2):
            slot, chunk = overflow_target(route, (16, 64), 1)
            for c in range(4):
                spread = jnp.where((slot == iota((16, 64), 0)) & (chunk == c), 1.0, 0.0)
                first = route * HALF + c * CHUNK
                tail = jnp.dot(
                    spread.astype(BF16), over[which, route], preferred_element_type=F32
                ).astype(BF16)
                if which == 0:
                    xbuf[16 * MAIN : ROWS, first : first + CHUNK] = tail
                else:
                    own_over[:, first : first + CHUNK] = tail

    tok_passed = gather_pass(0, tok_copies)
    cot_passed = gather_pass(1, cot_copies)
    x_arrivals = second_hop(0, tok_passed)
    g_arrivals = second_hop(1, cot_passed)
    for which in range(2):
        for route in range(2):
            select(which, route, 0)
    load_gu.wait()
    load_d.wait()

    core = lax.rem(lax.axis_index("dp"), 2)
    stores = []
    shared = []

    def store(src, dst):
        copy = pltpu.make_async_copy(src, dst, local_sem.at[2 + len(stores)])
        copy.start()
        stores.append(copy)

    def share(src, dst):
        slot = len(shared)
        copy = remote(src, dst, core_send.at[slot], core_recv.at[slot], other_core())
        copy.start()
        shared.append(copy)

    for route in range(2):
        here = coord(second_axis(route))
        columns = pl.ds(route * HALF, HALF)
        if route == 0:
            first = pl.multiple_of(here * 128, 128)
            store(own.at[route], g_hbm.at[pl.ds(first, 128), columns])
        else:
            for s in range(4):
                first = pl.multiple_of((s * 4 + here) * MAIN, MAIN)
                store(
                    own.at[route, pl.ds(s * MAIN, MAIN), :],
                    g_hbm.at[pl.ds(first, MAIN), columns],
                )

    mine, theirs = pl.ds(0, ROWS), pl.ds(ROWS, ROWS)

    def split(src, dst):
        for block in range(4):
            there = pl.ds(block * 512, 512)
            keep = pl.ds(pl.multiple_of((2 * block + core) * 512, 512), 512)
            give = pl.ds(pl.multiple_of((2 * block + 1 - core) * 512, 512), 512)
            share(src.at[:, give], dst.at[theirs, there])
            store(src.at[:, keep], dst.at[mine, there])

    finish(0, x_arrivals)
    split(xbuf, x_hbm)

    @pl.loop(0, 3)
    def _(n):
        u_cols = pl.ds(pl.multiple_of(n * 256, 256), 256)
        v_cols = pl.ds(pl.multiple_of(HID + n * 256, 256), 256)
        u = jnp.dot(xbuf[...], wgu[:, u_cols], preferred_element_type=F32)
        pre[:, u_cols] = u
        v = jnp.dot(xbuf[...], wgu[:, v_cols], preferred_element_type=F32)
        pre[:, v_cols] = v
        hid[:, u_cols] = (pre[:, u_cols] * jax.nn.sigmoid(pre[:, u_cols]) * v).astype(BF16)

    share(hid, h_hbm.at[theirs])
    store(pre, pre_hbm)
    store(hid, h_hbm.at[mine])

    @pl.loop(0, WIDTH // 256)
    def _(n):
        cols = pl.ds(pl.multiple_of(n * 256, 256), 256)
        obuf[:, cols] = jnp.dot(hid[...], wd[:, cols], preferred_element_type=F32).astype(BF16)

    store(obuf, out_hbm)
    finish(1, g_arrivals)
    store(own_over, g_hbm.at[pl.ds(16 * MAIN, 16), :])
    for copy in stores + shared:
        copy.wait()
    for copy in sends:
        copy.wait_send()


def return_kernel(
    out_hbm,
    wgu_hbm,
    x_hbm,
    g_hbm,
    h_hbm,
    pre_hbm,
    wd_hbm,
    rank_ref,
    share_ref,
    layer_out,
    token_grad,
    grad_out,
    grad_in,
    xb,
    gb,
    gall,
    hb,
    pre,
    wd,
    pgb,
    wgu,
    sum_in,
    sum_out,
    near_in,
    near_out,
    far_in,
    far_out,
    tail,
    compact,
    rows,
    rows_over,
    partial,
    final,
    local_sem,
    wgu_sem,
    main_send,
    main_recv,
    over_send,
    over_recv,
    part_send,
    part_recv,
    dp_send,
    dp_recv,
    core_send,
    core_recv,
):
    z, x = place()
    y = lax.axis_index("dp") // 2
    core = lax.rem(lax.axis_index("dp"), 2)
    sig = gall
    inputs = (out_hbm, sig)
    mine, theirs = pl.ds(0, ROWS), pl.ds(ROWS, ROWS)
    fetch = {}

    def load(name, src, dst):
        copy = pltpu.make_async_copy(src, dst, local_sem.at[18 + len(fetch)])
        copy.start()
        fetch[name] = copy

    def columns_of(ahead, of_core):
        first = (2 * lax.rem(y + ahead, 4) + of_core) * 512
        return pl.ds(pl.multiple_of(first, 512), 512)

    def place_of(ahead):
        return pl.ds(pl.multiple_of(lax.rem(y + ahead, 4) * 512, 512), 512)

    load("h", h_hbm, hb)
    for ahead in (2, 1, 3, 0):
        load(ahead, g_hbm.at[:, columns_of(ahead, core)], gb.at[mine, place_of(ahead)])
    load_tail = pltpu.make_async_copy(
        out_hbm.at[pl.ds(16 * MAIN, 16), :], tail, local_sem.at[0]
    )
    load_tail.start()

    def wgu_tile(n):
        rows = pl.ds(pl.multiple_of(n * 256, 256), 256)
        slot = lax.rem(n, 2)
        return pltpu.make_async_copy(wgu_hbm.at[0, rows, :], wgu.at[slot], wgu_sem.at[slot])

    wgu_tile(0).start()
    enter(
        [peer(axis, d) for axis in ("z", "x") for d in ORDER]
        + [along_y(d) for d in (1, 3)]
        + [other_core()]
    )
    sends = []
    swaps = {}
    for ahead in (2, 1, 3, 0):
        swaps[ahead] = remote(
            g_hbm.at[:, columns_of(ahead, 1 - core)],
            gb.at[theirs, place_of(ahead)],
            core_send.at[ahead],
            core_recv.at[ahead],
            other_core(),
        )
        swaps[ahead].start()

    def pieces(which, route, position, slot):
        columns = pl.ds(route * HALF, HALF)
        if route == 0:
            first = pl.multiple_of(position * 128, 128)
            return [
                (inputs[which].at[pl.ds(first, 128), columns], rows.at[which, route, slot])
            ]
        found = []
        for s in range(4):
            first = pl.multiple_of((s * 4 + position) * MAIN, MAIN)
            found.append(
                (
                    inputs[which].at[pl.ds(first, MAIN), columns],
                    rows.at[which, route, slot, pl.ds(s * MAIN, MAIN), :],
                )
            )
        return found

    def first_hop(which):
        arrivals = [[], []]
        for d in ORDER:
            for route in range(2):
                here = coord(second_axis(route))
                there = lax.rem(here + d, 4)
                for s, (src, dst) in enumerate(pieces(which, route, there, here)):
                    copy = remote(
                        src,
                        dst,
                        main_send.at[which, route, d, s],
                        main_recv.at[which, route, d, s],
                        peer(second_axis(route), d),
                    )
                    copy.start()
                    sends.append(copy)
                    arrivals[route].append(copy)
        owns = [[], []]
        for route in range(2):
            here = coord(second_axis(route))
            for s, (src, dst) in enumerate(pieces(which, route, here, here)):
                copy = pltpu.make_async_copy(src, dst, local_sem.at[2 + which * 8 + route * 4 + s])
                copy.start()
                owns[route].append(copy)
        if which == 0:
            load_tail.wait()
        last = tail if which == 0 else sig.at[pl.ds(16 * MAIN, 16), :]
        for route in range(2):
            here = coord(second_axis(route))
            slot, chunk = overflow_target(route, (64, 16), 0)
            total = jnp.zeros((64, CHUNK), F32)
            for c in range(4):
                take = jnp.where((slot == iota((64, 16), 1)) & (chunk == c), 1.0, 0.0)
                first = route * HALF + c * CHUNK
                total += jnp.dot(
                    take.astype(BF16),
                    last[:, first : first + CHUNK],
                    preferred_element_type=F32,
                )
            compact[which, route] = total.astype(BF16)
            mine = pl.ds(pl.multiple_of(here * 16, 16), 16)
            rows_over[which, route, mine, :] = compact[which, route, mine, :]
            for d in ORDER:
                there = lax.rem(here + d, 4)
                copy = remote(
                    compact.at[which, route, pl.ds(pl.multiple_of(there * 16, 16), 16), :],
                    rows_over.at[which, route, mine, :],
                    over_send.at[which, route, d],
                    over_recv.at[which, route, d],
                    peer(second_axis(route), d),
                )
                copy.start()
                sends.append(copy)
                arrivals[route].append(copy)
        return arrivals, owns

    def combine(which, arrivals, owns):
        for route in range(2):
            for copy in arrivals[route]:
                copy.wait_recv()
            for copy in owns[route]:
                copy.wait()
            ranks = [pick_row(rank_ref[route], expert_at(route, p)) for p in range(4)]
            shares = [pick_row(share_ref[route], expert_at(route, p)) for p in range(4)]
            for c in range(4):
                main, rest = [], []
                for p in range(4):
                    hit = slot_rows(ranks[p], c) == iota((4 * MAIN + 16, 4 * TOK), 0)
                    value = shares[p] if which == 0 else 1.0
                    spread = jnp.where(hit, value, 0.0)
                    main.append(spread[: 4 * MAIN])
                    rest.append(spread[4 * MAIN :])
                main = jnp.concatenate(main, axis=0).astype(BF16)
                rest = jnp.concatenate(rest, axis=0).astype(BF16)
                columns = slice(c * CHUNK, (c + 1) * CHUNK)
                along = (((0,), (0,)), ((), ()))
                total = lax.dot_general(
                    main,
                    rows[which, route, :, :, columns].reshape(16 * MAIN, CHUNK),
                    along,
                    preferred_element_type=F32,
                ) + lax.dot_general(
                    rest, rows_over[which, route], along, preferred_element_type=F32
                )
                partial[which, route, :, columns] = total.astype(BF16)

    def pass_partial(which):
        finals = []
        for d in ORDER:
            for route in range(2):
                here = coord(first_axis(route))
                there = lax.rem(here + d, 4)
                copy = remote(
                    partial.at[which, route, pl.ds(pl.multiple_of(there * TOK, TOK), TOK), :],
                    final.at[which, route, d - 1],
                    part_send.at[which, route, d],
                    part_recv.at[which, route, d],
                    peer(first_axis(route), d),
                )
                copy.start()
                sends.append(copy)
                finals.append(copy)
        return finals

    def finish(which, finals, result):
        for copy in finals:
            copy.wait_recv()
        for route in range(2):
            here = coord(first_axis(route))
            own = partial[which, route, pl.ds(pl.multiple_of(here * TOK, TOK), TOK), :]
            total = own.astype(F32)
            for d in range(3):
                total += final[which, route, d].astype(F32)
            result[:, route * HALF : (route + 1) * HALF] = total.astype(BF16)

    along = (((0,), (0,)), ((), ()))

    def weight_out(ahead):
        cols = place_of(ahead)

        @pl.loop(0, 3)
        def _(n):
            piece = pl.ds(pl.multiple_of(n * 256, 256), 256)
            sum_out[ahead, piece, :] = lax.dot_general(
                hb[:, piece], gb[:, cols], along, preferred_element_type=F32
            ).astype(BF16)

    def weight_in(ahead):
        first = lax.rem(y + ahead, 4) * 512

        @pl.loop(0, 2)
        def _(n):
            piece = pl.ds(pl.multiple_of(n * 256, 256), 256)
            part = pl.ds(pl.multiple_of(first + n * 256, 256), 256)
            sum_in[ahead, piece, :] = lax.dot_general(
                xb[:, part], pgb[...], along, preferred_element_type=F32
            ).astype(BF16)

    half_in = (pl.ds(0, 256), pl.ds(256, 256))
    half_out = (pl.ds(0, HID // 2), pl.ds(HID // 2, HID // 2))

    sums = (sum_out, sum_in)
    nears = (near_out, near_in)
    fars = (far_out, far_in)
    halves = (half_out, half_in)

    def pass_half(kind, ahead, half, side, dst, slot):
        copy = remote(
            sums[kind].at[ahead, halves[kind][half], :],
            dst,
            dp_send.at[slot, side, kind],
            dp_recv.at[slot, side, kind],
            along_y((1, 3)[side]),
        )
        copy.start()
        sends.append(copy)
        return copy

    def pass_near(kind):
        return [pass_half(kind, 2, side, side, nears[kind].at[side], 0) for side in range(2)]

    def pass_far(kind, side):
        ahead, half = (1, 3)[side], 1 - side
        return pass_half(kind, ahead, half, side, fars[kind].at[side, halves[kind][half], :], 1)

    def pass_sum(kind, near):
        found = []
        for side, ahead in ((0, 1), (1, 3)):
            near[side].wait_recv()
            part = halves[kind][side]
            sums[kind][ahead, part, :] = (
                sums[kind][ahead, part, :].astype(F32) + nears[kind][side].astype(F32)
            ).astype(BF16)
            found.append(
                pass_half(kind, ahead, side, side, fars[kind].at[side, part, :], 2)
            )
        return found

    out_state = first_hop(0)
    ends = []
    fetch["h"].wait()
    for ahead in (2, 1, 3):
        fetch[ahead].wait()
        swaps[ahead].wait_recv()
        if ahead == 2:
            load("g", g_hbm, gall)
            load("d", wd_hbm.at[0], wd)
            load("pre", pre_hbm, pre)
            load("x", x_hbm, xb)
        weight_out(ahead)
        if ahead == 2:
            near_sent_out = pass_near(0)
        else:
            ends.append(pass_far(0, ahead // 2))
    fetch["g"].wait()
    fetch["d"].wait()
    fetch["pre"].wait()

    @pl.loop(0, 3)
    def _(n):
        u_cols = pl.ds(pl.multiple_of(n * 256, 256), 256)
        v_cols = pl.ds(pl.multiple_of(HID + n * 256, 256), 256)
        grad = lax.dot_general(
            gall[...], wd[u_cols, :], (((1,), (1,)), ((), ())), preferred_element_type=F32
        )
        u = pre[:, u_cols]
        logistic = jax.nn.sigmoid(u)
        pgb[:ROWS, v_cols] = (grad * u * logistic).astype(BF16)
        pgb[:ROWS, u_cols] = (
            grad * pre[:, v_cols] * logistic * (1.0 + u * (1.0 - logistic))
        ).astype(BF16)

    swap = remote(
        pgb.at[mine], pgb.at[theirs], core_send.at[4], core_recv.at[4], other_core()
    )
    swap.start()
    def token_side(first, end):
        @pl.loop(first, end)
        def _(n):
            @pl.when(n + 1 < WIDTH // 256)
            def _():
                wgu_tile(n + 1).start()

            wgu_tile(n).wait()
            cols = pl.ds(pl.multiple_of(n * 256, 256), 256)
            sig[:, cols] = lax.dot_general(
                pgb[:ROWS, :],
                wgu[lax.rem(n, 2)],
                (((1,), (1,)), ((), ())),
                preferred_element_type=F32,
            ).astype(BF16)

    token_side(0, 6)
    fetch["x"].wait()
    swap.wait_recv()
    weight_in(2)
    near_sent_in = pass_near(1)
    token_side(6, WIDTH // 256)
    sig_state = first_hop(1)
    ends += pass_sum(0, near_sent_out)
    fetch[0].wait()
    swaps[0].wait_recv()
    weight_out(0)
    weight_in(0)
    combine(0, *out_state)
    for ahead in (1, 3):
        weight_in(ahead)
        ends.append(pass_far(1, ahead // 2))
    ends += pass_sum(1, near_sent_in)
    for route in range(2):
        for copy in sig_state[0][route]:
            copy.wait_recv()
    out_finals = pass_partial(0)
    combine(1, [[], []], sig_state[1])
    sig_finals = pass_partial(1)
    for copy in ends[:4]:
        copy.wait_recv()

    @pl.loop(0, 4)
    def _(n):
        part = pl.ds(pl.multiple_of(n * 192, 192), 192)
        total = sum_out[0, part, :].astype(F32)
        total += far_out[0, part, :].astype(F32) + far_out[1, part, :].astype(F32)
        grad_out[part, :] = total.astype(BF16)

    finish(0, out_finals, layer_out)
    finish(1, sig_finals, token_grad)
    for copy in ends[4:]:
        copy.wait_recv()

    @pl.loop(0, 4)
    def _(n):
        part = pl.ds(pl.multiple_of(n * 128, 128), 128)
        total = sum_in[0, part, :].astype(F32)
        total += far_in[0, part, :].astype(F32) + far_in[1, part, :].astype(F32)
        sum_in[0, part, :] = total.astype(BF16)

    store_in = pltpu.make_async_copy(sum_in.at[0], grad_in, local_sem.at[1])
    store_in.start()
    for copy in sends + [swaps[ahead] for ahead in range(4)] + [swap]:
        copy.wait_send()
    store_in.wait()


def last_kernel(*refs):
    count = len(refs) // 2
    for src, dst in zip(refs[:count], refs[count:]):
        dst[...] = src[...]


VMEM = pl.BlockSpec(memory_space=pltpu.VMEM)
ANY = pl.BlockSpec(memory_space=pl.ANY)
DMA = pltpu.SemaphoreType.DMA


def dispatch(ids, gates, tokens, cotangent, gate_up, down_weight):
    table = jax.ShapeDtypeStruct((2, 16, 4 * TOK), F32)
    return pl.pallas_call(
        dispatch_kernel,
        out_shape=(
            jax.ShapeDtypeStruct((ROWS, WIDTH), BF16),
            jax.ShapeDtypeStruct((2 * ROWS, HALF), BF16),
            jax.ShapeDtypeStruct((ROWS, WIDTH), BF16),
            jax.ShapeDtypeStruct((2 * ROWS, HID), BF16),
            jax.ShapeDtypeStruct((ROWS, 2 * HID), F32),
            table,
            table,
        ),
        in_specs=[VMEM] * 4 + [ANY] * 2,
        out_specs=(ANY,) * 5 + (VMEM,) * 2,
        scratch_shapes=[
            pltpu.VMEM((WIDTH, 2 * HID), BF16),
            pltpu.VMEM((HID, WIDTH), BF16),
            pltpu.VMEM((16, 2 * TOK), F32),
            pltpu.VMEM((2, 4, 16, 2 * TOK), F32),
            pltpu.VMEM((2, 2, 4 * TOK, HALF), BF16),
            pltpu.VMEM((2, 2, 3, 4 * MAIN, HALF), BF16),
            pltpu.VMEM((2, 2, 3, 16, CHUNK), BF16),
            pltpu.VMEM((2, 2, 64, CHUNK), BF16),
            pltpu.VMEM((ROWS, WIDTH), BF16),
            pltpu.VMEM((2, 4 * MAIN, HALF), BF16),
            pltpu.VMEM((16, WIDTH), BF16),
            pltpu.VMEM((ROWS, 2 * HID), F32),
            pltpu.VMEM((ROWS, HID), BF16),
            pltpu.VMEM((ROWS, WIDTH), BF16),
            DMA((16,)),
            DMA((2, 4)),
            DMA((2, 4)),
            DMA((2, 2, 4)),
            DMA((2, 2, 4)),
            DMA((2, 2, 4, 4)),
            DMA((2, 2, 4, 4)),
            DMA((2, 2, 4)),
            DMA((2, 2, 4)),
            DMA((5,)),
            DMA((5,)),
        ],
        compiler_params=pltpu.CompilerParams(
            collective_id=0, has_side_effects=True, vmem_limit_bytes=60 << 20
        ),
        cost_estimate=pl.CostEstimate(
            flops=20 * 10**9, bytes_accessed=40 * 10**6, transcendentals=10**6
        ),
    )(ids, gates, tokens, cotangent, gate_up, down_weight)


def give_back(out_rows, gate_up, x_rows, g_rows, hidden, pre_act, down_weight, rank, share):
    result = jax.ShapeDtypeStruct((TOK, WIDTH), BF16)
    return pl.pallas_call(
        return_kernel,
        out_shape=(
            result,
            result,
            jax.ShapeDtypeStruct((HID, 512), BF16),
            jax.ShapeDtypeStruct((512, 2 * HID), BF16),
        ),
        in_specs=[ANY] * 7 + [VMEM] * 2,
        out_specs=(VMEM,) * 3 + (ANY,),
        scratch_shapes=[
            pltpu.VMEM((2 * ROWS, HALF), BF16),
            pltpu.VMEM((2 * ROWS, HALF), BF16),
            pltpu.VMEM((ROWS, WIDTH), BF16),
            pltpu.VMEM((2 * ROWS, HID), BF16),
            pltpu.VMEM((ROWS, 2 * HID), F32),
            pltpu.VMEM((HID, WIDTH), BF16),
            pltpu.VMEM((2 * ROWS, 2 * HID), BF16),
            pltpu.VMEM((2, 256, 2 * HID), BF16),
            pltpu.VMEM((4, 512, 2 * HID), BF16),
            pltpu.VMEM((4, HID, 512), BF16),
            pltpu.VMEM((2, 256, 2 * HID), BF16),
            pltpu.VMEM((2, HID // 2, 512), BF16),
            pltpu.VMEM((2, 512, 2 * HID), BF16),
            pltpu.VMEM((2, HID, 512), BF16),
            pltpu.VMEM((16, WIDTH), BF16),
            pltpu.VMEM((2, 2, 64, CHUNK), BF16),
            pltpu.VMEM((2, 2, 4, 4 * MAIN, HALF), BF16),
            pltpu.VMEM((2, 2, 64, CHUNK), BF16),
            pltpu.VMEM((2, 2, 4 * TOK, HALF), BF16),
            pltpu.VMEM((2, 2, 3, TOK, HALF), BF16),
            DMA((27,)),
            DMA((2,)),
            DMA((2, 2, 4, 4)),
            DMA((2, 2, 4, 4)),
            DMA((2, 2, 4)),
            DMA((2, 2, 4)),
            DMA((2, 2, 4)),
            DMA((2, 2, 4)),
            DMA((3, 2, 2)),
            DMA((3, 2, 2)),
            DMA((5,)),
            DMA((5,)),
        ],
        compiler_params=pltpu.CompilerParams(
            collective_id=1, has_side_effects=True, vmem_limit_bytes=62 << 20
        ),
        cost_estimate=pl.CostEstimate(
            flops=26 * 10**9, bytes_accessed=100 * 10**6, transcendentals=0
        ),
    )(out_rows, gate_up, x_rows, g_rows, hidden, pre_act, down_weight, rank, share)


def last(*results):
    steps = 4
    specs = [
        pl.BlockSpec((a.shape[0] // steps, a.shape[1]), lambda n: (n, 0)) for a in results
    ]
    return pl.pallas_call(
        last_kernel,
        grid=(steps,),
        out_shape=tuple(jax.ShapeDtypeStruct(a.shape, a.dtype) for a in results),
        in_specs=specs,
        out_specs=tuple(specs),
        cost_estimate=pl.CostEstimate(
            flops=0, bytes_accessed=7 * 10**6, transcendentals=0
        ),
    )(*results)


def per_device(tokens, cotangent, expert_ids, gate_fixed, gate_up, down_weight):
    out_rows, x_rows, g_rows, hidden, pre_act, rank, share = dispatch(
        expert_ids.T, gate_fixed.T, tokens, cotangent, gate_up, down_weight
    )
    layer_out, token_grad, grad_out, grad_in = last(
        *give_back(
            out_rows, gate_up, x_rows, g_rows, hidden, pre_act, down_weight, rank, share
        )
    )
    return layer_out, token_grad, grad_in[None], grad_out[None]


def solution(mesh):
    rows = P(("ep", "dp"), None)
    return jax.shard_map(
        per_device,
        mesh=mesh,
        in_specs=(rows, rows, rows, rows, P("ep", None, None), P("ep", None, None)),
        out_specs=(rows, rows, P("ep", "dp", None), P("ep", None, "dp")),
        check_vma=False,
    )
```

```python
import functools

import jax
import jax.numpy as jnp
from jax import lax
from jax.experimental import pallas as pl
from jax.experimental.pallas import tpu as pltpu
from jax.sharding import PartitionSpec as P

BF16 = jnp.bfloat16
F32 = jnp.float32
MESH = pl.DeviceIdType.MESH
TOK = 64
WIDTH = 4096
HALF = WIDTH // 2
CHUNK = HALF // 4
HID = 768
MAIN = 32
ROWS = 16 * MAIN + 16
ORDER = (2, 1, 3)


def place():
    ep = lax.axis_index("ep")
    return ep // 4, ep % 4


def peer(axis, distance):
    z, x = place()
    if axis == "z":
        z = lax.rem(z + distance, 4)
    else:
        x = lax.rem(x + distance, 4)
    return {"ep": z * 4 + x, "dp": lax.axis_index("dp")}


def along_y(distance):
    dp = lax.axis_index("dp")
    return {"ep": lax.axis_index("ep"), "dp": lax.rem(dp + 2 * distance, 8)}


def other_core():
    dp = lax.axis_index("dp")
    return {"ep": lax.axis_index("ep"), "dp": dp + 1 - 2 * lax.rem(dp, 2)}


def first_axis(route):
    return ("z", "x")[route]


def second_axis(route):
    return ("x", "z")[route]


def coord(axis):
    z, x = place()
    return z if axis == "z" else x


def expert_at(route, position):
    z, x = place()
    return z * 4 + position if route == 0 else position * 4 + x


def iota(shape, dim):
    return lax.broadcasted_iota(jnp.int32, shape, dim)


def enter(peers):
    barrier = pltpu.get_barrier_semaphore()
    for device in peers:
        pl.semaphore_signal(barrier, 1, device_id=device, device_id_type=MESH)
    pl.semaphore_wait(barrier, len(peers))


def remote(src, dst, send_sem, recv_sem, device):
    return pltpu.make_async_remote_copy(
        src_ref=src,
        dst_ref=dst,
        send_sem=send_sem,
        recv_sem=recv_sem,
        device_id=device,
        device_id_type=MESH,
    )


def pick_row(table, index):
    rows = iota(table.shape, 0)
    return jnp.sum(jnp.where(rows == index, table, 0.0), axis=0, keepdims=True)


def slot_rows(rank, chunk):
    source = iota((1, 4 * TOK), 1) // TOK
    rank = rank.astype(jnp.int32)
    main = jnp.where(rank >= 0, rank + MAIN * source, -1)
    return jnp.where(rank == MAIN, 4 * MAIN + 4 * chunk + source, main)


def overflow_target(route, shape, dim):
    row = iota(shape, dim)
    sender, chunk, source = row // 16, lax.rem(row, 16) // 4, lax.rem(row, 4)
    slot = sender * 4 + source if route == 0 else source * 4 + sender
    return slot, chunk


def dispatch_kernel(
    ids_ref,
    gate_ref,
    tok_ref,
    cot_ref,
    wgu_hbm,
    wd_hbm,
    out_hbm,
    x_hbm,
    g_hbm,
    h_hbm,
    pre_hbm,
    rank_out,
    share_out,
    wgu,
    wd,
    meta_own,
    meta,
    gathered,
    staged,
    staged_over,
    over,
    xbuf,
    own,
    own_over,
    pre,
    hid,
    obuf,
    local_sem,
    meta_send,
    meta_recv,
    gat_send,
    gat_recv,
    main_send,
    main_recv,
    over_send,
    over_recv,
    core_send,
    core_recv,
):
    z, x = place()
    load_gu = pltpu.make_async_copy(wgu_hbm.at[0], wgu, local_sem.at[0])
    load_d = pltpu.make_async_copy(wd_hbm.at[0], wd, local_sem.at[1])
    load_gu.start()
    load_d.start()

    enter([peer(axis, d) for axis in ("z", "x") for d in ORDER] + [other_core()])

    sends = []
    sources = (tok_ref, cot_ref)

    def block(which, route, position, columns):
        rows = pl.ds(pl.multiple_of(position * TOK, TOK), TOK)
        return gathered.at[which, route, rows, columns]

    def gather_start(which):
        copies = [{}, {}]
        for d in (1, 3):
            for route in range(2):
                here = coord(first_axis(route))
                copy = remote(
                    sources[which].at[:, pl.ds(route * HALF, HALF)],
                    block(which, route, here, pl.ds(0, HALF)),
                    gat_send.at[which, route, d],
                    gat_recv.at[which, route, d],
                    peer(first_axis(route), d),
                )
                copy.start()
                sends.append(copy)
                copies[route][d] = copy
        for route in range(2):
            here = coord(first_axis(route))
            gathered[which, route, pl.ds(pl.multiple_of(here * TOK, TOK), TOK), :] = sources[
                which
            ][:, route * HALF : (route + 1) * HALF]
        return copies

    def gather_pass(which, copies):
        passed = []
        for d in (1, 3):
            for route in range(2):
                copies[route][d].wait_recv()
                axis = first_axis(route)
                behind = lax.rem(coord(axis) + 4 - d, 4)
                columns = pl.ds((d // 2) * (HALF // 2), HALF // 2)
                copy = remote(
                    block(which, route, behind, columns),
                    block(which, route, behind, columns),
                    gat_send.at[which, route, d - 1],
                    gat_recv.at[which, route, d - 1],
                    peer(axis, d),
                )
                copy.start()
                sends.append(copy)
                passed.append(copy)
        return passed

    tok_copies = gather_start(0)

    gates = gate_ref[...].astype(F32)
    share = gates / jnp.sum(gates, axis=0, keepdims=True)
    ids = ids_ref[...]
    expert = iota((16, TOK), 0)
    named = jnp.zeros((16, TOK), F32)
    weight = jnp.zeros((16, TOK), F32)
    for k in range(8):
        hit = ids[k : k + 1, :] == expert
        named += jnp.where(hit, 1.0, 0.0)
        weight += jnp.where(hit, share[k : k + 1, :], 0.0)
    before = jnp.where(iota((TOK, TOK), 0) < iota((TOK, TOK), 1), 1.0, 0.0)
    rank = jnp.dot(named.astype(BF16), before.astype(BF16), preferred_element_type=F32)
    rank = jnp.where(named > 0.0, rank, -1.0)
    meta_own[...] = jnp.concatenate([rank, weight], axis=1)

    meta_recvs = []
    for route in range(2):
        here = coord(first_axis(route))
        for d in ORDER:
            copy = remote(
                meta_own,
                meta.at[route, here],
                meta_send.at[route, d],
                meta_recv.at[route, d],
                peer(first_axis(route), d),
            )
            copy.start()
            sends.append(copy)
            meta_recvs.append(copy)
        meta[route, pl.ds(here, 1)] = meta_own[...][None]

    cot_copies = gather_start(1)
    for copy in meta_recvs:
        copy.wait_recv()
    for route in range(2):
        rank_out[route] = jnp.concatenate([meta[route, s][:, :TOK] for s in range(4)], axis=1)
        share_out[route] = jnp.concatenate([meta[route, s][:, TOK:] for s in range(4)], axis=1)

    buffers = (xbuf, g_hbm)

    def select(which, route, d):
        position = lax.rem(coord(second_axis(route)) + d, 4)
        expert = expert_at(route, position)
        rank_row = pick_row(rank_out[route], expert)
        share_row = pick_row(share_out[route], expert)
        here = coord(second_axis(route))
        target = buffers[which]
        total = jnp.zeros((16, CHUNK), F32)
        for c in range(4):
            hit = slot_rows(rank_row, c) == iota((4 * MAIN + 16, 4 * TOK), 0)
            choose = jnp.where(hit, 1.0, 0.0).astype(BF16)
            rows = jnp.dot(
                choose,
                gathered[which, route, :, c * CHUNK : (c + 1) * CHUNK],
                preferred_element_type=F32,
            )
            if which == 1:
                rows = rows * jnp.sum(jnp.where(hit, share_row, 0.0), axis=1, keepdims=True)
            main = rows[: 4 * MAIN].astype(BF16)
            total += rows[4 * MAIN :]
            if which == 1 and not d:
                own[route, :, c * CHUNK : (c + 1) * CHUNK] = main
            elif d:
                staged[which, route, d - 1, :, c * CHUNK : (c + 1) * CHUNK] = main
            else:
                columns = slice(route * HALF + c * CHUNK, route * HALF + (c + 1) * CHUNK)
                if route == 0:
                    target[pl.ds(pl.multiple_of(here * 128, 128), 128), columns] = main
                else:
                    for s in range(4):
                        first = pl.multiple_of((s * 4 + here) * MAIN, MAIN)
                        target[pl.ds(first, MAIN), columns] = main[s * MAIN : (s + 1) * MAIN]
        mine = pl.ds(pl.multiple_of(here * 16, 16), 16)
        if not d:
            over[which, route, mine, :] = total.astype(BF16)
            return []
        staged_over[which, route, d - 1] = total.astype(BF16)
        device = peer(second_axis(route), d)
        columns = pl.ds(route * HALF, HALF)
        copies = []
        if route == 0:
            copies.append(
                remote(
                    staged.at[which, route, d - 1],
                    target.at[pl.ds(pl.multiple_of(here * 128, 128), 128), columns],
                    main_send.at[which, route, d, 0],
                    main_recv.at[which, route, d, 0],
                    device,
                )
            )
        else:
            for s in range(4):
                first = pl.multiple_of((s * 4 + here) * MAIN, MAIN)
                copies.append(
                    remote(
                        staged.at[which, route, d - 1, pl.ds(s * MAIN, MAIN), :],
                        target.at[pl.ds(first, MAIN), columns],
                        main_send.at[which, route, d, s],
                        main_recv.at[which, route, d, s],
                        device,
                    )
                )
        copies.append(
            remote(
                staged_over.at[which, route, d - 1],
                over.at[which, route, mine, :],
                over_send.at[which, route, d],
                over_recv.at[which, route, d],
                device,
            )
        )
        for copy in copies:
            copy.start()
        sends.extend(copies)
        return copies

    def second_hop(which, passed):
        arrivals = []
        for copy in passed:
            copy.wait_recv()
        for d in ORDER:
            for route in range(2):
                arrivals.extend(select(which, route, d))
        return arrivals

    def finish(which, arrivals):
        for copy in arrivals:
            copy.wait_recv()
        for route in range(2):
            slot, chunk = overflow_target(route, (16, 64), 1)
            for c in range(4):
                spread = jnp.where((slot == iota((16, 64), 0)) & (chunk == c), 1.0, 0.0)
                first = route * HALF + c * CHUNK
                tail = jnp.dot(
                    spread.astype(BF16), over[which, route], preferred_element_type=F32
                ).astype(BF16)
                if which == 0:
                    xbuf[16 * MAIN : ROWS, first : first + CHUNK] = tail
                else:
                    own_over[:, first : first + CHUNK] = tail

    tok_passed = gather_pass(0, tok_copies)
    cot_passed = gather_pass(1, cot_copies)
    x_arrivals = second_hop(0, tok_passed)
    g_arrivals = second_hop(1, cot_passed)
    for which in range(2):
        for route in range(2):
            select(which, route, 0)
    load_gu.wait()
    load_d.wait()

    core = lax.rem(lax.axis_index("dp"), 2)
    stores = []
    shared = []

    def store(src, dst):
        copy = pltpu.make_async_copy(src, dst, local_sem.at[2 + len(stores)])
        copy.start()
        stores.append(copy)

    def share(src, dst):
        slot = len(shared)
        copy = remote(src, dst, core_send.at[slot], core_recv.at[slot], other_core())
        copy.start()
        shared.append(copy)

    for route in range(2):
        here = coord(second_axis(route))
        columns = pl.ds(route * HALF, HALF)
        if route == 0:
            first = pl.multiple_of(here * 128, 128)
            store(own.at[route], g_hbm.at[pl.ds(first, 128), columns])
        else:
            for s in range(4):
                first = pl.multiple_of((s * 4 + here) * MAIN, MAIN)
                store(
                    own.at[route, pl.ds(s * MAIN, MAIN), :],
                    g_hbm.at[pl.ds(first, MAIN), columns],
                )

    mine, theirs = pl.ds(0, ROWS), pl.ds(ROWS, ROWS)

    def split(src, dst):
        for block in range(4):
            there = pl.ds(block * 512, 512)
            keep = pl.ds(pl.multiple_of((2 * block + core) * 512, 512), 512)
            give = pl.ds(pl.multiple_of((2 * block + 1 - core) * 512, 512), 512)
            share(src.at[:, give], dst.at[theirs, there])
            store(src.at[:, keep], dst.at[mine, there])

    finish(0, x_arrivals)
    split(xbuf, x_hbm)

    @pl.loop(0, 3)
    def _(n):
        u_cols = pl.ds(pl.multiple_of(n * 256, 256), 256)
        v_cols = pl.ds(pl.multiple_of(HID + n * 256, 256), 256)
        u = jnp.dot(xbuf[...], wgu[:, u_cols], preferred_element_type=F32)
        pre[:, u_cols] = u
        v = jnp.dot(xbuf[...], wgu[:, v_cols], preferred_element_type=F32)
        pre[:, v_cols] = v
        hid[:, u_cols] = (pre[:, u_cols] * jax.nn.sigmoid(pre[:, u_cols]) * v).astype(BF16)

    share(hid, h_hbm.at[theirs])
    store(pre, pre_hbm)
    store(hid, h_hbm.at[mine])

    @pl.loop(0, WIDTH // 256)
    def _(n):
        cols = pl.ds(pl.multiple_of(n * 256, 256), 256)
        obuf[:, cols] = jnp.dot(hid[...], wd[:, cols], preferred_element_type=F32).astype(BF16)

    store(obuf, out_hbm)
    finish(1, g_arrivals)
    store(own_over, g_hbm.at[pl.ds(16 * MAIN, 16), :])
    for copy in stores + shared:
        copy.wait()
    for copy in sends:
        copy.wait_send()


def return_kernel(
    out_hbm,
    wgu_hbm,
    x_hbm,
    g_hbm,
    h_hbm,
    pre_hbm,
    wd_hbm,
    rank_ref,
    share_ref,
    layer_hbm,
    token_hbm,
    down_hbm,
    grad_in,
    layer_out,
    token_grad,
    grad_out,
    xb,
    gb,
    gall,
    hb,
    pre,
    wd,
    pgb,
    wgu,
    sum_in,
    sum_out,
    near_in,
    near_out,
    far_in,
    far_out,
    tail,
    compact,
    rows,
    rows_over,
    partial,
    final,
    local_sem,
    wgu_sem,
    main_send,
    main_recv,
    over_send,
    over_recv,
    part_send,
    part_recv,
    dp_send,
    dp_recv,
    core_send,
    core_recv,
):
    z, x = place()
    y = lax.axis_index("dp") // 2
    core = lax.rem(lax.axis_index("dp"), 2)
    sig = gall
    inputs = (out_hbm, sig)
    mine, theirs = pl.ds(0, ROWS), pl.ds(ROWS, ROWS)
    fetch = {}

    def load(name, src, dst):
        copy = pltpu.make_async_copy(src, dst, local_sem.at[18 + len(fetch)])
        copy.start()
        fetch[name] = copy

    def columns_of(ahead, of_core):
        first = (2 * lax.rem(y + ahead, 4) + of_core) * 512
        return pl.ds(pl.multiple_of(first, 512), 512)

    def place_of(ahead):
        return pl.ds(pl.multiple_of(lax.rem(y + ahead, 4) * 512, 512), 512)

    load("h", h_hbm, hb)
    for ahead in (2, 1, 3, 0):
        load(ahead, g_hbm.at[:, columns_of(ahead, core)], gb.at[mine, place_of(ahead)])
    load_tail = pltpu.make_async_copy(
        out_hbm.at[pl.ds(16 * MAIN, 16), :], tail, local_sem.at[0]
    )
    load_tail.start()

    def wgu_tile(n):
        rows = pl.ds(pl.multiple_of(n * 256, 256), 256)
        slot = lax.rem(n, 2)
        return pltpu.make_async_copy(wgu_hbm.at[0, rows, :], wgu.at[slot], wgu_sem.at[slot])

    wgu_tile(0).start()
    enter(
        [peer(axis, d) for axis in ("z", "x") for d in ORDER]
        + [along_y(d) for d in (1, 3)]
        + [other_core()]
    )
    sends = []
    swaps = {}
    for ahead in (2, 1, 3, 0):
        swaps[ahead] = remote(
            g_hbm.at[:, columns_of(ahead, 1 - core)],
            gb.at[theirs, place_of(ahead)],
            core_send.at[ahead],
            core_recv.at[ahead],
            other_core(),
        )
        swaps[ahead].start()

    def pieces(which, route, position, slot):
        columns = pl.ds(route * HALF, HALF)
        if route == 0:
            first = pl.multiple_of(position * 128, 128)
            return [
                (inputs[which].at[pl.ds(first, 128), columns], rows.at[which, route, slot])
            ]
        found = []
        for s in range(4):
            first = pl.multiple_of((s * 4 + position) * MAIN, MAIN)
            found.append(
                (
                    inputs[which].at[pl.ds(first, MAIN), columns],
                    rows.at[which, route, slot, pl.ds(s * MAIN, MAIN), :],
                )
            )
        return found

    def first_hop(which):
        arrivals = [[], []]
        for d in ORDER:
            for route in range(2):
                here = coord(second_axis(route))
                there = lax.rem(here + d, 4)
                for s, (src, dst) in enumerate(pieces(which, route, there, here)):
                    copy = remote(
                        src,
                        dst,
                        main_send.at[which, route, d, s],
                        main_recv.at[which, route, d, s],
                        peer(second_axis(route), d),
                    )
                    copy.start()
                    sends.append(copy)
                    arrivals[route].append(copy)
        owns = [[], []]
        for route in range(2):
            here = coord(second_axis(route))
            for s, (src, dst) in enumerate(pieces(which, route, here, here)):
                copy = pltpu.make_async_copy(src, dst, local_sem.at[2 + which * 8 + route * 4 + s])
                copy.start()
                owns[route].append(copy)
        if which == 0:
            load_tail.wait()
        last = tail if which == 0 else sig.at[pl.ds(16 * MAIN, 16), :]
        for route in range(2):
            here = coord(second_axis(route))
            slot, chunk = overflow_target(route, (64, 16), 0)
            total = jnp.zeros((64, CHUNK), F32)
            for c in range(4):
                take = jnp.where((slot == iota((64, 16), 1)) & (chunk == c), 1.0, 0.0)
                first = route * HALF + c * CHUNK
                total += jnp.dot(
                    take.astype(BF16),
                    last[:, first : first + CHUNK],
                    preferred_element_type=F32,
                )
            compact[which, route] = total.astype(BF16)
            mine = pl.ds(pl.multiple_of(here * 16, 16), 16)
            rows_over[which, route, mine, :] = compact[which, route, mine, :]
            for d in ORDER:
                there = lax.rem(here + d, 4)
                copy = remote(
                    compact.at[which, route, pl.ds(pl.multiple_of(there * 16, 16), 16), :],
                    rows_over.at[which, route, mine, :],
                    over_send.at[which, route, d],
                    over_recv.at[which, route, d],
                    peer(second_axis(route), d),
                )
                copy.start()
                sends.append(copy)
                arrivals[route].append(copy)
        return arrivals, owns

    def combine(which, arrivals, owns):
        for route in range(2):
            for copy in arrivals[route]:
                copy.wait_recv()
            for copy in owns[route]:
                copy.wait()
            ranks = [pick_row(rank_ref[route], expert_at(route, p)) for p in range(4)]
            shares = [pick_row(share_ref[route], expert_at(route, p)) for p in range(4)]
            for c in range(4):
                main, rest = [], []
                for p in range(4):
                    hit = slot_rows(ranks[p], c) == iota((4 * MAIN + 16, 4 * TOK), 0)
                    value = shares[p] if which == 0 else 1.0
                    spread = jnp.where(hit, value, 0.0)
                    main.append(spread[: 4 * MAIN])
                    rest.append(spread[4 * MAIN :])
                main = jnp.concatenate(main, axis=0).astype(BF16)
                rest = jnp.concatenate(rest, axis=0).astype(BF16)
                columns = slice(c * CHUNK, (c + 1) * CHUNK)
                along = (((0,), (0,)), ((), ()))
                total = lax.dot_general(
                    main,
                    rows[which, route, :, :, columns].reshape(16 * MAIN, CHUNK),
                    along,
                    preferred_element_type=F32,
                ) + lax.dot_general(
                    rest, rows_over[which, route], along, preferred_element_type=F32
                )
                partial[which, route, :, columns] = total.astype(BF16)

    def pass_partial(which):
        finals = []
        for d in ORDER:
            for route in range(2):
                here = coord(first_axis(route))
                there = lax.rem(here + d, 4)
                copy = remote(
                    partial.at[which, route, pl.ds(pl.multiple_of(there * TOK, TOK), TOK), :],
                    final.at[which, route, d - 1],
                    part_send.at[which, route, d],
                    part_recv.at[which, route, d],
                    peer(first_axis(route), d),
                )
                copy.start()
                sends.append(copy)
                finals.append(copy)
        return finals

    def finish(which, finals, result):
        for copy in finals:
            copy.wait_recv()
        for route in range(2):
            here = coord(first_axis(route))
            own = partial[which, route, pl.ds(pl.multiple_of(here * TOK, TOK), TOK), :]
            total = own.astype(F32)
            for d in range(3):
                total += final[which, route, d].astype(F32)
            result[:, route * HALF : (route + 1) * HALF] = total.astype(BF16)

    along = (((0,), (0,)), ((), ()))

    def weight_out(ahead):
        cols = place_of(ahead)

        @pl.loop(0, 3)
        def _(n):
            piece = pl.ds(pl.multiple_of(n * 256, 256), 256)
            sum_out[ahead, piece, :] = lax.dot_general(
                hb[:, piece], gb[:, cols], along, preferred_element_type=F32
            ).astype(BF16)

    def weight_in(ahead):
        first = lax.rem(y + ahead, 4) * 512

        @pl.loop(0, 2)
        def _(n):
            piece = pl.ds(pl.multiple_of(n * 256, 256), 256)
            part = pl.ds(pl.multiple_of(first + n * 256, 256), 256)
            sum_in[ahead, piece, :] = lax.dot_general(
                xb[:, part], pgb[...], along, preferred_element_type=F32
            ).astype(BF16)

    half_in = (pl.ds(0, 256), pl.ds(256, 256))
    half_out = (pl.ds(0, HID // 2), pl.ds(HID // 2, HID // 2))

    sums = (sum_out, sum_in)
    nears = (near_out, near_in)
    fars = (far_out, far_in)
    halves = (half_out, half_in)

    def pass_half(kind, ahead, half, side, dst, slot):
        copy = remote(
            sums[kind].at[ahead, halves[kind][half], :],
            dst,
            dp_send.at[slot, side, kind],
            dp_recv.at[slot, side, kind],
            along_y((1, 3)[side]),
        )
        copy.start()
        sends.append(copy)
        return copy

    def pass_near(kind):
        return [pass_half(kind, 2, side, side, nears[kind].at[side], 0) for side in range(2)]

    def pass_far(kind, side):
        ahead, half = (1, 3)[side], 1 - side
        return pass_half(kind, ahead, half, side, fars[kind].at[side, halves[kind][half], :], 1)

    def pass_sum(kind, near):
        found = []
        for side, ahead in ((0, 1), (1, 3)):
            near[side].wait_recv()
            part = halves[kind][side]
            sums[kind][ahead, part, :] = (
                sums[kind][ahead, part, :].astype(F32) + nears[kind][side].astype(F32)
            ).astype(BF16)
            found.append(
                pass_half(kind, ahead, side, side, fars[kind].at[side, part, :], 2)
            )
        return found

    out_state = first_hop(0)
    ends = []
    fetch["h"].wait()
    for ahead in (2, 1, 3):
        fetch[ahead].wait()
        swaps[ahead].wait_recv()
        if ahead == 2:
            load("g", g_hbm, gall)
            load("d", wd_hbm.at[0], wd)
            load("pre", pre_hbm, pre)
            load("x", x_hbm, xb)
        weight_out(ahead)
        if ahead == 2:
            near_sent_out = pass_near(0)
        else:
            ends.append(pass_far(0, ahead // 2))
    fetch["g"].wait()
    fetch["d"].wait()
    fetch["pre"].wait()

    @pl.loop(0, 3)
    def _(n):
        u_cols = pl.ds(pl.multiple_of(n * 256, 256), 256)
        v_cols = pl.ds(pl.multiple_of(HID + n * 256, 256), 256)
        grad = lax.dot_general(
            gall[...], wd[u_cols, :], (((1,), (1,)), ((), ())), preferred_element_type=F32
        )
        u = pre[:, u_cols]
        logistic = jax.nn.sigmoid(u)
        pgb[:ROWS, v_cols] = (grad * u * logistic).astype(BF16)
        pgb[:ROWS, u_cols] = (
            grad * pre[:, v_cols] * logistic * (1.0 + u * (1.0 - logistic))
        ).astype(BF16)

    swap = remote(
        pgb.at[mine], pgb.at[theirs], core_send.at[4], core_recv.at[4], other_core()
    )
    swap.start()
    def token_side(first, end):
        @pl.loop(first, end)
        def _(n):
            @pl.when(n + 1 < WIDTH // 256)
            def _():
                wgu_tile(n + 1).start()

            wgu_tile(n).wait()
            cols = pl.ds(pl.multiple_of(n * 256, 256), 256)
            sig[:, cols] = lax.dot_general(
                pgb[:ROWS, :],
                wgu[lax.rem(n, 2)],
                (((1,), (1,)), ((), ())),
                preferred_element_type=F32,
            ).astype(BF16)

    token_side(0, 6)
    fetch["x"].wait()
    swap.wait_recv()
    weight_in(2)
    near_sent_in = pass_near(1)
    token_side(6, WIDTH // 256)
    sig_state = first_hop(1)
    ends += pass_sum(0, near_sent_out)
    fetch[0].wait()
    swaps[0].wait_recv()
    weight_out(0)
    weight_in(0)
    combine(0, *out_state)
    for ahead in (1, 3):
        weight_in(ahead)
        ends.append(pass_far(1, ahead // 2))
    ends += pass_sum(1, near_sent_in)
    for route in range(2):
        for copy in sig_state[0][route]:
            copy.wait_recv()
    out_finals = pass_partial(0)
    combine(1, [[], []], sig_state[1])
    sig_finals = pass_partial(1)
    for copy in ends[:4]:
        copy.wait_recv()

    @pl.loop(0, 4)
    def _(n):
        part = pl.ds(pl.multiple_of(n * 192, 192), 192)
        total = sum_out[0, part, :].astype(F32)
        total += far_out[0, part, :].astype(F32) + far_out[1, part, :].astype(F32)
        grad_out[part, :] = total.astype(BF16)

    results = []

    def leave(src, dst):
        copy = pltpu.make_async_copy(src, dst, local_sem.at[27 + len(results)])
        copy.start()
        results.append(copy)

    leave(grad_out, down_hbm)
    finish(0, out_finals, layer_out)
    leave(layer_out, layer_hbm)
    finish(1, sig_finals, token_grad)
    leave(token_grad, token_hbm)
    for copy in ends[4:]:
        copy.wait_recv()

    @pl.loop(0, 4)
    def _(n):
        part = pl.ds(pl.multiple_of(n * 128, 128), 128)
        total = sum_in[0, part, :].astype(F32)
        total += far_in[0, part, :].astype(F32) + far_in[1, part, :].astype(F32)
        sum_in[0, part, :] = total.astype(BF16)

    store_in = pltpu.make_async_copy(sum_in.at[0], grad_in, local_sem.at[1])
    store_in.start()
    for copy in sends + [swaps[ahead] for ahead in range(4)] + [swap]:
        copy.wait_send()
    for copy in results + [store_in]:
        copy.wait()


def last_kernel(*refs):
    count = len(refs) // 3
    held, sems = refs[2 * count : 3 * count], refs[-1]
    steps = 4
    loads, stores = [], []
    for n in range(count):
        size = refs[n].shape[0] // steps
        for step in range(steps):
            part = pl.ds(step * size, size)
            loads.append(
                pltpu.make_async_copy(refs[n].at[part], held[n].at[part], sems.at[0, n, step])
            )
            stores.append(
                pltpu.make_async_copy(
                    held[n].at[part], refs[count + n].at[part], sems.at[1, n, step]
                )
            )
    for copy in loads:
        copy.start()
    for load, store in zip(loads, stores):
        load.wait()
        store.start()
    for copy in stores:
        copy.wait()


VMEM = pl.BlockSpec(memory_space=pltpu.VMEM)
ANY = pl.BlockSpec(memory_space=pl.ANY)
DMA = pltpu.SemaphoreType.DMA


def dispatch(ids, gates, tokens, cotangent, gate_up, down_weight):
    table = jax.ShapeDtypeStruct((2, 16, 4 * TOK), F32)
    return pl.pallas_call(
        dispatch_kernel,
        out_shape=(
            jax.ShapeDtypeStruct((ROWS, WIDTH), BF16),
            jax.ShapeDtypeStruct((2 * ROWS, HALF), BF16),
            jax.ShapeDtypeStruct((ROWS, WIDTH), BF16),
            jax.ShapeDtypeStruct((2 * ROWS, HID), BF16),
            jax.ShapeDtypeStruct((ROWS, 2 * HID), F32),
            table,
            table,
        ),
        in_specs=[VMEM] * 4 + [ANY] * 2,
        out_specs=(ANY,) * 5 + (VMEM,) * 2,
        scratch_shapes=[
            pltpu.VMEM((WIDTH, 2 * HID), BF16),
            pltpu.VMEM((HID, WIDTH), BF16),
            pltpu.VMEM((16, 2 * TOK), F32),
            pltpu.VMEM((2, 4, 16, 2 * TOK), F32),
            pltpu.VMEM((2, 2, 4 * TOK, HALF), BF16),
            pltpu.VMEM((2, 2, 3, 4 * MAIN, HALF), BF16),
            pltpu.VMEM((2, 2, 3, 16, CHUNK), BF16),
            pltpu.VMEM((2, 2, 64, CHUNK), BF16),
            pltpu.VMEM((ROWS, WIDTH), BF16),
            pltpu.VMEM((2, 4 * MAIN, HALF), BF16),
            pltpu.VMEM((16, WIDTH), BF16),
            pltpu.VMEM((ROWS, 2 * HID), F32),
            pltpu.VMEM((ROWS, HID), BF16),
            pltpu.VMEM((ROWS, WIDTH), BF16),
            DMA((16,)),
            DMA((2, 4)),
            DMA((2, 4)),
            DMA((2, 2, 4)),
            DMA((2, 2, 4)),
            DMA((2, 2, 4, 4)),
            DMA((2, 2, 4, 4)),
            DMA((2, 2, 4)),
            DMA((2, 2, 4)),
            DMA((5,)),
            DMA((5,)),
        ],
        compiler_params=pltpu.CompilerParams(
            collective_id=0, has_side_effects=True, vmem_limit_bytes=60 << 20
        ),
        cost_estimate=pl.CostEstimate(
            flops=20 * 10**9, bytes_accessed=40 * 10**6, transcendentals=10**6
        ),
    )(ids, gates, tokens, cotangent, gate_up, down_weight)


def give_back(out_rows, gate_up, x_rows, g_rows, hidden, pre_act, down_weight, rank, share):
    result = jax.ShapeDtypeStruct((TOK, WIDTH), BF16)
    return pl.pallas_call(
        return_kernel,
        out_shape=(
            result,
            result,
            jax.ShapeDtypeStruct((HID, 512), BF16),
            jax.ShapeDtypeStruct((512, 2 * HID), BF16),
        ),
        in_specs=[ANY] * 7 + [VMEM] * 2,
        out_specs=(ANY,) * 4,
        scratch_shapes=[
            pltpu.VMEM((TOK, WIDTH), BF16),
            pltpu.VMEM((TOK, WIDTH), BF16),
            pltpu.VMEM((HID, 512), BF16),
            pltpu.VMEM((2 * ROWS, HALF), BF16),
            pltpu.VMEM((2 * ROWS, HALF), BF16),
            pltpu.VMEM((ROWS, WIDTH), BF16),
            pltpu.VMEM((2 * ROWS, HID), BF16),
            pltpu.VMEM((ROWS, 2 * HID), F32),
            pltpu.VMEM((HID, WIDTH), BF16),
            pltpu.VMEM((2 * ROWS, 2 * HID), BF16),
            pltpu.VMEM((2, 256, 2 * HID), BF16),
            pltpu.VMEM((4, 512, 2 * HID), BF16),
            pltpu.VMEM((4, HID, 512), BF16),
            pltpu.VMEM((2, 256, 2 * HID), BF16),
            pltpu.VMEM((2, HID // 2, 512), BF16),
            pltpu.VMEM((2, 512, 2 * HID), BF16),
            pltpu.VMEM((2, HID, 512), BF16),
            pltpu.VMEM((16, WIDTH), BF16),
            pltpu.VMEM((2, 2, 64, CHUNK), BF16),
            pltpu.VMEM((2, 2, 4, 4 * MAIN, HALF), BF16),
            pltpu.VMEM((2, 2, 64, CHUNK), BF16),
            pltpu.VMEM((2, 2, 4 * TOK, HALF), BF16),
            pltpu.VMEM((2, 2, 3, TOK, HALF), BF16),
            DMA((30,)),
            DMA((2,)),
            DMA((2, 2, 4, 4)),
            DMA((2, 2, 4, 4)),
            DMA((2, 2, 4)),
            DMA((2, 2, 4)),
            DMA((2, 2, 4)),
            DMA((2, 2, 4)),
            DMA((3, 2, 2)),
            DMA((3, 2, 2)),
            DMA((5,)),
            DMA((5,)),
        ],
        compiler_params=pltpu.CompilerParams(
            collective_id=1, has_side_effects=True, vmem_limit_bytes=62 << 20
        ),
        cost_estimate=pl.CostEstimate(
            flops=26 * 10**9, bytes_accessed=100 * 10**6, transcendentals=0
        ),
    )(out_rows, gate_up, x_rows, g_rows, hidden, pre_act, down_weight, rank, share)


def last(*results):
    return pl.pallas_call(
        last_kernel,
        out_shape=tuple(jax.ShapeDtypeStruct(a.shape, a.dtype) for a in results),
        in_specs=[ANY] * len(results),
        out_specs=(ANY,) * len(results),
        scratch_shapes=[pltpu.VMEM(a.shape, a.dtype) for a in results]
        + [DMA((2, len(results), 4))],
        cost_estimate=pl.CostEstimate(
            flops=0, bytes_accessed=7 * 10**6, transcendentals=0
        ),
    )(*results)


def per_device(tokens, cotangent, expert_ids, gate_fixed, gate_up, down_weight):
    out_rows, x_rows, g_rows, hidden, pre_act, rank, share = dispatch(
        expert_ids.T, gate_fixed.T, tokens, cotangent, gate_up, down_weight
    )
    layer_out, token_grad, grad_out, grad_in = last(
        *give_back(
            out_rows, gate_up, x_rows, g_rows, hidden, pre_act, down_weight, rank, share
        )
    )
    return layer_out, token_grad, grad_in[None], grad_out[None]


def solution(mesh):
    rows = P(("ep", "dp"), None)
    return jax.shard_map(
        per_device,
        mesh=mesh,
        in_specs=(rows, rows, rows, rows, P("ep", None, None), P("ep", None, None)),
        out_specs=(rows, rows, P("ep", "dp", None), P("ep", None, "dp")),
        check_vma=False,
    )
```

```python
import functools

import jax
import jax.numpy as jnp
from jax import lax
from jax.experimental import pallas as pl
from jax.experimental.pallas import tpu as pltpu
from jax.sharding import PartitionSpec as P

BF16 = jnp.bfloat16
F32 = jnp.float32
MESH = pl.DeviceIdType.MESH
TOK = 64
WIDTH = 4096
HALF = WIDTH // 2
CHUNK = HALF // 4
HID = 768
MAIN = 32
ROWS = 16 * MAIN + 16
ORDER = (2, 1, 3)


def place():
    ep = lax.axis_index("ep")
    return ep // 4, ep % 4


def peer(axis, distance):
    z, x = place()
    if axis == "z":
        z = lax.rem(z + distance, 4)
    else:
        x = lax.rem(x + distance, 4)
    return {"ep": z * 4 + x, "dp": lax.axis_index("dp")}


def along_y(distance):
    dp = lax.axis_index("dp")
    return {"ep": lax.axis_index("ep"), "dp": lax.rem(dp + 2 * distance, 8)}


def other_core():
    dp = lax.axis_index("dp")
    return {"ep": lax.axis_index("ep"), "dp": dp + 1 - 2 * lax.rem(dp, 2)}


def first_axis(route):
    return ("z", "x")[route]


def second_axis(route):
    return ("x", "z")[route]


def coord(axis):
    z, x = place()
    return z if axis == "z" else x


def expert_at(route, position):
    z, x = place()
    return z * 4 + position if route == 0 else position * 4 + x


def iota(shape, dim):
    return lax.broadcasted_iota(jnp.int32, shape, dim)


def enter(peers):
    barrier = pltpu.get_barrier_semaphore()
    for device in peers:
        pl.semaphore_signal(barrier, 1, device_id=device, device_id_type=MESH)
    pl.semaphore_wait(barrier, len(peers))


def remote(src, dst, send_sem, recv_sem, device):
    return pltpu.make_async_remote_copy(
        src_ref=src,
        dst_ref=dst,
        send_sem=send_sem,
        recv_sem=recv_sem,
        device_id=device,
        device_id_type=MESH,
    )


def pick_row(table, index):
    rows = iota(table.shape, 0)
    return jnp.sum(jnp.where(rows == index, table, 0.0), axis=0, keepdims=True)


def slot_rows(rank, chunk):
    source = iota((1, 4 * TOK), 1) // TOK
    rank = rank.astype(jnp.int32)
    main = jnp.where(rank >= 0, rank + MAIN * source, -1)
    return jnp.where(rank == MAIN, 4 * MAIN + 4 * chunk + source, main)


def overflow_target(route, shape, dim):
    row = iota(shape, dim)
    sender, chunk, source = row // 16, lax.rem(row, 16) // 4, lax.rem(row, 4)
    slot = sender * 4 + source if route == 0 else source * 4 + sender
    return slot, chunk


def dispatch_kernel(
    ids_ref,
    gate_ref,
    tok_ref,
    cot_ref,
    wgu_hbm,
    wd_hbm,
    out_hbm,
    x_hbm,
    g_hbm,
    h_hbm,
    pre_hbm,
    far_hbm,
    rank_out,
    share_out,
    wgu,
    wd,
    meta_own,
    meta,
    gathered,
    staged,
    staged_over,
    over,
    xbuf,
    own,
    own_over,
    pre,
    hid,
    obuf,
    far_rows,
    far_sum,
    local_sem,
    meta_send,
    meta_recv,
    gat_send,
    gat_recv,
    main_send,
    main_recv,
    over_send,
    over_recv,
    core_send,
    core_recv,
):
    z, x = place()
    load_gu = pltpu.make_async_copy(wgu_hbm.at[0], wgu, local_sem.at[0])
    load_d = pltpu.make_async_copy(wd_hbm.at[0], wd, local_sem.at[1])
    load_gu.start()
    load_d.start()

    enter([peer(axis, d) for axis in ("z", "x") for d in ORDER] + [other_core()])

    sends = []
    sources = (tok_ref, cot_ref)

    def block(which, route, position, columns):
        rows = pl.ds(pl.multiple_of(position * TOK, TOK), TOK)
        return gathered.at[which, route, rows, columns]

    def gather_start(which):
        copies = [{}, {}]
        for d in (1, 3):
            for route in range(2):
                here = coord(first_axis(route))
                copy = remote(
                    sources[which].at[:, pl.ds(route * HALF, HALF)],
                    block(which, route, here, pl.ds(0, HALF)),
                    gat_send.at[which, route, d],
                    gat_recv.at[which, route, d],
                    peer(first_axis(route), d),
                )
                copy.start()
                sends.append(copy)
                copies[route][d] = copy
        for route in range(2):
            here = coord(first_axis(route))
            gathered[which, route, pl.ds(pl.multiple_of(here * TOK, TOK), TOK), :] = sources[
                which
            ][:, route * HALF : (route + 1) * HALF]
        return copies

    def gather_pass(which, copies):
        passed = []
        for d in (1, 3):
            for route in range(2):
                copies[route][d].wait_recv()
                axis = first_axis(route)
                behind = lax.rem(coord(axis) + 4 - d, 4)
                columns = pl.ds((d // 2) * (HALF // 2), HALF // 2)
                copy = remote(
                    block(which, route, behind, columns),
                    block(which, route, behind, columns),
                    gat_send.at[which, route, d - 1],
                    gat_recv.at[which, route, d - 1],
                    peer(axis, d),
                )
                copy.start()
                sends.append(copy)
                passed.append(copy)
        return passed

    tok_copies = gather_start(0)

    gates = gate_ref[...].astype(F32)
    share = gates / jnp.sum(gates, axis=0, keepdims=True)
    ids = ids_ref[...]
    expert = iota((16, TOK), 0)
    named = jnp.zeros((16, TOK), F32)
    weight = jnp.zeros((16, TOK), F32)
    for k in range(8):
        hit = ids[k : k + 1, :] == expert
        named += jnp.where(hit, 1.0, 0.0)
        weight += jnp.where(hit, share[k : k + 1, :], 0.0)
    before = jnp.where(iota((TOK, TOK), 0) < iota((TOK, TOK), 1), 1.0, 0.0)
    rank = jnp.dot(named.astype(BF16), before.astype(BF16), preferred_element_type=F32)
    rank = jnp.where(named > 0.0, rank, -1.0)
    meta_own[...] = jnp.concatenate([rank, weight], axis=1)

    meta_recvs = []
    for route in range(2):
        here = coord(first_axis(route))
        for d in ORDER:
            copy = remote(
                meta_own,
                meta.at[route, here],
                meta_send.at[route, d],
                meta_recv.at[route, d],
                peer(first_axis(route), d),
            )
            copy.start()
            sends.append(copy)
            meta_recvs.append(copy)
        meta[route, pl.ds(here, 1)] = meta_own[...][None]

    cot_copies = gather_start(1)
    for copy in meta_recvs:
        copy.wait_recv()
    for route in range(2):
        rank_out[route] = jnp.concatenate([meta[route, s][:, :TOK] for s in range(4)], axis=1)
        share_out[route] = jnp.concatenate([meta[route, s][:, TOK:] for s in range(4)], axis=1)

    buffers = (xbuf, g_hbm)
    postponed = []
    y = lax.axis_index("dp") // 2

    def halves_of(route):
        here = lax.rem(y, 2)
        far = (1 - y // 2) == route
        first = jnp.where(far, here, 1 - here)
        return first, 1 - first


    def select(which, route, d):
        position = lax.rem(coord(second_axis(route)) + d, 4)
        expert = expert_at(route, position)
        rank_row = pick_row(rank_out[route], expert)
        share_row = pick_row(share_out[route], expert)
        here = coord(second_axis(route))
        target = buffers[which]
        total = jnp.zeros((16, CHUNK), F32)
        for c in range(4):
            hit = slot_rows(rank_row, c) == iota((4 * MAIN + 16, 4 * TOK), 0)
            choose = jnp.where(hit, 1.0, 0.0).astype(BF16)
            rows = jnp.dot(
                choose,
                gathered[which, route, :, c * CHUNK : (c + 1) * CHUNK],
                preferred_element_type=F32,
            )
            if which == 1:
                rows = rows * jnp.sum(jnp.where(hit, share_row, 0.0), axis=1, keepdims=True)
            main = rows[: 4 * MAIN].astype(BF16)
            total += rows[4 * MAIN :]
            if which == 1 and not d:
                own[route, :, c * CHUNK : (c + 1) * CHUNK] = main
            elif d:
                staged[which, route, d - 1, :, c * CHUNK : (c + 1) * CHUNK] = main
            else:
                columns = slice(route * HALF + c * CHUNK, route * HALF + (c + 1) * CHUNK)
                if route == 0:
                    target[pl.ds(pl.multiple_of(here * 128, 128), 128), columns] = main
                else:
                    for s in range(4):
                        first = pl.multiple_of((s * 4 + here) * MAIN, MAIN)
                        target[pl.ds(first, MAIN), columns] = main[s * MAIN : (s + 1) * MAIN]
        mine = pl.ds(pl.multiple_of(here * 16, 16), 16)
        if not d:
            over[which, route, mine, :] = total.astype(BF16)
            return []
        staged_over[which, route, d - 1] = total.astype(BF16)
        device = peer(second_axis(route), d)
        size = HALF if which == 0 else HALF // 2
        later = []
        copies = [
            remote(
                staged_over.at[which, route, d - 1],
                over.at[which, route, mine, :],
                over_send.at[which, route, d],
                over_recv.at[which, route, d],
                device,
            )
        ]
        for part in range(HALF // size):
            begin = 0 if which == 0 else pl.multiple_of(halves_of(route)[part] * size, size)
            taken = pl.ds(begin, size)
            columns = pl.ds(pl.multiple_of(route * HALF + begin, size), size)
            found = later if part else copies
            if route == 0:
                found.append(
                    remote(
                        staged.at[which, route, d - 1, :, taken],
                        target.at[pl.ds(pl.multiple_of(here * 128, 128), 128), columns],
                        main_send.at[which, route, d, 4 * part],
                        main_recv.at[which, route, d, 4 * part],
                        device,
                    )
                )
            else:
                for s in range(4):
                    first = pl.multiple_of((s * 4 + here) * MAIN, MAIN)
                    found.append(
                        remote(
                            staged.at[which, route, d - 1, pl.ds(s * MAIN, MAIN), taken],
                            target.at[pl.ds(first, MAIN), columns],
                            main_send.at[which, route, d, 4 * part + s],
                            main_recv.at[which, route, d, 4 * part + s],
                            device,
                        )
                    )
        for copy in copies:
            copy.start()
        sends.extend(copies)
        postponed.extend(later)
        return copies

    def second_hop(which, passed):
        arrivals = []
        for copy in passed:
            copy.wait_recv()
        for d in ORDER:
            for route in range(2):
                arrivals.extend(select(which, route, d))
        return arrivals

    def finish(which, arrivals):
        for copy in arrivals:
            copy.wait_recv()
        for route in range(2):
            slot, chunk = overflow_target(route, (16, 64), 1)
            for c in range(4):
                spread = jnp.where((slot == iota((16, 64), 0)) & (chunk == c), 1.0, 0.0)
                first = route * HALF + c * CHUNK
                tail = jnp.dot(
                    spread.astype(BF16), over[which, route], preferred_element_type=F32
                ).astype(BF16)
                if which == 0:
                    xbuf[16 * MAIN : ROWS, first : first + CHUNK] = tail
                else:
                    own_over[:, first : first + CHUNK] = tail

    tok_passed = gather_pass(0, tok_copies)
    cot_passed = gather_pass(1, cot_copies)
    x_arrivals = second_hop(0, tok_passed)
    g_arrivals = second_hop(1, cot_passed)
    for copy in postponed:
        copy.start()
    sends.extend(postponed)
    for which in range(2):
        for route in range(2):
            select(which, route, 0)
    load_gu.wait()
    load_d.wait()

    core = lax.rem(lax.axis_index("dp"), 2)
    stores = []
    shared = []

    def store(src, dst):
        copy = pltpu.make_async_copy(src, dst, local_sem.at[2 + len(stores)])
        copy.start()
        stores.append(copy)
        return copy

    def share(src, dst):
        slot = len(shared)
        copy = remote(src, dst, core_send.at[slot], core_recv.at[slot], other_core())
        copy.start()
        shared.append(copy)
        return copy

    before_own = len(stores)
    for route in range(2):
        here = coord(second_axis(route))
        columns = pl.ds(route * HALF, HALF)
        if route == 0:
            first = pl.multiple_of(here * 128, 128)
            store(own.at[route], g_hbm.at[pl.ds(first, 128), columns])
        else:
            for s in range(4):
                first = pl.multiple_of((s * 4 + here) * MAIN, MAIN)
                store(
                    own.at[route, pl.ds(s * MAIN, MAIN), :],
                    g_hbm.at[pl.ds(first, MAIN), columns],
                )

    own_stores = stores[before_own:]
    mine, theirs = pl.ds(0, ROWS), pl.ds(ROWS, ROWS)

    def split(src, dst):
        for block in range(4):
            there = pl.ds(block * 512, 512)
            keep = pl.ds(pl.multiple_of((2 * block + core) * 512, 512), 512)
            give = pl.ds(pl.multiple_of((2 * block + 1 - core) * 512, 512), 512)
            share(src.at[:, give], dst.at[theirs, there])
            store(src.at[:, keep], dst.at[mine, there])

    finish(0, x_arrivals)
    split(xbuf, x_hbm)

    @pl.loop(0, 3)
    def _(n):
        u_cols = pl.ds(pl.multiple_of(n * 256, 256), 256)
        v_cols = pl.ds(pl.multiple_of(HID + n * 256, 256), 256)
        u = jnp.dot(xbuf[...], wgu[:, u_cols], preferred_element_type=F32)
        pre[:, u_cols] = u
        v = jnp.dot(xbuf[...], wgu[:, v_cols], preferred_element_type=F32)
        pre[:, v_cols] = v
        hid[:ROWS, u_cols] = (pre[:, u_cols] * jax.nn.sigmoid(pre[:, u_cols]) * v).astype(BF16)

    hid_share = share(hid.at[mine], hid.at[theirs])
    store(pre, pre_hbm)
    finish(1, g_arrivals)
    own_stores.append(store(own_over, g_hbm.at[pl.ds(16 * MAIN, 16), :]))
    for copy in own_stores:
        copy.wait()

    def far_columns(of_core):
        return pl.ds(pl.multiple_of((2 * lax.rem(y + 2, 4) + of_core) * 512, 512), 512)

    far_load = store(g_hbm.at[:, far_columns(core)], far_rows.at[mine])
    far_share = share(g_hbm.at[:, far_columns(1 - core)], far_rows.at[theirs])

    @pl.loop(0, HALF // 256)
    def _(n):
        cols = pl.ds(pl.multiple_of(n * 256, 256), 256)
        obuf[:, cols] = jnp.dot(
            hid[:ROWS, :], wd[:, cols], preferred_element_type=F32
        ).astype(BF16)

    store(obuf, out_hbm)
    hid_share.wait_recv()
    store(hid, h_hbm)
    far_load.wait()
    far_share.wait_recv()

    @pl.loop(0, 3)
    def _(n):
        piece = pl.ds(pl.multiple_of(n * 256, 256), 256)
        far_sum[piece, :] = lax.dot_general(
            hid[:, piece],
            far_rows[...],
            (((0,), (0,)), ((), ())),
            preferred_element_type=F32,
        ).astype(BF16)

    store(far_sum, far_hbm)
    for copy in postponed:
        copy.wait_recv()
    for copy in stores:
        if copy is not far_load and all(copy is not other for other in own_stores):
            copy.wait()
    for copy in shared:
        if copy is hid_share or copy is far_share:
            copy.wait_send()
        else:
            copy.wait()
    for copy in sends:
        copy.wait_send()


def return_kernel(
    out_hbm,
    wgu_hbm,
    x_hbm,
    g_hbm,
    h_hbm,
    pre_hbm,
    far_hbm,
    wd_hbm,
    rank_ref,
    share_ref,
    layer_hbm,
    token_hbm,
    down_hbm,
    grad_in,
    layer_out,
    token_grad,
    grad_out,
    xb,
    gb,
    gall,
    hb,
    pre,
    wd,
    pgb,
    wgu,
    sum_in,
    sum_out,
    near_in,
    near_out,
    far_in,
    far_out,
    tail,
    compact,
    rows,
    rows_over,
    partial,
    final,
    local_sem,
    wgu_sem,
    main_send,
    main_recv,
    over_send,
    over_recv,
    part_send,
    part_recv,
    dp_send,
    dp_recv,
    core_send,
    core_recv,
):
    z, x = place()
    y = lax.axis_index("dp") // 2
    core = lax.rem(lax.axis_index("dp"), 2)
    sig = gall
    mine, theirs = pl.ds(0, ROWS), pl.ds(ROWS, ROWS)
    fetch = {}

    def load(name, src, dst):
        copy = pltpu.make_async_copy(src, dst, local_sem.at[18 + len(fetch)])
        copy.start()
        fetch[name] = copy

    def columns_of(ahead, of_core):
        first = (2 * lax.rem(y + ahead, 4) + of_core) * 512
        return pl.ds(pl.multiple_of(first, 512), 512)

    def place_of(ahead):
        return pl.ds(pl.multiple_of(lax.rem(y + ahead, 4) * 512, 512), 512)

    load("h", h_hbm, hb)
    load("d", wd_hbm.at[0], wd)
    for ahead in (1, 3, 0):
        load(ahead, g_hbm.at[:, columns_of(ahead, core)], gb.at[mine, place_of(ahead)])
    load_tail = pltpu.make_async_copy(
        out_hbm.at[pl.ds(16 * MAIN, 16), :], tail.at[:, pl.ds(0, HALF)], local_sem.at[0]
    )
    load_tail.start()

    def wgu_tile(n):
        rows = pl.ds(pl.multiple_of(n * 256, 256), 256)
        slot = lax.rem(n, 2)
        return pltpu.make_async_copy(wgu_hbm.at[0, rows, :], wgu.at[slot], wgu_sem.at[slot])

    wgu_tile(0).start()
    enter(
        [peer(axis, d) for axis in ("z", "x") for d in ORDER]
        + [along_y(d) for d in (1, 3)]
        + [other_core()]
    )
    sends = []
    def pieces(which, route, position, slot):
        columns = pl.ds(route * HALF, HALF)
        if route == 0:
            rows_there = pl.ds(pl.multiple_of(position * 128, 128), 128)
            if which == 0:
                src = out_hbm.at[rows_there]
            else:
                src = sig.at[rows_there, columns]
            return [(src, rows.at[which, route, slot])]
        found = []
        for s in range(4):
            dst = rows.at[which, route, slot, pl.ds(s * MAIN, MAIN), :]
            if which == 0:
                first = pl.multiple_of((s % 2) * 128 + position * MAIN, MAIN)
                found.append((partial.at[1, s // 2, pl.ds(first, MAIN), :], dst))
            else:
                first = pl.multiple_of((s * 4 + position) * MAIN, MAIN)
                found.append((sig.at[pl.ds(first, MAIN), columns], dst))
        return found

    early = []

    def first_hop(which, routes):
        arrivals = [[], []]
        for d in ORDER:
            for route in routes:
                here = coord(second_axis(route))
                there = lax.rem(here + d, 4)
                for s, (src, dst) in enumerate(pieces(which, route, there, here)):
                    copy = remote(
                        src,
                        dst,
                        main_send.at[which, route, d, s],
                        main_recv.at[which, route, d, s],
                        peer(second_axis(route), d),
                    )
                    copy.start()
                    (early if which == 0 and route == 1 else sends).append(copy)
                    arrivals[route].append(copy)
        owns = [[], []]
        for route in routes:
            here = coord(second_axis(route))
            for s, (src, dst) in enumerate(pieces(which, route, here, here)):
                copy = pltpu.make_async_copy(src, dst, local_sem.at[2 + which * 8 + route * 4 + s])
                copy.start()
                owns[route].append(copy)
        if which == 0 and routes[0] == 0:
            load_tail.wait()
        last = tail if which == 0 else sig.at[pl.ds(16 * MAIN, 16), :]
        for route in routes:
            here = coord(second_axis(route))
            slot, chunk = overflow_target(route, (64, 16), 0)
            total = jnp.zeros((64, CHUNK), F32)
            for c in range(4):
                take = jnp.where((slot == iota((64, 16), 1)) & (chunk == c), 1.0, 0.0)
                first = route * HALF + c * CHUNK
                total += jnp.dot(
                    take.astype(BF16),
                    last[:, first : first + CHUNK],
                    preferred_element_type=F32,
                )
            compact[which, route] = total.astype(BF16)
            mine = pl.ds(pl.multiple_of(here * 16, 16), 16)
            rows_over[which, route, mine, :] = compact[which, route, mine, :]
            for d in ORDER:
                there = lax.rem(here + d, 4)
                copy = remote(
                    compact.at[which, route, pl.ds(pl.multiple_of(there * 16, 16), 16), :],
                    rows_over.at[which, route, mine, :],
                    over_send.at[which, route, d],
                    over_recv.at[which, route, d],
                    peer(second_axis(route), d),
                )
                copy.start()
                sends.append(copy)
                arrivals[route].append(copy)
        return arrivals, owns

    def combine(which, arrivals, owns):
        for route in range(2):
            for copy in arrivals[route]:
                copy.wait_recv()
            for copy in owns[route]:
                copy.wait()
            ranks = [pick_row(rank_ref[route], expert_at(route, p)) for p in range(4)]
            shares = [pick_row(share_ref[route], expert_at(route, p)) for p in range(4)]
            for c in range(4):
                main, rest = [], []
                for p in range(4):
                    hit = slot_rows(ranks[p], c) == iota((4 * MAIN + 16, 4 * TOK), 0)
                    value = shares[p] if which == 0 else 1.0
                    spread = jnp.where(hit, value, 0.0)
                    main.append(spread[: 4 * MAIN])
                    rest.append(spread[4 * MAIN :])
                main = jnp.concatenate(main, axis=0).astype(BF16)
                rest = jnp.concatenate(rest, axis=0).astype(BF16)
                columns = slice(c * CHUNK, (c + 1) * CHUNK)
                along = (((0,), (0,)), ((), ()))
                total = lax.dot_general(
                    main,
                    rows[which, route, :, :, columns].reshape(16 * MAIN, CHUNK),
                    along,
                    preferred_element_type=F32,
                ) + lax.dot_general(
                    rest, rows_over[which, route], along, preferred_element_type=F32
                )
                partial[which, route, :, columns] = total.astype(BF16)

    def pass_partial(which):
        finals = []
        for d in ORDER:
            for route in range(2):
                here = coord(first_axis(route))
                there = lax.rem(here + d, 4)
                copy = remote(
                    partial.at[which, route, pl.ds(pl.multiple_of(there * TOK, TOK), TOK), :],
                    final.at[which, route, d - 1],
                    part_send.at[which, route, d],
                    part_recv.at[which, route, d],
                    peer(first_axis(route), d),
                )
                copy.start()
                sends.append(copy)
                finals.append(copy)
        return finals

    def finish(which, finals, result):
        for copy in finals:
            copy.wait_recv()
        for route in range(2):
            here = coord(first_axis(route))
            own = partial[which, route, pl.ds(pl.multiple_of(here * TOK, TOK), TOK), :]
            total = own.astype(F32)
            for d in range(3):
                total += final[which, route, d].astype(F32)
            result[:, route * HALF : (route + 1) * HALF] = total.astype(BF16)

    along = (((0,), (0,)), ((), ()))

    def weight_out(ahead):
        cols = place_of(ahead)

        @pl.loop(0, 3)
        def _(n):
            piece = pl.ds(pl.multiple_of(n * 256, 256), 256)
            sum_out[ahead, piece, :] = lax.dot_general(
                hb[:, piece], gb[:, cols], along, preferred_element_type=F32
            ).astype(BF16)

    def weight_in(ahead):
        first = lax.rem(y + ahead, 4) * 512

        @pl.loop(0, 2)
        def _(n):
            piece = pl.ds(pl.multiple_of(n * 256, 256), 256)
            part = pl.ds(pl.multiple_of(first + n * 256, 256), 256)
            sum_in[ahead, piece, :] = lax.dot_general(
                xb[:, part], pgb[...], along, preferred_element_type=F32
            ).astype(BF16)

    half_in = (pl.ds(0, 256), pl.ds(256, 256))
    half_out = (pl.ds(0, HID // 2), pl.ds(HID // 2, HID // 2))

    sums = (sum_out, sum_in)
    nears = (near_out, near_in)
    fars = (far_out, far_in)
    halves = (half_out, half_in)

    def pass_half(kind, ahead, half, side, dst, slot):
        src = far_hbm.at[halves[kind][half], :]
        if kind or ahead != 2:
            src = sums[kind].at[ahead, halves[kind][half], :]
        copy = remote(
            src,
            dst,
            dp_send.at[slot, side, kind],
            dp_recv.at[slot, side, kind],
            along_y((1, 3)[side]),
        )
        copy.start()
        sends.append(copy)
        return copy

    def pass_near(kind):
        return [pass_half(kind, 2, side, side, nears[kind].at[side], 0) for side in range(2)]

    def pass_far(kind, side):
        ahead, half = (1, 3)[side], 1 - side
        return pass_half(kind, ahead, half, side, fars[kind].at[side, halves[kind][half], :], 1)

    def pass_sum(kind, near):
        found = []
        for side, ahead in ((0, 1), (1, 3)):
            near[side].wait_recv()
            part = halves[kind][side]
            sums[kind][ahead, part, :] = (
                sums[kind][ahead, part, :].astype(F32) + nears[kind][side].astype(F32)
            ).astype(BF16)
            found.append(
                pass_half(kind, ahead, side, side, fars[kind].at[side, part, :], 2)
            )
        return found

    near_sent_out = pass_near(0)
    swaps = {}
    for ahead in (1, 3, 0):
        swaps[ahead] = remote(
            g_hbm.at[:, columns_of(ahead, 1 - core)],
            gb.at[theirs, place_of(ahead)],
            core_send.at[ahead],
            core_recv.at[ahead],
            other_core(),
        )
        swaps[ahead].start()

    out_state = first_hop(0, (0,))
    ends = []
    fetch["h"].wait()
    fetch["d"].wait()
    load("g", g_hbm, gall)
    load("pre", pre_hbm, pre)
    load("x", x_hbm, xb)

    @pl.loop(0, HALF // 256)
    def _(n):
        cols = pl.ds(pl.multiple_of(n * 256, 256), 256)
        there = pl.ds(pl.multiple_of(HALF + n * 256, 256), 256)
        tile = jnp.dot(hb[:ROWS, :], wd[:, there], preferred_element_type=F32).astype(BF16)
        partial[1, 0, :, cols] = tile[:256]
        partial[1, 1, :, cols] = tile[256:512]
        tail[:, there] = tile[512:]

    for old, new in zip(out_state, first_hop(0, (1,))):
        old[1] = new[1]
    for ahead in (1, 3):
        fetch[ahead].wait()
        swaps[ahead].wait_recv()
        weight_out(ahead)
        ends.append(pass_far(0, ahead // 2))
    fetch["g"].wait()
    fetch["pre"].wait()

    @pl.loop(0, 3)
    def _(n):
        u_cols = pl.ds(pl.multiple_of(n * 256, 256), 256)
        v_cols = pl.ds(pl.multiple_of(HID + n * 256, 256), 256)
        grad = lax.dot_general(
            gall[...], wd[u_cols, :], (((1,), (1,)), ((), ())), preferred_element_type=F32
        )
        u = pre[:, u_cols]
        logistic = jax.nn.sigmoid(u)
        pgb[:ROWS, v_cols] = (grad * u * logistic).astype(BF16)
        pgb[:ROWS, u_cols] = (
            grad * pre[:, v_cols] * logistic * (1.0 + u * (1.0 - logistic))
        ).astype(BF16)

    swap = remote(
        pgb.at[mine], pgb.at[theirs], core_send.at[4], core_recv.at[4], other_core()
    )
    swap.start()
    def token_side(first, end):
        @pl.loop(first, end)
        def _(n):
            @pl.when(n + 1 < WIDTH // 256)
            def _():
                wgu_tile(n + 1).start()

            wgu_tile(n).wait()
            cols = pl.ds(pl.multiple_of(n * 256, 256), 256)
            sig[:, cols] = lax.dot_general(
                pgb[:ROWS, :],
                wgu[lax.rem(n, 2)],
                (((1,), (1,)), ((), ())),
                preferred_element_type=F32,
            ).astype(BF16)

    token_side(0, 6)
    fetch["x"].wait()
    swap.wait_recv()
    weight_in(2)
    near_sent_in = pass_near(1)
    token_side(6, WIDTH // 256)
    sig_state = first_hop(1, (0, 1))
    ends += pass_sum(0, near_sent_out)
    fetch[0].wait()
    swaps[0].wait_recv()
    weight_out(0)
    weight_in(0)
    combine(0, *out_state)
    for ahead in (1, 3):
        weight_in(ahead)
        ends.append(pass_far(1, ahead // 2))
    ends += pass_sum(1, near_sent_in)
    for route in range(2):
        for copy in sig_state[0][route]:
            copy.wait_recv()
    out_finals = pass_partial(0)
    for copy in early:
        copy.wait_send()
    combine(1, [[], []], sig_state[1])
    sig_finals = pass_partial(1)
    for copy in ends[:4]:
        copy.wait_recv()

    @pl.loop(0, 4)
    def _(n):
        part = pl.ds(pl.multiple_of(n * 192, 192), 192)
        total = sum_out[0, part, :].astype(F32)
        total += far_out[0, part, :].astype(F32) + far_out[1, part, :].astype(F32)
        grad_out[part, :] = total.astype(BF16)

    results = []

    def leave(src, dst):
        copy = pltpu.make_async_copy(src, dst, local_sem.at[27 + len(results)])
        copy.start()
        results.append(copy)

    leave(grad_out, down_hbm)
    finish(0, out_finals, layer_out)
    leave(layer_out, layer_hbm)
    finish(1, sig_finals, token_grad)
    leave(token_grad, token_hbm)
    for copy in ends[4:]:
        copy.wait_recv()

    @pl.loop(0, 4)
    def _(n):
        part = pl.ds(pl.multiple_of(n * 128, 128), 128)
        total = sum_in[0, part, :].astype(F32)
        total += far_in[0, part, :].astype(F32) + far_in[1, part, :].astype(F32)
        sum_in[0, part, :] = total.astype(BF16)

    store_in = pltpu.make_async_copy(sum_in.at[0], grad_in, local_sem.at[1])
    store_in.start()
    for copy in sends + [swaps[ahead] for ahead in (1, 3, 0)] + [swap]:
        copy.wait_send()
    for copy in results + [store_in]:
        copy.wait()


def last_kernel(*refs):
    count = len(refs) // 3
    held, sems = refs[2 * count : 3 * count], refs[-1]
    steps = 4
    loads, stores = [], []
    for n in range(count):
        size = refs[n].shape[0] // steps
        for step in range(steps):
            part = pl.ds(step * size, size)
            loads.append(
                pltpu.make_async_copy(refs[n].at[part], held[n].at[part], sems.at[0, n, step])
            )
            stores.append(
                pltpu.make_async_copy(
                    held[n].at[part], refs[count + n].at[part], sems.at[1, n, step]
                )
            )
    for copy in loads:
        copy.start()
    for load, store in zip(loads, stores):
        load.wait()
        store.start()
    for copy in stores:
        copy.wait()


VMEM = pl.BlockSpec(memory_space=pltpu.VMEM)
ANY = pl.BlockSpec(memory_space=pl.ANY)
DMA = pltpu.SemaphoreType.DMA


def dispatch(ids, gates, tokens, cotangent, gate_up, down_weight):
    table = jax.ShapeDtypeStruct((2, 16, 4 * TOK), F32)
    return pl.pallas_call(
        dispatch_kernel,
        out_shape=(
            jax.ShapeDtypeStruct((ROWS, HALF), BF16),
            jax.ShapeDtypeStruct((2 * ROWS, HALF), BF16),
            jax.ShapeDtypeStruct((ROWS, WIDTH), BF16),
            jax.ShapeDtypeStruct((2 * ROWS, HID), BF16),
            jax.ShapeDtypeStruct((ROWS, 2 * HID), F32),
            jax.ShapeDtypeStruct((HID, 512), BF16),
            table,
            table,
        ),
        in_specs=[VMEM] * 4 + [ANY] * 2,
        out_specs=(ANY,) * 6 + (VMEM,) * 2,
        scratch_shapes=[
            pltpu.VMEM((WIDTH, 2 * HID), BF16),
            pltpu.VMEM((HID, WIDTH), BF16),
            pltpu.VMEM((16, 2 * TOK), F32),
            pltpu.VMEM((2, 4, 16, 2 * TOK), F32),
            pltpu.VMEM((2, 2, 4 * TOK, HALF), BF16),
            pltpu.VMEM((2, 2, 3, 4 * MAIN, HALF), BF16),
            pltpu.VMEM((2, 2, 3, 16, CHUNK), BF16),
            pltpu.VMEM((2, 2, 64, CHUNK), BF16),
            pltpu.VMEM((ROWS, WIDTH), BF16),
            pltpu.VMEM((2, 4 * MAIN, HALF), BF16),
            pltpu.VMEM((16, WIDTH), BF16),
            pltpu.VMEM((ROWS, 2 * HID), F32),
            pltpu.VMEM((2 * ROWS, HID), BF16),
            pltpu.VMEM((ROWS, HALF), BF16),
            pltpu.VMEM((2 * ROWS, 512), BF16),
            pltpu.VMEM((HID, 512), BF16),
            DMA((20,)),
            DMA((2, 4)),
            DMA((2, 4)),
            DMA((2, 2, 4)),
            DMA((2, 2, 4)),
            DMA((2, 2, 4, 8)),
            DMA((2, 2, 4, 8)),
            DMA((2, 2, 4)),
            DMA((2, 2, 4)),
            DMA((6,)),
            DMA((6,)),
        ],
        compiler_params=pltpu.CompilerParams(
            collective_id=0, has_side_effects=True, vmem_limit_bytes=60 << 20
        ),
        cost_estimate=pl.CostEstimate(
            flops=20 * 10**9, bytes_accessed=40 * 10**6, transcendentals=10**6
        ),
    )(ids, gates, tokens, cotangent, gate_up, down_weight)


def give_back(out_rows, gate_up, x_rows, g_rows, hidden, pre_act, far_sum, down_weight, rank, share):
    result = jax.ShapeDtypeStruct((TOK, WIDTH), BF16)
    return pl.pallas_call(
        return_kernel,
        out_shape=(
            result,
            result,
            jax.ShapeDtypeStruct((HID, 512), BF16),
            jax.ShapeDtypeStruct((512, 2 * HID), BF16),
        ),
        in_specs=[ANY] * 8 + [VMEM] * 2,
        out_specs=(ANY,) * 4,
        scratch_shapes=[
            pltpu.VMEM((TOK, WIDTH), BF16),
            pltpu.VMEM((TOK, WIDTH), BF16),
            pltpu.VMEM((HID, 512), BF16),
            pltpu.VMEM((2 * ROWS, HALF), BF16),
            pltpu.VMEM((2 * ROWS, HALF), BF16),
            pltpu.VMEM((ROWS, WIDTH), BF16),
            pltpu.VMEM((2 * ROWS, HID), BF16),
            pltpu.VMEM((ROWS, 2 * HID), F32),
            pltpu.VMEM((HID, WIDTH), BF16),
            pltpu.VMEM((2 * ROWS, 2 * HID), BF16),
            pltpu.VMEM((2, 256, 2 * HID), BF16),
            pltpu.VMEM((4, 512, 2 * HID), BF16),
            pltpu.VMEM((4, HID, 512), BF16),
            pltpu.VMEM((2, 256, 2 * HID), BF16),
            pltpu.VMEM((2, HID // 2, 512), BF16),
            pltpu.VMEM((2, 512, 2 * HID), BF16),
            pltpu.VMEM((2, HID, 512), BF16),
            pltpu.VMEM((16, WIDTH), BF16),
            pltpu.VMEM((2, 2, 64, CHUNK), BF16),
            pltpu.VMEM((2, 2, 4, 4 * MAIN, HALF), BF16),
            pltpu.VMEM((2, 2, 64, CHUNK), BF16),
            pltpu.VMEM((2, 2, 4 * TOK, HALF), BF16),
            pltpu.VMEM((2, 2, 3, TOK, HALF), BF16),
            DMA((30,)),
            DMA((2,)),
            DMA((2, 2, 4, 4)),
            DMA((2, 2, 4, 4)),
            DMA((2, 2, 4)),
            DMA((2, 2, 4)),
            DMA((2, 2, 4)),
            DMA((2, 2, 4)),
            DMA((3, 2, 2)),
            DMA((3, 2, 2)),
            DMA((5,)),
            DMA((5,)),
        ],
        compiler_params=pltpu.CompilerParams(
            collective_id=1, has_side_effects=True, vmem_limit_bytes=62 << 20
        ),
        cost_estimate=pl.CostEstimate(
            flops=26 * 10**9, bytes_accessed=100 * 10**6, transcendentals=0
        ),
    )(out_rows, gate_up, x_rows, g_rows, hidden, pre_act, far_sum, down_weight, rank, share)


def last(*results):
    return pl.pallas_call(
        last_kernel,
        out_shape=tuple(jax.ShapeDtypeStruct(a.shape, a.dtype) for a in results),
        in_specs=[ANY] * len(results),
        out_specs=(ANY,) * len(results),
        scratch_shapes=[pltpu.VMEM(a.shape, a.dtype) for a in results]
        + [DMA((2, len(results), 4))],
        cost_estimate=pl.CostEstimate(
            flops=0, bytes_accessed=7 * 10**6, transcendentals=0
        ),
    )(*results)


def per_device(tokens, cotangent, expert_ids, gate_fixed, gate_up, down_weight):
    out_rows, x_rows, g_rows, hidden, pre_act, far_sum, rank, share = dispatch(
        expert_ids.T, gate_fixed.T, tokens, cotangent, gate_up, down_weight
    )
    layer_out, token_grad, grad_out, grad_in = last(
        *give_back(
            out_rows, gate_up, x_rows, g_rows, hidden, pre_act, far_sum, down_weight, rank, share
        )
    )
    return layer_out, token_grad, grad_in[None], grad_out[None]


def solution(mesh):
    rows = P(("ep", "dp"), None)
    return jax.shard_map(
        per_device,
        mesh=mesh,
        in_specs=(rows, rows, rows, rows, P("ep", None, None), P("ep", None, None)),
        out_specs=(rows, rows, P("ep", "dp", None), P("ep", None, "dp")),
        check_vma=False,
    )
```

```python
import functools

import jax
import jax.numpy as jnp
from jax import lax
from jax.experimental import pallas as pl
from jax.experimental.pallas import tpu as pltpu
from jax.sharding import PartitionSpec as P

BF16 = jnp.bfloat16
F32 = jnp.float32
MESH = pl.DeviceIdType.MESH
TOK = 64
WIDTH = 4096
HALF = WIDTH // 2
CHUNK = HALF // 4
HID = 768
MAIN = 32
ROWS = 16 * MAIN + 16
ORDER = (2, 1, 3)


def place():
    ep = lax.axis_index("ep")
    return ep // 4, ep % 4


def peer(axis, distance):
    z, x = place()
    if axis == "z":
        z = lax.rem(z + distance, 4)
    else:
        x = lax.rem(x + distance, 4)
    return {"ep": z * 4 + x, "dp": lax.axis_index("dp")}


def along_y(distance):
    dp = lax.axis_index("dp")
    return {"ep": lax.axis_index("ep"), "dp": lax.rem(dp + 2 * distance, 8)}


def other_core():
    dp = lax.axis_index("dp")
    return {"ep": lax.axis_index("ep"), "dp": dp + 1 - 2 * lax.rem(dp, 2)}


def first_axis(route):
    return ("z", "x")[route]


def second_axis(route):
    return ("x", "z")[route]


def coord(axis):
    z, x = place()
    return z if axis == "z" else x


def expert_at(route, position):
    z, x = place()
    return z * 4 + position if route == 0 else position * 4 + x


def iota(shape, dim):
    return lax.broadcasted_iota(jnp.int32, shape, dim)


def enter(peers):
    barrier = pltpu.get_barrier_semaphore()
    for device in peers:
        pl.semaphore_signal(barrier, 1, device_id=device, device_id_type=MESH)
    pl.semaphore_wait(barrier, len(peers))


def remote(src, dst, send_sem, recv_sem, device):
    return pltpu.make_async_remote_copy(
        src_ref=src,
        dst_ref=dst,
        send_sem=send_sem,
        recv_sem=recv_sem,
        device_id=device,
        device_id_type=MESH,
    )


def pick_row(table, index):
    rows = iota(table.shape, 0)
    return jnp.sum(jnp.where(rows == index, table, 0.0), axis=0, keepdims=True)


def slot_rows(rank, chunk):
    source = iota((1, 4 * TOK), 1) // TOK
    rank = rank.astype(jnp.int32)
    main = jnp.where(rank >= 0, rank + MAIN * source, -1)
    return jnp.where(rank == MAIN, 4 * MAIN + 4 * chunk + source, main)


def overflow_target(route, shape, dim):
    row = iota(shape, dim)
    sender, chunk, source = row // 16, lax.rem(row, 16) // 4, lax.rem(row, 4)
    slot = sender * 4 + source if route == 0 else source * 4 + sender
    return slot, chunk


def dispatch_kernel(
    ids_ref,
    gate_ref,
    tok_ref,
    cot_ref,
    wgu_hbm,
    wd_hbm,
    out_hbm,
    x_hbm,
    g_hbm,
    h_hbm,
    pre_hbm,
    far_hbm,
    rank_out,
    share_out,
    wgu,
    wd,
    meta_own,
    meta,
    gathered,
    staged,
    staged_over,
    over,
    xbuf,
    own,
    own_over,
    pre,
    hid,
    obuf,
    far_rows,
    far_sum,
    local_sem,
    meta_send,
    meta_recv,
    gat_send,
    gat_recv,
    main_send,
    main_recv,
    over_send,
    over_recv,
    core_send,
    core_recv,
):
    z, x = place()
    load_gu = pltpu.make_async_copy(wgu_hbm.at[0], wgu, local_sem.at[0])
    load_d = pltpu.make_async_copy(wd_hbm.at[0], wd, local_sem.at[1])
    load_gu.start()
    load_d.start()

    enter([peer(axis, d) for axis in ("z", "x") for d in ORDER] + [other_core()])

    sends = []
    sources = (tok_ref, cot_ref)

    def block(which, route, position, columns):
        rows = pl.ds(pl.multiple_of(position * TOK, TOK), TOK)
        return gathered.at[which, route, rows, columns]

    def gather_start(which):
        copies = [{}, {}]
        for d in (1, 3):
            for route in range(2):
                here = coord(first_axis(route))
                copy = remote(
                    sources[which].at[:, pl.ds(route * HALF, HALF)],
                    block(which, route, here, pl.ds(0, HALF)),
                    gat_send.at[which, route, d],
                    gat_recv.at[which, route, d],
                    peer(first_axis(route), d),
                )
                copy.start()
                sends.append(copy)
                copies[route][d] = copy
        for route in range(2):
            here = coord(first_axis(route))
            gathered[which, route, pl.ds(pl.multiple_of(here * TOK, TOK), TOK), :] = sources[
                which
            ][:, route * HALF : (route + 1) * HALF]
        return copies

    def gather_pass(which, copies):
        passed = []
        for d in (1, 3):
            for route in range(2):
                copies[route][d].wait_recv()
                axis = first_axis(route)
                behind = lax.rem(coord(axis) + 4 - d, 4)
                columns = pl.ds((d // 2) * (HALF // 2), HALF // 2)
                copy = remote(
                    block(which, route, behind, columns),
                    block(which, route, behind, columns),
                    gat_send.at[which, route, d - 1],
                    gat_recv.at[which, route, d - 1],
                    peer(axis, d),
                )
                copy.start()
                sends.append(copy)
                passed.append(copy)
        return passed

    tok_copies = gather_start(0)

    gates = gate_ref[...].astype(F32)
    share = gates / jnp.sum(gates, axis=0, keepdims=True)
    ids = ids_ref[...]
    expert = iota((16, TOK), 0)
    named = jnp.zeros((16, TOK), F32)
    weight = jnp.zeros((16, TOK), F32)
    for k in range(8):
        hit = ids[k : k + 1, :] == expert
        named += jnp.where(hit, 1.0, 0.0)
        weight += jnp.where(hit, share[k : k + 1, :], 0.0)
    before = jnp.where(iota((TOK, TOK), 0) < iota((TOK, TOK), 1), 1.0, 0.0)
    rank = jnp.dot(named.astype(BF16), before.astype(BF16), preferred_element_type=F32)
    rank = jnp.where(named > 0.0, rank, -1.0)
    meta_own[...] = jnp.concatenate([rank, weight], axis=1)

    meta_recvs = []
    for route in range(2):
        here = coord(first_axis(route))
        for d in ORDER:
            copy = remote(
                meta_own,
                meta.at[route, here],
                meta_send.at[route, d],
                meta_recv.at[route, d],
                peer(first_axis(route), d),
            )
            copy.start()
            sends.append(copy)
            meta_recvs.append(copy)
        meta[route, pl.ds(here, 1)] = meta_own[...][None]

    cot_copies = gather_start(1)
    for copy in meta_recvs:
        copy.wait_recv()
    for route in range(2):
        rank_out[route] = jnp.concatenate([meta[route, s][:, :TOK] for s in range(4)], axis=1)
        share_out[route] = jnp.concatenate([meta[route, s][:, TOK:] for s in range(4)], axis=1)

    buffers = (xbuf, g_hbm)
    postponed = []
    y = lax.axis_index("dp") // 2

    def halves_of(route):
        here = lax.rem(y, 2)
        far = (1 - y // 2) == route
        first = jnp.where(far, here, 1 - here)
        return first, 1 - first


    def select(which, route, d):
        position = lax.rem(coord(second_axis(route)) + d, 4)
        expert = expert_at(route, position)
        rank_row = pick_row(rank_out[route], expert)
        share_row = pick_row(share_out[route], expert)
        here = coord(second_axis(route))
        target = buffers[which]
        total = jnp.zeros((16, CHUNK), F32)
        for c in range(4):
            hit = slot_rows(rank_row, c) == iota((4 * MAIN + 16, 4 * TOK), 0)
            choose = jnp.where(hit, 1.0, 0.0).astype(BF16)
            rows = jnp.dot(
                choose,
                gathered[which, route, :, c * CHUNK : (c + 1) * CHUNK],
                preferred_element_type=F32,
            )
            if which == 1:
                rows = rows * jnp.sum(jnp.where(hit, share_row, 0.0), axis=1, keepdims=True)
            main = rows[: 4 * MAIN].astype(BF16)
            total += rows[4 * MAIN :]
            if which == 1 and not d:
                own[route, :, c * CHUNK : (c + 1) * CHUNK] = main
            elif d:
                staged[which, route, d - 1, :, c * CHUNK : (c + 1) * CHUNK] = main
            else:
                columns = slice(route * HALF + c * CHUNK, route * HALF + (c + 1) * CHUNK)
                if route == 0:
                    target[pl.ds(pl.multiple_of(here * 128, 128), 128), columns] = main
                else:
                    for s in range(4):
                        first = pl.multiple_of((s * 4 + here) * MAIN, MAIN)
                        target[pl.ds(first, MAIN), columns] = main[s * MAIN : (s + 1) * MAIN]
        mine = pl.ds(pl.multiple_of(here * 16, 16), 16)
        if not d:
            over[which, route, mine, :] = total.astype(BF16)
            return []
        staged_over[which, route, d - 1] = total.astype(BF16)
        device = peer(second_axis(route), d)
        size = HALF if which == 0 else HALF // 2
        later = []
        copies = [
            remote(
                staged_over.at[which, route, d - 1],
                over.at[which, route, mine, :],
                over_send.at[which, route, d],
                over_recv.at[which, route, d],
                device,
            )
        ]
        for part in range(HALF // size):
            begin = 0 if which == 0 else pl.multiple_of(halves_of(route)[part] * size, size)
            taken = pl.ds(begin, size)
            columns = pl.ds(pl.multiple_of(route * HALF + begin, size), size)
            found = later if part else copies
            if route == 0:
                found.append(
                    remote(
                        staged.at[which, route, d - 1, :, taken],
                        target.at[pl.ds(pl.multiple_of(here * 128, 128), 128), columns],
                        main_send.at[which, route, d, 4 * part],
                        main_recv.at[which, route, d, 4 * part],
                        device,
                    )
                )
            else:
                for s in range(4):
                    first = pl.multiple_of((s * 4 + here) * MAIN, MAIN)
                    found.append(
                        remote(
                            staged.at[which, route, d - 1, pl.ds(s * MAIN, MAIN), taken],
                            target.at[pl.ds(first, MAIN), columns],
                            main_send.at[which, route, d, 4 * part + s],
                            main_recv.at[which, route, d, 4 * part + s],
                            device,
                        )
                    )
        for copy in copies:
            copy.start()
        sends.extend(copies)
        postponed.extend(later)
        return copies

    def second_hop(which, passed):
        arrivals = []
        for copy in passed:
            copy.wait_recv()
        for d in ORDER:
            for route in range(2):
                arrivals.extend(select(which, route, d))
        return arrivals

    def finish(which, arrivals):
        for copy in arrivals:
            copy.wait_recv()
        for route in range(2):
            slot, chunk = overflow_target(route, (16, 64), 1)
            for c in range(4):
                spread = jnp.where((slot == iota((16, 64), 0)) & (chunk == c), 1.0, 0.0)
                first = route * HALF + c * CHUNK
                tail = jnp.dot(
                    spread.astype(BF16), over[which, route], preferred_element_type=F32
                ).astype(BF16)
                if which == 0:
                    xbuf[16 * MAIN : ROWS, first : first + CHUNK] = tail
                else:
                    own_over[:, first : first + CHUNK] = tail

    tok_passed = gather_pass(0, tok_copies)
    cot_passed = gather_pass(1, cot_copies)
    x_arrivals = second_hop(0, tok_passed)
    g_arrivals = second_hop(1, cot_passed)
    for copy in postponed:
        copy.start()
    sends.extend(postponed)
    for which in range(2):
        for route in range(2):
            select(which, route, 0)
    load_gu.wait()
    load_d.wait()

    core = lax.rem(lax.axis_index("dp"), 2)
    stores = []
    shared = []

    def store(src, dst):
        copy = pltpu.make_async_copy(src, dst, local_sem.at[2 + len(stores)])
        copy.start()
        stores.append(copy)
        return copy

    def share(src, dst):
        slot = len(shared)
        copy = remote(src, dst, core_send.at[slot], core_recv.at[slot], other_core())
        copy.start()
        shared.append(copy)
        return copy

    before_own = len(stores)
    for route in range(2):
        here = coord(second_axis(route))
        columns = pl.ds(route * HALF, HALF)
        if route == 0:
            first = pl.multiple_of(here * 128, 128)
            store(own.at[route], g_hbm.at[pl.ds(first, 128), columns])
        else:
            for s in range(4):
                first = pl.multiple_of((s * 4 + here) * MAIN, MAIN)
                store(
                    own.at[route, pl.ds(s * MAIN, MAIN), :],
                    g_hbm.at[pl.ds(first, MAIN), columns],
                )

    own_stores = stores[before_own:]
    mine, theirs = pl.ds(0, ROWS), pl.ds(ROWS, ROWS)

    def split(src, dst):
        for block in range(4):
            there = pl.ds(block * 512, 512)
            keep = pl.ds(pl.multiple_of((2 * block + core) * 512, 512), 512)
            give = pl.ds(pl.multiple_of((2 * block + 1 - core) * 512, 512), 512)
            share(src.at[:, give], dst.at[theirs, there])
            store(src.at[:, keep], dst.at[mine, there])

    finish(0, x_arrivals)
    split(xbuf, x_hbm)

    @pl.loop(0, 3)
    def _(n):
        u_cols = pl.ds(pl.multiple_of(n * 256, 256), 256)
        v_cols = pl.ds(pl.multiple_of(HID + n * 256, 256), 256)
        u = jnp.dot(xbuf[...], wgu[:, u_cols], preferred_element_type=F32)
        pre[:, u_cols] = u
        v = jnp.dot(xbuf[...], wgu[:, v_cols], preferred_element_type=F32)
        pre[:, v_cols] = v
        hid[:ROWS, u_cols] = (pre[:, u_cols] * jax.nn.sigmoid(pre[:, u_cols]) * v).astype(BF16)

    hid_share = share(hid.at[mine], hid.at[theirs])
    store(pre, pre_hbm)
    finish(1, g_arrivals)
    own_stores.append(store(own_over, g_hbm.at[pl.ds(16 * MAIN, 16), :]))
    for copy in own_stores:
        copy.wait()

    def far_columns(of_core):
        return pl.ds(pl.multiple_of((2 * lax.rem(y + 2, 4) + of_core) * 512, 512), 512)

    far_load = store(g_hbm.at[:, far_columns(core)], far_rows.at[mine])
    far_share = share(g_hbm.at[:, far_columns(1 - core)], far_rows.at[theirs])

    @pl.loop(0, HALF // 256)
    def _(n):
        cols = pl.ds(pl.multiple_of(n * 256, 256), 256)
        obuf[:, cols] = jnp.dot(
            hid[:ROWS, :], wd[:, cols], preferred_element_type=F32
        ).astype(BF16)

    store(obuf, out_hbm)
    hid_share.wait_recv()
    store(hid, h_hbm)
    far_load.wait()
    far_share.wait_recv()

    @pl.loop(0, 3)
    def _(n):
        piece = pl.ds(pl.multiple_of(n * 256, 256), 256)
        far_sum[piece, :] = lax.dot_general(
            hid[:, piece],
            far_rows[...],
            (((0,), (0,)), ((), ())),
            preferred_element_type=F32,
        ).astype(BF16)

    store(far_sum, far_hbm)
    for copy in postponed:
        copy.wait_recv()
    for copy in stores:
        if copy is not far_load and all(copy is not other for other in own_stores):
            copy.wait()
    for copy in shared:
        if copy is hid_share or copy is far_share:
            copy.wait_send()
        else:
            copy.wait()
    for copy in sends:
        copy.wait_send()


def return_kernel(
    out_hbm,
    wgu_hbm,
    x_hbm,
    g_hbm,
    h_hbm,
    pre_hbm,
    far_hbm,
    wd_hbm,
    rank_ref,
    share_ref,
    layer_hbm,
    token_hbm,
    down_hbm,
    grad_in,
    layer_out,
    token_grad,
    grad_out,
    xb,
    gb,
    gall,
    hb,
    pre,
    wd,
    pgb,
    wgu,
    sum_in,
    sum_out,
    near_in,
    near_out,
    far_in,
    far_out,
    tail,
    compact,
    rows,
    rows_over,
    partial,
    final,
    local_sem,
    wgu_sem,
    main_send,
    main_recv,
    over_send,
    over_recv,
    part_send,
    part_recv,
    dp_send,
    dp_recv,
    core_send,
    core_recv,
):
    z, x = place()
    y = lax.axis_index("dp") // 2
    core = lax.rem(lax.axis_index("dp"), 2)
    sig = gall
    mine, theirs = pl.ds(0, ROWS), pl.ds(ROWS, ROWS)
    fetch = {}

    def load(name, src, dst):
        copy = pltpu.make_async_copy(src, dst, local_sem.at[18 + len(fetch)])
        copy.start()
        fetch[name] = copy

    def columns_of(ahead, of_core):
        first = (2 * lax.rem(y + ahead, 4) + of_core) * 512
        return pl.ds(pl.multiple_of(first, 512), 512)

    def place_of(ahead):
        return pl.ds(pl.multiple_of(lax.rem(y + ahead, 4) * 512, 512), 512)

    load("h", h_hbm, hb)
    load("d", wd_hbm.at[0], wd)
    for ahead in (1, 3, 0):
        load(ahead, g_hbm.at[:, columns_of(ahead, core)], gb.at[mine, place_of(ahead)])
    load_tail = pltpu.make_async_copy(
        out_hbm.at[pl.ds(16 * MAIN, 16), :], tail.at[:, pl.ds(0, HALF)], local_sem.at[0]
    )
    load_tail.start()

    def wgu_tile(n):
        rows = pl.ds(pl.multiple_of(n * 256, 256), 256)
        slot = lax.rem(n, 2)
        return pltpu.make_async_copy(wgu_hbm.at[0, rows, :], wgu.at[slot], wgu_sem.at[slot])

    wgu_tile(0).start()
    enter(
        [peer(axis, d) for axis in ("z", "x") for d in ORDER]
        + [along_y(d) for d in (1, 3)]
        + [other_core()]
    )
    sends = []
    def pieces(which, route, position, slot):
        columns = pl.ds(route * HALF, HALF)
        if route == 0:
            rows_there = pl.ds(pl.multiple_of(position * 128, 128), 128)
            if which == 0:
                src = out_hbm.at[rows_there]
            else:
                src = sig.at[rows_there, columns]
            return [(src, rows.at[which, route, slot])]
        found = []
        for s in range(4):
            dst = rows.at[which, route, slot, pl.ds(s * MAIN, MAIN), :]
            if which == 0:
                first = pl.multiple_of((s % 2) * 128 + position * MAIN, MAIN)
                found.append((partial.at[1, s // 2, pl.ds(first, MAIN), :], dst))
            else:
                first = pl.multiple_of((s * 4 + position) * MAIN, MAIN)
                found.append((sig.at[pl.ds(first, MAIN), columns], dst))
        return found

    early = []

    def first_hop(which, routes):
        arrivals = [[], []]
        for d in ORDER:
            for route in routes:
                here = coord(second_axis(route))
                there = lax.rem(here + d, 4)
                for s, (src, dst) in enumerate(pieces(which, route, there, here)):
                    copy = remote(
                        src,
                        dst,
                        main_send.at[which, route, d, s],
                        main_recv.at[which, route, d, s],
                        peer(second_axis(route), d),
                    )
                    copy.start()
                    (early if which == 0 and route == 1 else sends).append(copy)
                    arrivals[route].append(copy)
        owns = [[], []]
        for route in routes:
            here = coord(second_axis(route))
            for s, (src, dst) in enumerate(pieces(which, route, here, here)):
                copy = pltpu.make_async_copy(src, dst, local_sem.at[2 + which * 8 + route * 4 + s])
                copy.start()
                owns[route].append(copy)
        if which == 0 and routes[0] == 0:
            load_tail.wait()
        last = tail if which == 0 else sig.at[pl.ds(16 * MAIN, 16), :]
        for route in routes:
            here = coord(second_axis(route))
            slot, chunk = overflow_target(route, (64, 16), 0)
            total = jnp.zeros((64, CHUNK), F32)
            for c in range(4):
                take = jnp.where((slot == iota((64, 16), 1)) & (chunk == c), 1.0, 0.0)
                first = route * HALF + c * CHUNK
                total += jnp.dot(
                    take.astype(BF16),
                    last[:, first : first + CHUNK],
                    preferred_element_type=F32,
                )
            compact[which, route] = total.astype(BF16)
            mine = pl.ds(pl.multiple_of(here * 16, 16), 16)
            rows_over[which, route, mine, :] = compact[which, route, mine, :]
            for d in ORDER:
                there = lax.rem(here + d, 4)
                copy = remote(
                    compact.at[which, route, pl.ds(pl.multiple_of(there * 16, 16), 16), :],
                    rows_over.at[which, route, mine, :],
                    over_send.at[which, route, d],
                    over_recv.at[which, route, d],
                    peer(second_axis(route), d),
                )
                copy.start()
                sends.append(copy)
                arrivals[route].append(copy)
        return arrivals, owns

    def combine(which, arrivals, owns):
        for route in range(2):
            for copy in arrivals[route]:
                copy.wait_recv()
            for copy in owns[route]:
                copy.wait()
            ranks = [pick_row(rank_ref[route], expert_at(route, p)) for p in range(4)]
            shares = [pick_row(share_ref[route], expert_at(route, p)) for p in range(4)]
            for c in range(4):
                main, rest = [], []
                for p in range(4):
                    hit = slot_rows(ranks[p], c) == iota((4 * MAIN + 16, 4 * TOK), 0)
                    value = shares[p] if which == 0 else 1.0
                    spread = jnp.where(hit, value, 0.0)
                    main.append(spread[: 4 * MAIN])
                    rest.append(spread[4 * MAIN :])
                main = jnp.concatenate(main, axis=0).astype(BF16)
                rest = jnp.concatenate(rest, axis=0).astype(BF16)
                columns = slice(c * CHUNK, (c + 1) * CHUNK)
                along = (((0,), (0,)), ((), ()))
                total = lax.dot_general(
                    main,
                    rows[which, route, :, :, columns].reshape(16 * MAIN, CHUNK),
                    along,
                    preferred_element_type=F32,
                ) + lax.dot_general(
                    rest, rows_over[which, route], along, preferred_element_type=F32
                )
                partial[which, route, :, columns] = total.astype(BF16)

    def pass_partial(which):
        finals = []
        for d in ORDER:
            for route in range(2):
                here = coord(first_axis(route))
                there = lax.rem(here + d, 4)
                copy = remote(
                    partial.at[which, route, pl.ds(pl.multiple_of(there * TOK, TOK), TOK), :],
                    final.at[which, route, d - 1],
                    part_send.at[which, route, d],
                    part_recv.at[which, route, d],
                    peer(first_axis(route), d),
                )
                copy.start()
                sends.append(copy)
                finals.append(copy)
        return finals

    def finish(which, finals, result):
        for copy in finals:
            copy.wait_recv()
        for route in range(2):
            here = coord(first_axis(route))
            own = partial[which, route, pl.ds(pl.multiple_of(here * TOK, TOK), TOK), :]
            total = own.astype(F32)
            for d in range(3):
                total += final[which, route, d].astype(F32)
            result[:, route * HALF : (route + 1) * HALF] = total.astype(BF16)

    along = (((0,), (0,)), ((), ()))

    def weight_out(ahead):
        cols = place_of(ahead)

        @pl.loop(0, 3)
        def _(n):
            piece = pl.ds(pl.multiple_of(n * 256, 256), 256)
            sum_out[ahead, piece, :] = lax.dot_general(
                hb[:, piece], gb[:, cols], along, preferred_element_type=F32
            ).astype(BF16)

    def weight_in(ahead):
        first = lax.rem(y + ahead, 4) * 512

        @pl.loop(0, 2)
        def _(n):
            piece = pl.ds(pl.multiple_of(n * 256, 256), 256)
            part = pl.ds(pl.multiple_of(first + n * 256, 256), 256)
            sum_in[ahead, piece, :] = lax.dot_general(
                xb[:, part], pgb[...], along, preferred_element_type=F32
            ).astype(BF16)

    half_in = (pl.ds(0, 256), pl.ds(256, 256))
    half_out = (pl.ds(0, HID // 2), pl.ds(HID // 2, HID // 2))

    sums = (sum_out, sum_in)
    nears = (near_out, near_in)
    fars = (far_out, far_in)
    halves = (half_out, half_in)

    def pass_half(kind, ahead, half, side, dst, slot):
        src = far_hbm.at[halves[kind][half], :]
        if kind or ahead != 2:
            src = sums[kind].at[ahead, halves[kind][half], :]
        copy = remote(
            src,
            dst,
            dp_send.at[slot, side, kind],
            dp_recv.at[slot, side, kind],
            along_y((1, 3)[side]),
        )
        copy.start()
        sends.append(copy)
        return copy

    def pass_near(kind):
        return [pass_half(kind, 2, side, side, nears[kind].at[side], 0) for side in range(2)]

    def pass_far(kind, side):
        ahead, half = (1, 3)[side], 1 - side
        return pass_half(kind, ahead, half, side, fars[kind].at[side, halves[kind][half], :], 1)

    def pass_sum(kind, near):
        found = []
        for side, ahead in ((0, 1), (1, 3)):
            near[side].wait_recv()
            part = halves[kind][side]
            sums[kind][ahead, part, :] = (
                sums[kind][ahead, part, :].astype(F32) + nears[kind][side].astype(F32)
            ).astype(BF16)
            found.append(
                pass_half(kind, ahead, side, side, fars[kind].at[side, part, :], 2)
            )
        return found

    near_sent_out = pass_near(0)
    swaps = {}
    for ahead in (1, 3, 0):
        swaps[ahead] = remote(
            g_hbm.at[:, columns_of(ahead, 1 - core)],
            gb.at[theirs, place_of(ahead)],
            core_send.at[ahead],
            core_recv.at[ahead],
            other_core(),
        )
        swaps[ahead].start()

    out_state = first_hop(0, (0,))
    ends = []
    fetch["h"].wait()
    fetch["d"].wait()
    load("g", g_hbm, gall)
    load("pre", pre_hbm, pre)
    load("x", x_hbm, xb)

    @pl.loop(0, HALF // 256)
    def _(n):
        cols = pl.ds(pl.multiple_of(n * 256, 256), 256)
        there = pl.ds(pl.multiple_of(HALF + n * 256, 256), 256)
        tile = jnp.dot(hb[:ROWS, :], wd[:, there], preferred_element_type=F32).astype(BF16)
        partial[1, 0, :, cols] = tile[:256]
        partial[1, 1, :, cols] = tile[256:512]
        tail[:, there] = tile[512:]

    for old, new in zip(out_state, first_hop(0, (1,))):
        old[1] = new[1]
    for ahead in (1, 3):
        fetch[ahead].wait()
        swaps[ahead].wait_recv()
        weight_out(ahead)
        ends.append(pass_far(0, ahead // 2))
    fetch["g"].wait()
    fetch["pre"].wait()

    @pl.loop(0, 3)
    def _(n):
        u_cols = pl.ds(pl.multiple_of(n * 256, 256), 256)
        v_cols = pl.ds(pl.multiple_of(HID + n * 256, 256), 256)
        grad = lax.dot_general(
            gall[...], wd[u_cols, :], (((1,), (1,)), ((), ())), preferred_element_type=F32
        )
        u = pre[:, u_cols]
        logistic = jax.nn.sigmoid(u)
        pgb[:ROWS, v_cols] = (grad * u * logistic).astype(BF16)
        pgb[:ROWS, u_cols] = (
            grad * pre[:, v_cols] * logistic * (1.0 + u * (1.0 - logistic))
        ).astype(BF16)

    swap = remote(
        pgb.at[mine], pgb.at[theirs], core_send.at[4], core_recv.at[4], other_core()
    )
    swap.start()
    ends += pass_sum(0, near_sent_out)
    def token_side(first, end):
        @pl.loop(first, end)
        def _(n):
            @pl.when(n + 1 < WIDTH // 256)
            def _():
                wgu_tile(n + 1).start()

            wgu_tile(n).wait()
            cols = pl.ds(pl.multiple_of(n * 256, 256), 256)
            sig[:, cols] = lax.dot_general(
                pgb[:ROWS, :],
                wgu[lax.rem(n, 2)],
                (((1,), (1,)), ((), ())),
                preferred_element_type=F32,
            ).astype(BF16)

    token_side(0, 6)
    fetch["x"].wait()
    swap.wait_recv()
    weight_in(2)
    near_sent_in = pass_near(1)
    token_side(6, WIDTH // 256)
    sig_state = first_hop(1, (0, 1))
    fetch[0].wait()
    swaps[0].wait_recv()
    weight_out(0)
    weight_in(0)
    combine(0, *out_state)
    out_finals = pass_partial(0)
    for ahead in (1, 3):
        weight_in(ahead)
        ends.append(pass_far(1, ahead // 2))
    ends += pass_sum(1, near_sent_in)
    for route in range(2):
        for copy in sig_state[0][route]:
            copy.wait_recv()
    for copy in early:
        copy.wait_send()
    combine(1, [[], []], sig_state[1])
    sig_finals = pass_partial(1)
    for copy in ends[:4]:
        copy.wait_recv()

    @pl.loop(0, 4)
    def _(n):
        part = pl.ds(pl.multiple_of(n * 192, 192), 192)
        total = sum_out[0, part, :].astype(F32)
        total += far_out[0, part, :].astype(F32) + far_out[1, part, :].astype(F32)
        grad_out[part, :] = total.astype(BF16)

    results = []

    def leave(src, dst):
        copy = pltpu.make_async_copy(src, dst, local_sem.at[27 + len(results)])
        copy.start()
        results.append(copy)

    leave(grad_out, down_hbm)
    finish(0, out_finals, layer_out)
    leave(layer_out, layer_hbm)
    finish(1, sig_finals, token_grad)
    leave(token_grad, token_hbm)
    for copy in ends[4:]:
        copy.wait_recv()
    for n in range(4):
        part = pl.ds(n * 128, 128)
        total = sum_in[0, part, :].astype(F32)
        total += far_in[0, part, :].astype(F32) + far_in[1, part, :].astype(F32)
        sum_in[0, part, :] = total.astype(BF16)
        leave(sum_in.at[0, part, :], grad_in.at[part, :])

    for copy in sends + [swaps[ahead] for ahead in (1, 3, 0)] + [swap]:
        copy.wait_send()
    for copy in results:
        copy.wait()


def last_kernel(*refs):
    count = len(refs) // 3
    held, sems = refs[2 * count : 3 * count], refs[-1]
    steps = 4
    loads, stores = [], []
    for n in range(count):
        size = refs[n].shape[0] // steps
        for step in range(steps):
            part = pl.ds(step * size, size)
            loads.append(
                pltpu.make_async_copy(refs[n].at[part], held[n].at[part], sems.at[0, n, step])
            )
            stores.append(
                pltpu.make_async_copy(
                    held[n].at[part], refs[count + n].at[part], sems.at[1, n, step]
                )
            )
    for copy in loads:
        copy.start()
    for load, store in zip(loads, stores):
        load.wait()
        store.start()
    for copy in stores:
        copy.wait()


VMEM = pl.BlockSpec(memory_space=pltpu.VMEM)
ANY = pl.BlockSpec(memory_space=pl.ANY)
DMA = pltpu.SemaphoreType.DMA


def dispatch(ids, gates, tokens, cotangent, gate_up, down_weight):
    table = jax.ShapeDtypeStruct((2, 16, 4 * TOK), F32)
    return pl.pallas_call(
        dispatch_kernel,
        out_shape=(
            jax.ShapeDtypeStruct((ROWS, HALF), BF16),
            jax.ShapeDtypeStruct((2 * ROWS, HALF), BF16),
            jax.ShapeDtypeStruct((ROWS, WIDTH), BF16),
            jax.ShapeDtypeStruct((2 * ROWS, HID), BF16),
            jax.ShapeDtypeStruct((ROWS, 2 * HID), F32),
            jax.ShapeDtypeStruct((HID, 512), BF16),
            table,
            table,
        ),
        in_specs=[VMEM] * 4 + [ANY] * 2,
        out_specs=(ANY,) * 6 + (VMEM,) * 2,
        scratch_shapes=[
            pltpu.VMEM((WIDTH, 2 * HID), BF16),
            pltpu.VMEM((HID, WIDTH), BF16),
            pltpu.VMEM((16, 2 * TOK), F32),
            pltpu.VMEM((2, 4, 16, 2 * TOK), F32),
            pltpu.VMEM((2, 2, 4 * TOK, HALF), BF16),
            pltpu.VMEM((2, 2, 3, 4 * MAIN, HALF), BF16),
            pltpu.VMEM((2, 2, 3, 16, CHUNK), BF16),
            pltpu.VMEM((2, 2, 64, CHUNK), BF16),
            pltpu.VMEM((ROWS, WIDTH), BF16),
            pltpu.VMEM((2, 4 * MAIN, HALF), BF16),
            pltpu.VMEM((16, WIDTH), BF16),
            pltpu.VMEM((ROWS, 2 * HID), F32),
            pltpu.VMEM((2 * ROWS, HID), BF16),
            pltpu.VMEM((ROWS, HALF), BF16),
            pltpu.VMEM((2 * ROWS, 512), BF16),
            pltpu.VMEM((HID, 512), BF16),
            DMA((20,)),
            DMA((2, 4)),
            DMA((2, 4)),
            DMA((2, 2, 4)),
            DMA((2, 2, 4)),
            DMA((2, 2, 4, 8)),
            DMA((2, 2, 4, 8)),
            DMA((2, 2, 4)),
            DMA((2, 2, 4)),
            DMA((6,)),
            DMA((6,)),
        ],
        compiler_params=pltpu.CompilerParams(
            collective_id=0, has_side_effects=True, vmem_limit_bytes=60 << 20
        ),
        cost_estimate=pl.CostEstimate(
            flops=20 * 10**9, bytes_accessed=40 * 10**6, transcendentals=10**6
        ),
    )(ids, gates, tokens, cotangent, gate_up, down_weight)


def give_back(out_rows, gate_up, x_rows, g_rows, hidden, pre_act, far_sum, down_weight, rank, share):
    result = jax.ShapeDtypeStruct((TOK, WIDTH), BF16)
    return pl.pallas_call(
        return_kernel,
        out_shape=(
            result,
            result,
            jax.ShapeDtypeStruct((HID, 512), BF16),
            jax.ShapeDtypeStruct((512, 2 * HID), BF16),
        ),
        in_specs=[ANY] * 8 + [VMEM] * 2,
        out_specs=(ANY,) * 4,
        scratch_shapes=[
            pltpu.VMEM((TOK, WIDTH), BF16),
            pltpu.VMEM((TOK, WIDTH), BF16),
            pltpu.VMEM((HID, 512), BF16),
            pltpu.VMEM((2 * ROWS, HALF), BF16),
            pltpu.VMEM((2 * ROWS, HALF), BF16),
            pltpu.VMEM((ROWS, WIDTH), BF16),
            pltpu.VMEM((2 * ROWS, HID), BF16),
            pltpu.VMEM((ROWS, 2 * HID), F32),
            pltpu.VMEM((HID, WIDTH), BF16),
            pltpu.VMEM((2 * ROWS, 2 * HID), BF16),
            pltpu.VMEM((2, 256, 2 * HID), BF16),
            pltpu.VMEM((4, 512, 2 * HID), BF16),
            pltpu.VMEM((4, HID, 512), BF16),
            pltpu.VMEM((2, 256, 2 * HID), BF16),
            pltpu.VMEM((2, HID // 2, 512), BF16),
            pltpu.VMEM((2, 512, 2 * HID), BF16),
            pltpu.VMEM((2, HID, 512), BF16),
            pltpu.VMEM((16, WIDTH), BF16),
            pltpu.VMEM((2, 2, 64, CHUNK), BF16),
            pltpu.VMEM((2, 2, 4, 4 * MAIN, HALF), BF16),
            pltpu.VMEM((2, 2, 64, CHUNK), BF16),
            pltpu.VMEM((2, 2, 4 * TOK, HALF), BF16),
            pltpu.VMEM((2, 2, 3, TOK, HALF), BF16),
            DMA((34,)),
            DMA((2,)),
            DMA((2, 2, 4, 4)),
            DMA((2, 2, 4, 4)),
            DMA((2, 2, 4)),
            DMA((2, 2, 4)),
            DMA((2, 2, 4)),
            DMA((2, 2, 4)),
            DMA((3, 2, 2)),
            DMA((3, 2, 2)),
            DMA((5,)),
            DMA((5,)),
        ],
        compiler_params=pltpu.CompilerParams(
            collective_id=1, has_side_effects=True, vmem_limit_bytes=62 << 20
        ),
        cost_estimate=pl.CostEstimate(
            flops=26 * 10**9, bytes_accessed=100 * 10**6, transcendentals=0
        ),
    )(out_rows, gate_up, x_rows, g_rows, hidden, pre_act, far_sum, down_weight, rank, share)


def last(*results):
    return pl.pallas_call(
        last_kernel,
        out_shape=tuple(jax.ShapeDtypeStruct(a.shape, a.dtype) for a in results),
        in_specs=[ANY] * len(results),
        out_specs=(ANY,) * len(results),
        scratch_shapes=[pltpu.VMEM(a.shape, a.dtype) for a in results]
        + [DMA((2, len(results), 4))],
        cost_estimate=pl.CostEstimate(
            flops=0, bytes_accessed=7 * 10**6, transcendentals=0
        ),
    )(*results)


def per_device(tokens, cotangent, expert_ids, gate_fixed, gate_up, down_weight):
    out_rows, x_rows, g_rows, hidden, pre_act, far_sum, rank, share = dispatch(
        expert_ids.T, gate_fixed.T, tokens, cotangent, gate_up, down_weight
    )
    layer_out, token_grad, grad_out, grad_in = last(
        *give_back(
            out_rows, gate_up, x_rows, g_rows, hidden, pre_act, far_sum, down_weight, rank, share
        )
    )
    return layer_out, token_grad, grad_in[None], grad_out[None]


def solution(mesh):
    rows = P(("ep", "dp"), None)
    return jax.shard_map(
        per_device,
        mesh=mesh,
        in_specs=(rows, rows, rows, rows, P("ep", None, None), P("ep", None, None)),
        out_specs=(rows, rows, P("ep", "dp", None), P("ep", None, "dp")),
        check_vma=False,
    )
```

```python
import functools

import jax
import jax.numpy as jnp
from jax import lax
from jax.experimental import pallas as pl
from jax.experimental.pallas import tpu as pltpu
from jax.sharding import PartitionSpec as P

BF16 = jnp.bfloat16
F32 = jnp.float32
MESH = pl.DeviceIdType.MESH
TOK = 64
WIDTH = 4096
HALF = WIDTH // 2
CHUNK = HALF // 4
HID = 768
MAIN = 32
ROWS = 16 * MAIN + 16
ORDER = (2, 1, 3)


def place():
    ep = lax.axis_index("ep")
    return ep // 4, ep % 4


def peer(axis, distance):
    z, x = place()
    if axis == "z":
        z = lax.rem(z + distance, 4)
    else:
        x = lax.rem(x + distance, 4)
    return {"ep": z * 4 + x, "dp": lax.axis_index("dp")}


def along_y(distance):
    dp = lax.axis_index("dp")
    return {"ep": lax.axis_index("ep"), "dp": lax.rem(dp + 2 * distance, 8)}


def other_core():
    dp = lax.axis_index("dp")
    return {"ep": lax.axis_index("ep"), "dp": dp + 1 - 2 * lax.rem(dp, 2)}


def first_axis(route):
    return ("z", "x")[route]


def second_axis(route):
    return ("x", "z")[route]


def coord(axis):
    z, x = place()
    return z if axis == "z" else x


def expert_at(route, position):
    z, x = place()
    return z * 4 + position if route == 0 else position * 4 + x


def iota(shape, dim):
    return lax.broadcasted_iota(jnp.int32, shape, dim)


def enter(peers):
    barrier = pltpu.get_barrier_semaphore()
    for device in peers:
        pl.semaphore_signal(barrier, 1, device_id=device, device_id_type=MESH)
    pl.semaphore_wait(barrier, len(peers))


def remote(src, dst, send_sem, recv_sem, device):
    return pltpu.make_async_remote_copy(
        src_ref=src,
        dst_ref=dst,
        send_sem=send_sem,
        recv_sem=recv_sem,
        device_id=device,
        device_id_type=MESH,
    )


def pick_row(table, index):
    rows = iota(table.shape, 0)
    return jnp.sum(jnp.where(rows == index, table, 0.0), axis=0, keepdims=True)


def slot_rows(rank, chunk):
    source = iota((1, 4 * TOK), 1) // TOK
    rank = rank.astype(jnp.int32)
    main = jnp.where(rank >= 0, rank + MAIN * source, -1)
    return jnp.where(rank == MAIN, 4 * MAIN + 4 * chunk + source, main)


def overflow_target(route, shape, dim):
    row = iota(shape, dim)
    sender, chunk, source = row // 16, lax.rem(row, 16) // 4, lax.rem(row, 4)
    slot = sender * 4 + source if route == 0 else source * 4 + sender
    return slot, chunk


def dispatch_kernel(
    ids_ref,
    gate_ref,
    tok_ref,
    cot_ref,
    wgu_hbm,
    wd_hbm,
    out_hbm,
    x_hbm,
    g_hbm,
    h_hbm,
    pre_hbm,
    far_hbm,
    rank_out,
    share_out,
    wgu,
    wd,
    meta_own,
    meta,
    gathered,
    staged,
    staged_over,
    over,
    xbuf,
    own,
    own_over,
    pre,
    hid,
    obuf,
    far_rows,
    far_sum,
    local_sem,
    meta_send,
    meta_recv,
    gat_send,
    gat_recv,
    main_send,
    main_recv,
    over_send,
    over_recv,
    core_send,
    core_recv,
):
    z, x = place()
    load_gu = pltpu.make_async_copy(wgu_hbm.at[0], wgu, local_sem.at[0])
    load_d = pltpu.make_async_copy(wd_hbm.at[0], wd, local_sem.at[1])
    load_gu.start()
    load_d.start()

    enter([peer(axis, d) for axis in ("z", "x") for d in ORDER] + [other_core()])

    sends = []
    sources = (tok_ref, cot_ref)

    def block(which, route, position, columns):
        rows = pl.ds(pl.multiple_of(position * TOK, TOK), TOK)
        return gathered.at[which, route, rows, columns]

    def gather_start(which):
        copies = [{}, {}]
        for d in (1, 3):
            for route in range(2):
                here = coord(first_axis(route))
                copy = remote(
                    sources[which].at[:, pl.ds(route * HALF, HALF)],
                    block(which, route, here, pl.ds(0, HALF)),
                    gat_send.at[which, route, d],
                    gat_recv.at[which, route, d],
                    peer(first_axis(route), d),
                )
                copy.start()
                sends.append(copy)
                copies[route][d] = copy
        for route in range(2):
            here = coord(first_axis(route))
            gathered[which, route, pl.ds(pl.multiple_of(here * TOK, TOK), TOK), :] = sources[
                which
            ][:, route * HALF : (route + 1) * HALF]
        return copies

    def gather_pass(which, copies):
        passed = []
        for d in (1, 3):
            for route in range(2):
                copies[route][d].wait_recv()
                axis = first_axis(route)
                behind = lax.rem(coord(axis) + 4 - d, 4)
                columns = pl.ds((d // 2) * (HALF // 2), HALF // 2)
                copy = remote(
                    block(which, route, behind, columns),
                    block(which, route, behind, columns),
                    gat_send.at[which, route, d - 1],
                    gat_recv.at[which, route, d - 1],
                    peer(axis, d),
                )
                copy.start()
                sends.append(copy)
                passed.append(copy)
        return passed

    tok_copies = gather_start(0)

    gates = gate_ref[...].astype(F32)
    share = gates / jnp.sum(gates, axis=0, keepdims=True)
    ids = ids_ref[...]
    expert = iota((16, TOK), 0)
    named = jnp.zeros((16, TOK), F32)
    weight = jnp.zeros((16, TOK), F32)
    for k in range(8):
        hit = ids[k : k + 1, :] == expert
        named += jnp.where(hit, 1.0, 0.0)
        weight += jnp.where(hit, share[k : k + 1, :], 0.0)
    before = jnp.where(iota((TOK, TOK), 0) < iota((TOK, TOK), 1), 1.0, 0.0)
    rank = jnp.dot(named.astype(BF16), before.astype(BF16), preferred_element_type=F32)
    rank = jnp.where(named > 0.0, rank, -1.0)
    meta_own[...] = jnp.concatenate([rank, weight], axis=1)

    meta_recvs = []
    for route in range(2):
        here = coord(first_axis(route))
        for d in ORDER:
            copy = remote(
                meta_own,
                meta.at[route, here],
                meta_send.at[route, d],
                meta_recv.at[route, d],
                peer(first_axis(route), d),
            )
            copy.start()
            sends.append(copy)
            meta_recvs.append(copy)
        meta[route, pl.ds(here, 1)] = meta_own[...][None]

    cot_copies = gather_start(1)
    for copy in meta_recvs:
        copy.wait_recv()
    for route in range(2):
        rank_out[route] = jnp.concatenate([meta[route, s][:, :TOK] for s in range(4)], axis=1)
        share_out[route] = jnp.concatenate([meta[route, s][:, TOK:] for s in range(4)], axis=1)

    buffers = (xbuf, g_hbm)
    postponed = []
    y = lax.axis_index("dp") // 2

    def halves_of(route):
        here = lax.rem(y, 2)
        far = (1 - y // 2) == route
        first = jnp.where(far, here, 1 - here)
        return first, 1 - first


    def select(which, route, d):
        position = lax.rem(coord(second_axis(route)) + d, 4)
        expert = expert_at(route, position)
        rank_row = pick_row(rank_out[route], expert)
        share_row = pick_row(share_out[route], expert)
        here = coord(second_axis(route))
        target = buffers[which]
        total = jnp.zeros((16, CHUNK), F32)
        for c in range(4):
            hit = slot_rows(rank_row, c) == iota((4 * MAIN + 16, 4 * TOK), 0)
            choose = jnp.where(hit, 1.0, 0.0).astype(BF16)
            rows = jnp.dot(
                choose,
                gathered[which, route, :, c * CHUNK : (c + 1) * CHUNK],
                preferred_element_type=F32,
            )
            if which == 1:
                rows = rows * jnp.sum(jnp.where(hit, share_row, 0.0), axis=1, keepdims=True)
            main = rows[: 4 * MAIN].astype(BF16)
            total += rows[4 * MAIN :]
            if which == 1 and not d:
                own[route, :, c * CHUNK : (c + 1) * CHUNK] = main
            elif d:
                staged[which, route, d - 1, :, c * CHUNK : (c + 1) * CHUNK] = main
            else:
                columns = slice(route * HALF + c * CHUNK, route * HALF + (c + 1) * CHUNK)
                if route == 0:
                    target[pl.ds(pl.multiple_of(here * 128, 128), 128), columns] = main
                else:
                    for s in range(4):
                        first = pl.multiple_of((s * 4 + here) * MAIN, MAIN)
                        target[pl.ds(first, MAIN), columns] = main[s * MAIN : (s + 1) * MAIN]
        mine = pl.ds(pl.multiple_of(here * 16, 16), 16)
        if not d:
            over[which, route, mine, :] = total.astype(BF16)
            return []
        staged_over[which, route, d - 1] = total.astype(BF16)
        device = peer(second_axis(route), d)
        size = HALF if which == 0 else HALF // 2
        later = []
        copies = [
            remote(
                staged_over.at[which, route, d - 1],
                over.at[which, route, mine, :],
                over_send.at[which, route, d],
                over_recv.at[which, route, d],
                device,
            )
        ]
        for part in range(HALF // size):
            begin = 0 if which == 0 else pl.multiple_of(halves_of(route)[part] * size, size)
            taken = pl.ds(begin, size)
            columns = pl.ds(pl.multiple_of(route * HALF + begin, size), size)
            found = later if part else copies
            if route == 0:
                found.append(
                    remote(
                        staged.at[which, route, d - 1, :, taken],
                        target.at[pl.ds(pl.multiple_of(here * 128, 128), 128), columns],
                        main_send.at[which, route, d, 4 * part],
                        main_recv.at[which, route, d, 4 * part],
                        device,
                    )
                )
            else:
                for s in range(4):
                    first = pl.multiple_of((s * 4 + here) * MAIN, MAIN)
                    found.append(
                        remote(
                            staged.at[which, route, d - 1, pl.ds(s * MAIN, MAIN), taken],
                            target.at[pl.ds(first, MAIN), columns],
                            main_send.at[which, route, d, 4 * part + s],
                            main_recv.at[which, route, d, 4 * part + s],
                            device,
                        )
                    )
        for copy in copies:
            copy.start()
        sends.extend(copies)
        postponed.extend(later)
        return copies

    def second_hop(which, passed):
        arrivals = []
        for copy in passed:
            copy.wait_recv()
        for d in ORDER:
            for route in range(2):
                arrivals.extend(select(which, route, d))
        return arrivals

    def finish(which, arrivals):
        for copy in arrivals:
            copy.wait_recv()
        for route in range(2):
            slot, chunk = overflow_target(route, (16, 64), 1)
            for c in range(4):
                spread = jnp.where((slot == iota((16, 64), 0)) & (chunk == c), 1.0, 0.0)
                first = route * HALF + c * CHUNK
                tail = jnp.dot(
                    spread.astype(BF16), over[which, route], preferred_element_type=F32
                ).astype(BF16)
                if which == 0:
                    xbuf[16 * MAIN : ROWS, first : first + CHUNK] = tail
                else:
                    own_over[:, first : first + CHUNK] = tail

    tok_passed = gather_pass(0, tok_copies)
    cot_passed = gather_pass(1, cot_copies)
    x_arrivals = second_hop(0, tok_passed)
    g_arrivals = second_hop(1, cot_passed)
    for copy in postponed:
        copy.start()
    sends.extend(postponed)
    for which in range(2):
        for route in range(2):
            select(which, route, 0)
    load_gu.wait()
    load_d.wait()

    core = lax.rem(lax.axis_index("dp"), 2)
    stores = []
    shared = []

    def store(src, dst):
        copy = pltpu.make_async_copy(src, dst, local_sem.at[2 + len(stores)])
        copy.start()
        stores.append(copy)
        return copy

    def share(src, dst):
        slot = len(shared)
        copy = remote(src, dst, core_send.at[slot], core_recv.at[slot], other_core())
        copy.start()
        shared.append(copy)
        return copy

    before_own = len(stores)
    for route in range(2):
        here = coord(second_axis(route))
        columns = pl.ds(route * HALF, HALF)
        if route == 0:
            first = pl.multiple_of(here * 128, 128)
            store(own.at[route], g_hbm.at[pl.ds(first, 128), columns])
        else:
            for s in range(4):
                first = pl.multiple_of((s * 4 + here) * MAIN, MAIN)
                store(
                    own.at[route, pl.ds(s * MAIN, MAIN), :],
                    g_hbm.at[pl.ds(first, MAIN), columns],
                )

    own_stores = stores[before_own:]
    mine, theirs = pl.ds(0, ROWS), pl.ds(ROWS, ROWS)

    def split(src, dst):
        for block in range(4):
            there = pl.ds(block * 512, 512)
            keep = pl.ds(pl.multiple_of((2 * block + core) * 512, 512), 512)
            give = pl.ds(pl.multiple_of((2 * block + 1 - core) * 512, 512), 512)
            share(src.at[:, give], dst.at[theirs, there])
            store(src.at[:, keep], dst.at[mine, there])

    finish(0, x_arrivals)
    split(xbuf, x_hbm)

    @pl.loop(0, 3)
    def _(n):
        u_cols = pl.ds(pl.multiple_of(n * 256, 256), 256)
        v_cols = pl.ds(pl.multiple_of(HID + n * 256, 256), 256)
        u = jnp.dot(xbuf[...], wgu[:, u_cols], preferred_element_type=F32)
        pre[:, u_cols] = u
        v = jnp.dot(xbuf[...], wgu[:, v_cols], preferred_element_type=F32)
        pre[:, v_cols] = v
        hid[:ROWS, u_cols] = (pre[:, u_cols] * jax.nn.sigmoid(pre[:, u_cols]) * v).astype(BF16)

    hid_share = share(hid.at[mine], hid.at[theirs])
    store(pre, pre_hbm)
    finish(1, g_arrivals)
    own_stores.append(store(own_over, g_hbm.at[pl.ds(16 * MAIN, 16), :]))
    for copy in own_stores:
        copy.wait()

    def far_columns(of_core):
        return pl.ds(pl.multiple_of((2 * lax.rem(y + 2, 4) + of_core) * 512, 512), 512)

    far_load = store(g_hbm.at[:, far_columns(core)], far_rows.at[mine])
    far_share = share(g_hbm.at[:, far_columns(1 - core)], far_rows.at[theirs])

    @pl.loop(0, HALF // 256)
    def _(n):
        cols = pl.ds(pl.multiple_of(n * 256, 256), 256)
        obuf[:, cols] = jnp.dot(
            hid[:ROWS, :], wd[:, cols], preferred_element_type=F32
        ).astype(BF16)

    store(obuf, out_hbm)
    hid_share.wait_recv()
    store(hid, h_hbm)
    far_load.wait()
    far_share.wait_recv()

    @pl.loop(0, 3)
    def _(n):
        piece = pl.ds(pl.multiple_of(n * 256, 256), 256)
        far_sum[piece, :] = lax.dot_general(
            hid[:, piece],
            far_rows[...],
            (((0,), (0,)), ((), ())),
            preferred_element_type=F32,
        ).astype(BF16)

    store(far_sum, far_hbm)
    for copy in postponed:
        copy.wait_recv()
    for copy in stores:
        if copy is not far_load and all(copy is not other for other in own_stores):
            copy.wait()
    for copy in shared:
        if copy is hid_share or copy is far_share:
            copy.wait_send()
        else:
            copy.wait()
    for copy in sends:
        copy.wait_send()


def return_kernel(
    out_hbm,
    wgu_hbm,
    x_hbm,
    g_hbm,
    h_hbm,
    pre_hbm,
    far_hbm,
    wd_hbm,
    rank_ref,
    share_ref,
    layer_hbm,
    token_hbm,
    down_hbm,
    grad_in,
    layer_out,
    token_grad,
    grad_out,
    xb,
    gb,
    gall,
    hb,
    pre,
    wd,
    pgb,
    wgu,
    sum_in,
    sum_out,
    near_in,
    near_out,
    far_in,
    far_out,
    tail,
    compact,
    rows,
    rows_over,
    partial,
    final,
    local_sem,
    wgu_sem,
    main_send,
    main_recv,
    over_send,
    over_recv,
    part_send,
    part_recv,
    dp_send,
    dp_recv,
    core_send,
    core_recv,
):
    z, x = place()
    y = lax.axis_index("dp") // 2
    core = lax.rem(lax.axis_index("dp"), 2)
    sig = gall
    mine, theirs = pl.ds(0, ROWS), pl.ds(ROWS, ROWS)
    fetch = {}

    def load(name, src, dst):
        copy = pltpu.make_async_copy(src, dst, local_sem.at[18 + len(fetch)])
        copy.start()
        fetch[name] = copy

    def columns_of(ahead, of_core):
        first = (2 * lax.rem(y + ahead, 4) + of_core) * 512
        return pl.ds(pl.multiple_of(first, 512), 512)

    def place_of(ahead):
        return pl.ds(pl.multiple_of(lax.rem(y + ahead, 4) * 512, 512), 512)

    load("h", h_hbm, hb)
    load("d", wd_hbm.at[0], wd)
    for ahead in (1, 3, 0):
        load(ahead, g_hbm.at[:, columns_of(ahead, core)], gb.at[mine, place_of(ahead)])
    load_tail = pltpu.make_async_copy(
        out_hbm.at[pl.ds(16 * MAIN, 16), :], tail.at[:, pl.ds(0, HALF)], local_sem.at[0]
    )
    load_tail.start()

    def wgu_tile(n):
        rows = pl.ds(pl.multiple_of(n * 256, 256), 256)
        slot = lax.rem(n, 2)
        return pltpu.make_async_copy(wgu_hbm.at[0, rows, :], wgu.at[slot], wgu_sem.at[slot])

    wgu_tile(0).start()
    enter(
        [peer(axis, d) for axis in ("z", "x") for d in ORDER]
        + [along_y(d) for d in (1, 3)]
        + [other_core()]
    )
    sends = []
    def pieces(which, route, position, slot):
        columns = pl.ds(route * HALF, HALF)
        if route == 0:
            rows_there = pl.ds(pl.multiple_of(position * 128, 128), 128)
            if which == 0:
                src = out_hbm.at[rows_there]
            else:
                src = sig.at[rows_there, columns]
            return [(src, rows.at[which, route, slot])]
        found = []
        for s in range(4):
            dst = rows.at[which, route, slot, pl.ds(s * MAIN, MAIN), :]
            if which == 0:
                first = pl.multiple_of((s % 2) * 128 + position * MAIN, MAIN)
                found.append((partial.at[1, s // 2, pl.ds(first, MAIN), :], dst))
            else:
                first = pl.multiple_of((s * 4 + position) * MAIN, MAIN)
                found.append((sig.at[pl.ds(first, MAIN), columns], dst))
        return found

    early = []

    def first_hop(which, routes):
        arrivals = [[], []]
        for d in ORDER:
            for route in routes:
                here = coord(second_axis(route))
                there = lax.rem(here + d, 4)
                for s, (src, dst) in enumerate(pieces(which, route, there, here)):
                    copy = remote(
                        src,
                        dst,
                        main_send.at[which, route, d, s],
                        main_recv.at[which, route, d, s],
                        peer(second_axis(route), d),
                    )
                    copy.start()
                    (early if which == 0 and route == 1 else sends).append(copy)
                    arrivals[route].append(copy)
        owns = [[], []]
        for route in routes:
            here = coord(second_axis(route))
            for s, (src, dst) in enumerate(pieces(which, route, here, here)):
                copy = pltpu.make_async_copy(src, dst, local_sem.at[2 + which * 8 + route * 4 + s])
                copy.start()
                owns[route].append(copy)
        if which == 0 and routes[0] == 0:
            load_tail.wait()
        last = tail if which == 0 else sig.at[pl.ds(16 * MAIN, 16), :]
        for route in routes:
            here = coord(second_axis(route))
            slot, chunk = overflow_target(route, (64, 16), 0)
            total = jnp.zeros((64, CHUNK), F32)
            for c in range(4):
                take = jnp.where((slot == iota((64, 16), 1)) & (chunk == c), 1.0, 0.0)
                first = route * HALF + c * CHUNK
                total += jnp.dot(
                    take.astype(BF16),
                    last[:, first : first + CHUNK],
                    preferred_element_type=F32,
                )
            compact[which, route] = total.astype(BF16)
            mine = pl.ds(pl.multiple_of(here * 16, 16), 16)
            rows_over[which, route, mine, :] = compact[which, route, mine, :]
            for d in ORDER:
                there = lax.rem(here + d, 4)
                copy = remote(
                    compact.at[which, route, pl.ds(pl.multiple_of(there * 16, 16), 16), :],
                    rows_over.at[which, route, mine, :],
                    over_send.at[which, route, d],
                    over_recv.at[which, route, d],
                    peer(second_axis(route), d),
                )
                copy.start()
                sends.append(copy)
                arrivals[route].append(copy)
        return arrivals, owns

    def combine(which, arrivals, owns):
        for route in range(2):
            for copy in arrivals[route]:
                copy.wait_recv()
            for copy in owns[route]:
                copy.wait()
            ranks = [pick_row(rank_ref[route], expert_at(route, p)) for p in range(4)]
            shares = [pick_row(share_ref[route], expert_at(route, p)) for p in range(4)]
            for c in range(4):
                main, rest = [], []
                for p in range(4):
                    hit = slot_rows(ranks[p], c) == iota((4 * MAIN + 16, 4 * TOK), 0)
                    value = shares[p] if which == 0 else 1.0
                    spread = jnp.where(hit, value, 0.0)
                    main.append(spread[: 4 * MAIN])
                    rest.append(spread[4 * MAIN :])
                main = jnp.concatenate(main, axis=0).astype(BF16)
                rest = jnp.concatenate(rest, axis=0).astype(BF16)
                columns = slice(c * CHUNK, (c + 1) * CHUNK)
                along = (((0,), (0,)), ((), ()))
                total = lax.dot_general(
                    main,
                    rows[which, route, :, :, columns].reshape(16 * MAIN, CHUNK),
                    along,
                    preferred_element_type=F32,
                ) + lax.dot_general(
                    rest, rows_over[which, route], along, preferred_element_type=F32
                )
                partial[which, route, :, columns] = total.astype(BF16)

    def pass_partial(which):
        finals = []
        for d in ORDER:
            for route in range(2):
                here = coord(first_axis(route))
                there = lax.rem(here + d, 4)
                copy = remote(
                    partial.at[which, route, pl.ds(pl.multiple_of(there * TOK, TOK), TOK), :],
                    final.at[which, route, d - 1],
                    part_send.at[which, route, d],
                    part_recv.at[which, route, d],
                    peer(first_axis(route), d),
                )
                copy.start()
                sends.append(copy)
                finals.append(copy)
        return finals

    def finish(which, finals, result):
        for copy in finals:
            copy.wait_recv()
        for route in range(2):
            here = coord(first_axis(route))
            own = partial[which, route, pl.ds(pl.multiple_of(here * TOK, TOK), TOK), :]
            total = own.astype(F32)
            for d in range(3):
                total += final[which, route, d].astype(F32)
            result[:, route * HALF : (route + 1) * HALF] = total.astype(BF16)

    along = (((0,), (0,)), ((), ()))

    def weight_out(ahead):
        cols = place_of(ahead)

        @pl.loop(0, 3)
        def _(n):
            piece = pl.ds(pl.multiple_of(n * 256, 256), 256)
            sum_out[ahead, piece, :] = lax.dot_general(
                hb[:, piece], gb[:, cols], along, preferred_element_type=F32
            ).astype(BF16)

    def weight_in(ahead):
        first = lax.rem(y + ahead, 4) * 512

        @pl.loop(0, 2)
        def _(n):
            piece = pl.ds(pl.multiple_of(n * 256, 256), 256)
            part = pl.ds(pl.multiple_of(first + n * 256, 256), 256)
            sum_in[ahead, piece, :] = lax.dot_general(
                xb[:, part], pgb[...], along, preferred_element_type=F32
            ).astype(BF16)

    half_in = (pl.ds(0, 256), pl.ds(256, 256))
    half_out = (pl.ds(0, HID // 2), pl.ds(HID // 2, HID // 2))

    sums = (sum_out, sum_in)
    nears = (near_out, near_in)
    fars = (far_out, far_in)
    halves = (half_out, half_in)

    def pass_half(kind, ahead, half, side, dst, slot):
        src = far_hbm.at[halves[kind][half], :]
        if kind or ahead != 2:
            src = sums[kind].at[ahead, halves[kind][half], :]
        copy = remote(
            src,
            dst,
            dp_send.at[slot, side, kind],
            dp_recv.at[slot, side, kind],
            along_y((1, 3)[side]),
        )
        copy.start()
        sends.append(copy)
        return copy

    def pass_near(kind):
        return [pass_half(kind, 2, side, side, nears[kind].at[side], 0) for side in range(2)]

    def pass_far(kind, side):
        ahead, half = (1, 3)[side], 1 - side
        return pass_half(kind, ahead, half, side, fars[kind].at[side, halves[kind][half], :], 1)

    def pass_sum(kind, near):
        found = []
        for side, ahead in ((0, 1), (1, 3)):
            near[side].wait_recv()
            whole = halves[kind][side]
            size = whole.size // (1 + kind)
            for piece in range(1 + kind):
                part = pl.ds(whole.start + piece * size, size)
                arrived = nears[kind][side, piece * size : (piece + 1) * size, :]
                sums[kind][ahead, part, :] = (
                    sums[kind][ahead, part, :].astype(F32) + arrived.astype(F32)
                ).astype(BF16)
                copy = remote(
                    sums[kind].at[ahead, part, :],
                    fars[kind].at[side, part, :],
                    dp_send.at[2 + piece, side, kind],
                    dp_recv.at[2 + piece, side, kind],
                    along_y((1, 3)[side]),
                )
                copy.start()
                sends.append(copy)
                found.append(copy)
        return found

    near_sent_out = pass_near(0)
    swaps = {}
    for ahead in (1, 3, 0):
        swaps[ahead] = remote(
            g_hbm.at[:, columns_of(ahead, 1 - core)],
            gb.at[theirs, place_of(ahead)],
            core_send.at[ahead],
            core_recv.at[ahead],
            other_core(),
        )
        swaps[ahead].start()

    out_state = first_hop(0, (0,))
    ends = []
    fetch["h"].wait()
    fetch["d"].wait()
    load("g", g_hbm, gall)
    load("pre", pre_hbm, pre)
    load("x", x_hbm, xb)

    @pl.loop(0, HALF // 256)
    def _(n):
        cols = pl.ds(pl.multiple_of(n * 256, 256), 256)
        there = pl.ds(pl.multiple_of(HALF + n * 256, 256), 256)
        tile = jnp.dot(hb[:ROWS, :], wd[:, there], preferred_element_type=F32).astype(BF16)
        partial[1, 0, :, cols] = tile[:256]
        partial[1, 1, :, cols] = tile[256:512]
        tail[:, there] = tile[512:]

    for old, new in zip(out_state, first_hop(0, (1,))):
        old[1] = new[1]
    for ahead in (1, 3):
        fetch[ahead].wait()
        swaps[ahead].wait_recv()
        weight_out(ahead)
        ends.append(pass_far(0, ahead // 2))
    fetch["g"].wait()
    fetch["pre"].wait()

    @pl.loop(0, 3)
    def _(n):
        u_cols = pl.ds(pl.multiple_of(n * 256, 256), 256)
        v_cols = pl.ds(pl.multiple_of(HID + n * 256, 256), 256)
        grad = lax.dot_general(
            gall[...], wd[u_cols, :], (((1,), (1,)), ((), ())), preferred_element_type=F32
        )
        u = pre[:, u_cols]
        logistic = jax.nn.sigmoid(u)
        pgb[:ROWS, v_cols] = (grad * u * logistic).astype(BF16)
        pgb[:ROWS, u_cols] = (
            grad * pre[:, v_cols] * logistic * (1.0 + u * (1.0 - logistic))
        ).astype(BF16)

    swap = remote(
        pgb.at[mine], pgb.at[theirs], core_send.at[4], core_recv.at[4], other_core()
    )
    swap.start()
    ends += pass_sum(0, near_sent_out)
    def token_side(first, end):
        @pl.loop(first, end)
        def _(n):
            @pl.when(n + 1 < WIDTH // 256)
            def _():
                wgu_tile(n + 1).start()

            wgu_tile(n).wait()
            cols = pl.ds(pl.multiple_of(n * 256, 256), 256)
            sig[:, cols] = lax.dot_general(
                pgb[:ROWS, :],
                wgu[lax.rem(n, 2)],
                (((1,), (1,)), ((), ())),
                preferred_element_type=F32,
            ).astype(BF16)

    token_side(0, 6)
    fetch["x"].wait()
    swap.wait_recv()
    weight_in(2)
    near_sent_in = pass_near(1)
    token_side(6, WIDTH // 256)
    sig_state = first_hop(1, (0, 1))
    fetch[0].wait()
    swaps[0].wait_recv()
    weight_out(0)
    weight_in(0)
    combine(0, *out_state)
    out_finals = pass_partial(0)
    for ahead in (1, 3):
        weight_in(ahead)
        ends.append(pass_far(1, ahead // 2))
    ends += pass_sum(1, near_sent_in)
    for route in range(2):
        for copy in sig_state[0][route]:
            copy.wait_recv()
    for copy in early:
        copy.wait_send()
    combine(1, [[], []], sig_state[1])
    sig_finals = pass_partial(1)
    for copy in ends[:4]:
        copy.wait_recv()

    @pl.loop(0, 4)
    def _(n):
        part = pl.ds(pl.multiple_of(n * 192, 192), 192)
        total = sum_out[0, part, :].astype(F32)
        total += far_out[0, part, :].astype(F32) + far_out[1, part, :].astype(F32)
        grad_out[part, :] = total.astype(BF16)

    results = []

    def leave(src, dst):
        copy = pltpu.make_async_copy(src, dst, local_sem.at[27 + len(results)])
        copy.start()
        results.append(copy)

    leave(grad_out, down_hbm)
    finish(0, out_finals, layer_out)
    leave(layer_out, layer_hbm)
    finish(1, sig_finals, token_grad)
    leave(token_grad, token_hbm)
    for copy in ends[4:6]:
        copy.wait_recv()
    for n, copy in ((0, ends[6]), (2, ends[8]), (1, ends[7]), (3, ends[9])):
        copy.wait_recv()
        part = pl.ds(n * 128, 128)
        total = sum_in[0, part, :].astype(F32)
        total += far_in[0, part, :].astype(F32) + far_in[1, part, :].astype(F32)
        sum_in[0, part, :] = total.astype(BF16)
        leave(sum_in.at[0, part, :], grad_in.at[part, :])

    for copy in sends + [swaps[ahead] for ahead in (1, 3, 0)] + [swap]:
        copy.wait_send()
    for copy in results:
        copy.wait()


def last_kernel(*refs):
    count = len(refs) // 3
    held, sems = refs[2 * count : 3 * count], refs[-1]
    steps = 4
    loads, stores = [], []
    for n in range(count):
        size = refs[n].shape[0] // steps
        for step in range(steps):
            part = pl.ds(step * size, size)
            loads.append(
                pltpu.make_async_copy(refs[n].at[part], held[n].at[part], sems.at[0, n, step])
            )
            stores.append(
                pltpu.make_async_copy(
                    held[n].at[part], refs[count + n].at[part], sems.at[1, n, step]
                )
            )
    for copy in loads:
        copy.start()
    for load, store in zip(loads, stores):
        load.wait()
        store.start()
    for copy in stores:
        copy.wait()


VMEM = pl.BlockSpec(memory_space=pltpu.VMEM)
ANY = pl.BlockSpec(memory_space=pl.ANY)
DMA = pltpu.SemaphoreType.DMA


def dispatch(ids, gates, tokens, cotangent, gate_up, down_weight):
    table = jax.ShapeDtypeStruct((2, 16, 4 * TOK), F32)
    return pl.pallas_call(
        dispatch_kernel,
        out_shape=(
            jax.ShapeDtypeStruct((ROWS, HALF), BF16),
            jax.ShapeDtypeStruct((2 * ROWS, HALF), BF16),
            jax.ShapeDtypeStruct((ROWS, WIDTH), BF16),
            jax.ShapeDtypeStruct((2 * ROWS, HID), BF16),
            jax.ShapeDtypeStruct((ROWS, 2 * HID), F32),
            jax.ShapeDtypeStruct((HID, 512), BF16),
            table,
            table,
        ),
        in_specs=[VMEM] * 4 + [ANY] * 2,
        out_specs=(ANY,) * 6 + (VMEM,) * 2,
        scratch_shapes=[
            pltpu.VMEM((WIDTH, 2 * HID), BF16),
            pltpu.VMEM((HID, WIDTH), BF16),
            pltpu.VMEM((16, 2 * TOK), F32),
            pltpu.VMEM((2, 4, 16, 2 * TOK), F32),
            pltpu.VMEM((2, 2, 4 * TOK, HALF), BF16),
            pltpu.VMEM((2, 2, 3, 4 * MAIN, HALF), BF16),
            pltpu.VMEM((2, 2, 3, 16, CHUNK), BF16),
            pltpu.VMEM((2, 2, 64, CHUNK), BF16),
            pltpu.VMEM((ROWS, WIDTH), BF16),
            pltpu.VMEM((2, 4 * MAIN, HALF), BF16),
            pltpu.VMEM((16, WIDTH), BF16),
            pltpu.VMEM((ROWS, 2 * HID), F32),
            pltpu.VMEM((2 * ROWS, HID), BF16),
            pltpu.VMEM((ROWS, HALF), BF16),
            pltpu.VMEM((2 * ROWS, 512), BF16),
            pltpu.VMEM((HID, 512), BF16),
            DMA((20,)),
            DMA((2, 4)),
            DMA((2, 4)),
            DMA((2, 2, 4)),
            DMA((2, 2, 4)),
            DMA((2, 2, 4, 8)),
            DMA((2, 2, 4, 8)),
            DMA((2, 2, 4)),
            DMA((2, 2, 4)),
            DMA((6,)),
            DMA((6,)),
        ],
        compiler_params=pltpu.CompilerParams(
            collective_id=0, has_side_effects=True, vmem_limit_bytes=60 << 20
        ),
        cost_estimate=pl.CostEstimate(
            flops=20 * 10**9, bytes_accessed=40 * 10**6, transcendentals=10**6
        ),
    )(ids, gates, tokens, cotangent, gate_up, down_weight)


def give_back(out_rows, gate_up, x_rows, g_rows, hidden, pre_act, far_sum, down_weight, rank, share):
    result = jax.ShapeDtypeStruct((TOK, WIDTH), BF16)
    return pl.pallas_call(
        return_kernel,
        out_shape=(
            result,
            result,
            jax.ShapeDtypeStruct((HID, 512), BF16),
            jax.ShapeDtypeStruct((512, 2 * HID), BF16),
        ),
        in_specs=[ANY] * 8 + [VMEM] * 2,
        out_specs=(ANY,) * 4,
        scratch_shapes=[
            pltpu.VMEM((TOK, WIDTH), BF16),
            pltpu.VMEM((TOK, WIDTH), BF16),
            pltpu.VMEM((HID, 512), BF16),
            pltpu.VMEM((2 * ROWS, HALF), BF16),
            pltpu.VMEM((2 * ROWS, HALF), BF16),
            pltpu.VMEM((ROWS, WIDTH), BF16),
            pltpu.VMEM((2 * ROWS, HID), BF16),
            pltpu.VMEM((ROWS, 2 * HID), F32),
            pltpu.VMEM((HID, WIDTH), BF16),
            pltpu.VMEM((2 * ROWS, 2 * HID), BF16),
            pltpu.VMEM((2, 256, 2 * HID), BF16),
            pltpu.VMEM((4, 512, 2 * HID), BF16),
            pltpu.VMEM((4, HID, 512), BF16),
            pltpu.VMEM((2, 256, 2 * HID), BF16),
            pltpu.VMEM((2, HID // 2, 512), BF16),
            pltpu.VMEM((2, 512, 2 * HID), BF16),
            pltpu.VMEM((2, HID, 512), BF16),
            pltpu.VMEM((16, WIDTH), BF16),
            pltpu.VMEM((2, 2, 64, CHUNK), BF16),
            pltpu.VMEM((2, 2, 4, 4 * MAIN, HALF), BF16),
            pltpu.VMEM((2, 2, 64, CHUNK), BF16),
            pltpu.VMEM((2, 2, 4 * TOK, HALF), BF16),
            pltpu.VMEM((2, 2, 3, TOK, HALF), BF16),
            DMA((34,)),
            DMA((2,)),
            DMA((2, 2, 4, 4)),
            DMA((2, 2, 4, 4)),
            DMA((2, 2, 4)),
            DMA((2, 2, 4)),
            DMA((2, 2, 4)),
            DMA((2, 2, 4)),
            DMA((4, 2, 2)),
            DMA((4, 2, 2)),
            DMA((5,)),
            DMA((5,)),
        ],
        compiler_params=pltpu.CompilerParams(
            collective_id=1, has_side_effects=True, vmem_limit_bytes=62 << 20
        ),
        cost_estimate=pl.CostEstimate(
            flops=26 * 10**9, bytes_accessed=100 * 10**6, transcendentals=0
        ),
    )(out_rows, gate_up, x_rows, g_rows, hidden, pre_act, far_sum, down_weight, rank, share)


def last(*results):
    return pl.pallas_call(
        last_kernel,
        out_shape=tuple(jax.ShapeDtypeStruct(a.shape, a.dtype) for a in results),
        in_specs=[ANY] * len(results),
        out_specs=(ANY,) * len(results),
        scratch_shapes=[pltpu.VMEM(a.shape, a.dtype) for a in results]
        + [DMA((2, len(results), 4))],
        cost_estimate=pl.CostEstimate(
            flops=0, bytes_accessed=7 * 10**6, transcendentals=0
        ),
    )(*results)


def per_device(tokens, cotangent, expert_ids, gate_fixed, gate_up, down_weight):
    out_rows, x_rows, g_rows, hidden, pre_act, far_sum, rank, share = dispatch(
        expert_ids.T, gate_fixed.T, tokens, cotangent, gate_up, down_weight
    )
    layer_out, token_grad, grad_out, grad_in = last(
        *give_back(
            out_rows, gate_up, x_rows, g_rows, hidden, pre_act, far_sum, down_weight, rank, share
        )
    )
    return layer_out, token_grad, grad_in[None], grad_out[None]


def solution(mesh):
    rows = P(("ep", "dp"), None)
    return jax.shard_map(
        per_device,
        mesh=mesh,
        in_specs=(rows, rows, rows, rows, P("ep", None, None), P("ep", None, None)),
        out_specs=(rows, rows, P("ep", "dp", None), P("ep", None, "dp")),
        check_vma=False,
    )
```
